256 devices in a mesh: row: 8 (over x, core), col: 32 (over z, y).
Axes of the slice: x: 4, y: 4, z: 8, core: 2. Of those that a mesh axis runs over, the one named last changes fastest.
Arguments:
- field_start: float32 [8192, 24576], P('row', 'col'), may hold values from -6 to 6
- w_sensor: bfloat16 [512, 512], replicated, may hold values from -0.25 to 0.25
- bias_sensor: float32 [512], replicated, may hold values from -3 to 3
- w_middle: bfloat16 [512, 512], replicated, may hold values from -0.25 to 0.25
- bias_middle: float32 [512], replicated, may hold values from -3 to 3
- w_latent: bfloat16 [512, 512], replicated, may hold values from -0.25 to 0.25
- bias_latent: float32 [512], replicated, may hold values from -3 to 3
- trunk_basis: bfloat16 [512, 4096], replicated, may hold values from -1 to 1
- coarse_matrix: float32 [3072, 3072], P(('row', 'col')), may hold values from -0.4375 to 0.4375
Outputs:
- field_final: float32 [8192, 24576], P('row', 'col')
The draws below stay inside these ranges and needn't reach their ends.
All inputs are finite; a program needn't handle non-finite values.
Results may differ from the reference program's by a relative error of at most 0.024.
Values may be sent and summed in bfloat16 or wider, within the bound.
No kernel may reach another device: no remote copies, remote signals or barrier semaphores. Data moves between devices by JAX's collectives and lax.ppermute only.
A program may use at most 128 MiB of HBM per device.

```python
import jax
import jax.numpy as jnp
from jax import lax

TILE = 64
HID = 512
LATENT = 512
ITERS = 4
CYCLE = 512
NPTS = 4096
CELL = 256
KX = 4
KY = 3
NX = 8192
NY = 24576
M = 3072
N_ROW = 8
N_COL = 32


def draw_trunk_basis(key, part):
    key = jax.random.fold_in(key, 11)
    key_offset, key_noise = jax.random.split(key)
    offsets = jnp.clip(jax.random.normal(key_offset, (LATENT, 1), jnp.float32), -2.0, 2.0)
    noise = jnp.clip(jax.random.normal(key_noise, (LATENT, NPTS), jnp.float32), -3.0, 3.0)
    return ((noise + offsets) * LATENT ** (-0.5)).astype(jnp.bfloat16)


def raised(drawn, rng, source, target, shards_of, factor):
    owner, partner = [(jnp.arange(drawn.shape[dim]) // (drawn.shape[dim] // shards_of)).reshape([-1 if axis == dim else 1 for axis in range(drawn.ndim)]) for dim in (source, target)]
    chosen = jax.random.permutation(rng, shards_of)[partner]
    strong = (owner == chosen) | (owner == (partner + shards_of // 2) % shards_of)
    return jnp.where(strong, factor * drawn, drawn)


def block_levels(own_key, extent, pieces, low, high):
    def one(axis_at, shards_of):
        draws = jax.random.uniform(jax.random.fold_in(jax.random.fold_in(own_key, 6), axis_at), (shards_of,), jnp.float32, low / len(pieces), high / len(pieces))
        return jnp.repeat(jnp.exp(draws), extent[axis_at] // shards_of).reshape((-1,) + (1,) * (len(extent) - axis_at - 1))

    factor_of = one(*pieces[0])
    for cut in pieces[1:]:
        factor_of = factor_of * one(*cut)
    return factor_of


def gaussian(stream_key, extent, scale, bound, shards=(), dtype=jnp.bfloat16):
    loudness = block_levels(stream_key, extent, shards, -0.22, 0.18) if shards else 1.0
    values = jax.random.normal(stream_key, extent, jnp.float32) * scale * loudness
    return jnp.minimum(jnp.maximum(values, -bound), bound).astype(dtype)


def bell_draw_with(rng, extent, deviation, limit, cuts, heavy, held_as=jnp.bfloat16):
    values = deviation * jax.random.normal(rng, extent, jnp.float32)
    if cuts:
        values = values * block_levels(rng, extent, cuts, -0.22, 0.18)
    return jnp.clip(raised(values, jax.random.fold_in(rng, 3), *heavy), -limit, limit).astype(held_as)


def setup_inputs(seed: int = 0) -> dict:
    arg_keys = jax.random.split(jax.random.key(seed), 10)
    return {
        "field_start": gaussian(arg_keys[0], (NX, NY), 1.0, 6.0, ((0, 8), (1, 32)), jnp.float32),
        "w_sensor": gaussian(arg_keys[1], (CYCLE, HID), CYCLE ** -0.5, 0.25),
        "bias_sensor": gaussian(arg_keys[2], (HID,), 0.5, 3.0, (), jnp.float32),
        "w_middle": gaussian(arg_keys[3], (HID, HID), HID ** -0.5, 0.25),
        "bias_middle": gaussian(arg_keys[4], (HID,), 0.5, 3.0, (), jnp.float32),
        "w_latent": gaussian(arg_keys[5], (HID, LATENT), HID ** -0.5, 0.25),
        "bias_latent": gaussian(arg_keys[6], (LATENT,), 0.5, 3.0, (), jnp.float32),
        "trunk_basis": draw_trunk_basis(jax.random.fold_in(arg_keys[9], 71), 0),
        "coarse_matrix": bell_draw_with(arg_keys[8], (M, M), M ** -0.5, 0.4375, ((0, 256),), (1, 0, 256, 6.0), jnp.float32),
    }


def strip_windows(strips, count, tile):
    blocks = strips.reshape(strips.shape[0], count + 1, tile)
    return jnp.concatenate([blocks[:, :-1], blocks[:, 1:]], axis=2)


def cycle_values(padded, tile, count_x, count_y):
    side = 2 * tile
    top_rows = padded[0:count_x * tile:tile, :]
    bottom_rows = padded[side - 1:side - 1 + count_x * tile:tile, :]
    left_cols = padded[:, 0:count_y * tile:tile].T
    right_cols = padded[:, side - 1:side - 1 + count_y * tile:tile].T
    tops = strip_windows(top_rows, count_y, tile)
    bottoms = strip_windows(bottom_rows, count_y, tile)
    lefts = strip_windows(left_cols, count_x, tile).transpose(1, 0, 2)
    rights = strip_windows(right_cols, count_x, tile).transpose(1, 0, 2)
    joined = jnp.concatenate([tops, bottoms, lefts, rights], axis=2)
    return joined.reshape(count_x * count_y, 4 * side)


def branch_net(cycle, w_sensor, bias_sensor, w_middle, bias_middle, w_latent, bias_latent):
    hidden = jnp.tanh(jnp.dot(cycle, w_sensor, preferred_element_type=jnp.float32) + bias_sensor).astype(jnp.bfloat16)
    hidden = jnp.tanh(jnp.dot(hidden, w_middle, preferred_element_type=jnp.float32) + bias_middle).astype(jnp.bfloat16)
    return (jnp.dot(hidden, w_latent, preferred_element_type=jnp.float32) + bias_latent).astype(jnp.bfloat16)


def reference(field_start, w_sensor, bias_sensor, w_middle, bias_middle, w_latent, bias_latent, trunk_basis, coarse_matrix):
    tile = TILE
    count_x = NX // tile
    count_y = NY // tile
    field = field_start
    for step in range(ITERS):
        padded = jnp.pad(field.astype(jnp.bfloat16), tile // 2)
        cycle = cycle_values(padded, tile, count_x, count_y)
        coeffs = branch_net(cycle, w_sensor, bias_sensor, w_middle, bias_middle, w_latent, bias_latent)
        coeffs = coeffs.reshape(count_x, count_y, -1)

        def one_strip(row_coeffs):
            values = jnp.dot(row_coeffs, trunk_basis, preferred_element_type=jnp.float32)
            return values.reshape(count_y, tile, tile).transpose(1, 0, 2).reshape(tile, count_y * tile)

        prediction = lax.map(one_strip, coeffs).reshape(NX, NY)
        blocks = prediction.reshape(N_ROW, KX, CELL, N_COL, KY, CELL)
        means = jnp.mean(blocks, axis=(2, 5)).transpose(0, 2, 1, 3).reshape(M)
        correction = jnp.dot(coarse_matrix, means, precision=lax.Precision.HIGHEST)
        correction = correction.reshape(N_ROW, N_COL, KX, KY).transpose(0, 2, 1, 3).reshape(N_ROW * KX, N_COL * KY)
        field = (prediction.reshape(N_ROW * KX, CELL, N_COL * KY, CELL) + correction[:, None, :, None]).reshape(NX, NY)
    return field
```

```python
import functools

import jax
import jax.numpy as jnp
import numpy as np
from jax import lax
from jax.experimental import pallas as pl
from jax.experimental.pallas import tpu as pltpu
from jax.sharding import PartitionSpec as P

TILE = 64
ITERS = 4
CELL = 256
PER_CELL = CELL // TILE
HALO = ITERS
LANES = 128
F32 = jnp.float32
BF16 = jnp.bfloat16
VMEM_LIMIT = 48 * 1024 * 1024


def dot(a, b, **kw):
    return jnp.dot(a, b, preferred_element_type=F32, **kw)


def nt_dot(a, b):
    return lax.dot_general(a, b, (((1,), (1,)), ((), ())), preferred_element_type=F32)


def low_lanes(shape):
    return lax.broadcasted_iota(jnp.int32, shape, 1) < TILE


def call(kernel, out_shape, *args, grid=(), in_specs=None, out_specs=None, scratch=(), flops=0):
    whole = pl.BlockSpec(memory_space=pltpu.VMEM)
    specs = {}
    if grid:
        specs["grid"] = grid
    return pl.pallas_call(
        kernel,
        out_shape=out_shape,
        in_specs=in_specs or [whole] * len(args),
        out_specs=out_specs or jax.tree.map(lambda _: whole, out_shape),
        scratch_shapes=list(scratch),
        compiler_params=pltpu.CompilerParams(vmem_limit_bytes=VMEM_LIMIT),
        cost_estimate=pl.CostEstimate(flops=flops, bytes_accessed=1 << 20, transcendentals=0),
        **specs,
    )(*args)


def sensor_layout():
    half = TILE // 2
    row31, row32, col31, col32 = (np.arange(TILE) + TILE * i for i in range(4))
    top, bottom, left, right = (np.arange(2 * TILE) + 2 * TILE * i for i in range(4))
    mid = slice(half, half + TILE)
    groups = [
        (row32, top[mid]),
        (row31, bottom[mid]),
        (np.r_[row32[half:], col32[half:]], np.r_[top[:half], left[:half]]),
        (np.r_[row31[half:], col32[:half]], np.r_[bottom[:half], left[-half:]]),
        (np.r_[row32[:half], col31[half:]], np.r_[top[-half:], right[:half]]),
        (np.r_[row31[:half], col31[:half]], np.r_[bottom[-half:], right[-half:]]),
        (col32, left[mid]),
        (col31, right[mid]),
    ]
    source = np.concatenate([g[0] for g in groups])
    order = np.concatenate([g[1] for g in groups])
    spread = np.zeros((4 * TILE, 8 * TILE), np.float32)
    spread[source, np.arange(8 * TILE)] = 1.0
    return spread, order


def extract_kernel(na, nb, field, own, up, down, row_part, col_part):
    step = pl.program_id(0)
    here, _, cols = field.shape
    sel_row = lax.broadcasted_iota(jnp.int32, (2 * 16, cols), 0)
    sel_col = lax.broadcasted_iota(jnp.int32, (2 * 16, cols), 1)
    side, b_of = sel_row // 16, sel_row % 16
    pick = jnp.where(sel_col == b_of * TILE + (TILE // 2 - 1) + side, 1.0, 0.0).astype(BF16)
    picked = nt_dot(pick, field[...].reshape(here * TILE, cols).astype(BF16))
    r31 = field[:, TILE // 2 - 1, :].astype(BF16).astype(F32)
    r32 = field[:, TILE // 2, :].astype(BF16).astype(F32)
    low = low_lanes((here, LANES))
    base = step * here
    for pair in range(nb // 2):
        lanes = slice(pair * LANES, (pair + 1) * LANES)
        x, y = r31[:, lanes], r32[:, lanes]
        row_part[pl.ds(pl.multiple_of(2 * pair * na + base, 8), here), :] = jnp.where(
            low, x, pltpu.roll(y, TILE, 1)
        )
        row_part[pl.ds(pl.multiple_of((2 * pair + 1) * na + base, 8), here), :] = jnp.where(
            low, pltpu.roll(x, TILE, 1), y
        )
    low = low_lanes((16, LANES))
    for pair in range(here // 2):
        lanes = slice(pair * LANES, (pair + 1) * LANES)
        x, y = picked[0:16, lanes], picked[16:32, lanes]
        even = jnp.where(low, x, pltpu.roll(y, TILE, 1))
        odd = jnp.where(low, pltpu.roll(x, TILE, 1), y)
        col_part[pl.ds(base + 2 * pair, nb, stride=na), :] = even[0:nb]
        col_part[pl.ds(base + 2 * pair + 1, nb, stride=na), :] = odd[0:nb]

    @pl.when(step == pl.num_programs(0) - 1)
    def _():
        all_tiles = jnp.concatenate([row_part[...], col_part[...]], axis=1)
        own[...] = all_tiles.astype(BF16)
        by_b = all_tiles.reshape(nb, na, 4 * TILE)
        up[...] = by_b[:, 0:HALO, :].reshape(nb * HALO, 4 * TILE).astype(BF16)
        down[...] = by_b[:, na - HALO :, :].reshape(nb * HALO, 4 * TILE).astype(BF16)


def columns_kernel(na, nb, own, above, below, c_own, c_above, c_below, both, left, right, c_left, c_right):
    tall = jnp.concatenate(
        [
            above[...].astype(F32).reshape(nb, HALO, 4 * TILE),
            own[...].astype(F32).reshape(nb, na, 4 * TILE),
            below[...].astype(F32).reshape(nb, HALO, 4 * TILE),
        ],
        axis=1,
    )
    height = na + 2 * HALO
    both[...] = tall.reshape(nb * height, 4 * TILE).astype(BF16)
    left[...] = tall[0:HALO].reshape(HALO * height, 4 * TILE).astype(BF16)
    right[...] = tall[nb - HALO :].reshape(HALO * height, 4 * TILE).astype(BF16)
    kx, ky = na // PER_CELL, nb // PER_CELL
    for target, j in ((c_left, 0), (c_right, ky - 1)):
        target[0:1, :] = c_above[j : j + 1, :]
        for i in range(kx):
            target[i + 1 : i + 2, :] = c_own[i * ky + j : i * ky + j + 1, :]
        target[kx + 1 : kx + 2, :] = c_below[j : j + 1, :]


def trunk_kernel(trunk, w_sensor, spread, blocks, sensor_trunk, mean_trunk, w_out, total, rows):
    step = pl.program_id(0)
    width = trunk.shape[1]
    per = width // TILE
    point = lax.broadcasted_iota(jnp.int32, (width, LANES), 0)
    lane = lax.broadcasted_iota(jnp.int32, (width, LANES), 1)
    row = step * per + point // TILE
    side = lane // TILE
    hit = (row == lane % TILE) & (point % TILE == TILE // 2 - 1 + side)
    pick = jnp.concatenate(
        [
            jnp.where(hit, 1.0, 0.0).astype(BF16),
            jnp.full((width, LANES), 1.0 / (TILE * TILE), BF16),
        ],
        axis=1,
    )
    part = dot(trunk[...], pick)

    @pl.when(step == 0)
    def _():
        total[...] = part

    @pl.when(step > 0)
    def _():
        total[...] += part

    half = pl.num_programs(0) // 2

    @pl.when(step == half - 1)
    def _():
        last = trunk[:, width - LANES : width].astype(F32)
        rows[:, 0:LANES] = pltpu.roll(last, TILE, 1)

    @pl.when(step == half)
    def _():
        first = trunk[:, 0:LANES].astype(F32)
        rows[:, LANES : 2 * LANES] = pltpu.roll(first, TILE, 1)

    @pl.when(step == pl.num_programs(0) - 1)
    def _():
        low = low_lanes((trunk.shape[0], LANES))
        row_part = jnp.where(low, rows[:, 0:LANES], rows[:, LANES : 2 * LANES])
        unique = jnp.concatenate([row_part, total[:, 0:LANES]], axis=1).astype(BF16)
        sensor_trunk[...] = dot(unique, spread[...]).astype(BF16)
        mean_trunk[...] = total[:, LANES : 2 * LANES]
        at = 0
        for start, size in blocks:
            w_out[at : at + size, :] = w_sensor[start : start + size, :]
            at += size


def sensor_vectors(sensors, base, count):
    height = HALO * 2 + 16
    low = low_lanes((count, LANES))

    def part(shift, group):
        return sensors[base + shift : base + shift + count, group * LANES : (group + 1) * LANES]

    parts = [
        jnp.where(low, part(-1, 0), part(1, 0)),
        jnp.where(low, part(-height - 1, 1), part(-height + 1, 1)),
        jnp.where(low, part(height - 1, 2), part(height + 1, 2)),
        jnp.where(low, part(-height, 3), part(height, 3)),
    ]
    return jnp.concatenate([p.astype(BF16) for p in parts], axis=1)


def branch(vectors, w1, b1, w2, b2, w3, b3):
    hidden = jnp.tanh(dot(vectors, w1[...]) + b1[...]).astype(BF16)
    hidden = jnp.tanh(dot(hidden, w2[...]) + b2[...]).astype(BF16)
    return (dot(hidden, w3[...]) + b3[...]).astype(BF16)


def send_means(coeffs, pool, mean_trunk, col, cells, payload):
    pooled = dot(pool[...], coeffs)
    means = dot(pooled, mean_trunk[...], precision=lax.Precision.HIGHEST)
    lane = lax.broadcasted_iota(jnp.int32, means.shape, 1)
    cell = lax.broadcasted_iota(jnp.int32, means.shape, 0)
    mine = ((lane - cells * col) & (LANES - 1)) == cell
    line = jnp.sum(jnp.where(mine, means, 0.0), axis=0, keepdims=True)
    payload[...] = jnp.broadcast_to(line, payload.shape)


def corrections(gathered, coarse, n_row, n_col, cells):
    blocks = n_col * cells // LANES
    lane = lax.broadcasted_iota(jnp.int32, (n_col, LANES), 1)
    source = cells * lax.broadcasted_iota(jnp.int32, (n_col, LANES), 0)
    block = (source + ((lane - source) & (LANES - 1))) // LANES
    total = None
    for r in range(n_row):
        values = gathered[r * n_col : (r + 1) * n_col, :]
        for k in range(blocks):
            line = jnp.sum(jnp.where(block == k, values, 0.0), axis=0, keepdims=True)
            at = (r * blocks + k) * LANES
            term = coarse[:, at : at + LANES] * line
            total = term if total is None else total + term
    return jnp.sum(total, axis=1, keepdims=True)


def first_kernel(
    na, nb, cells, mid, left, right, c_own, c_above, c_below, c_left, c_right, spread, w1, b1, w2, b2, w3, b3,
    pool, mean_trunk, coeffs, payload, coarse, sensors,
):
    height = na + 2 * HALO
    side = HALO * height
    wide = nb * height
    sensors[0:8, :] = jnp.zeros((8, 8 * TILE), F32)
    sensors[8 : 8 + side, :] = dot(left[...], spread[...])
    sensors[8 + side : 8 + side + wide, :] = dot(mid[...], spread[...])
    sensors[8 + side + wide : 8 + 2 * side + wide, :] = dot(right[...], spread[...])
    sensors[8 + 2 * side + wide : 16 + 2 * side + wide, :] = jnp.zeros((8, 8 * TILE), F32)
    count = (nb + 2 * HALO - 2) * height
    vectors = sensor_vectors(sensors, 8 + height, count)
    result = branch(vectors, w1, b1, w2, b2, w3, b3)
    coeffs[...] = result
    send_means(result, pool, mean_trunk, lax.axis_index("col"), cells, payload)
    kx, ky = na // PER_CELL, nb // PER_CELL
    for j in range(ky + 2):
        for i in range(kx + 2):
            if j == 0:
                line = c_left[i : i + 1, :]
            elif j == ky + 1:
                line = c_right[i : i + 1, :]
            elif i == 0:
                line = c_above[j - 1 : j, :]
            elif i == kx + 1:
                line = c_below[j - 1 : j, :]
            else:
                at = (i - 1) * ky + j - 1
                line = c_own[at : at + 1, :]
            at = j * height + i * PER_CELL
            coarse[at : at + PER_CELL, :] = jnp.broadcast_to(line, (PER_CELL, line.shape[1]))


def next_kernel(
    k, na, nb, n_row, n_col, cells, gathered, before, sensor_trunk, coarse, w1, b1, w2, b2, w3, b3,
    pool, mean_trunk, coeffs, payload, sensors,
):
    height = na + 2 * HALO
    first = k - 1
    have = nb + 2 * HALO - 2 * first
    rows = have * height
    predicted = dot(before[...], sensor_trunk[...])
    correction = corrections(gathered, coarse, n_row, n_col, cells)
    row, col = lax.axis_index("row"), lax.axis_index("col")
    a_at = row * na - HALO + lax.broadcasted_iota(jnp.int32, (height, 1), 0)
    a_ok = (a_at >= 0) & (a_at < n_row * na)
    sensors[0:8, :] = jnp.zeros((8, 8 * TILE), F32)
    sensors[8 + rows : 16 + rows, :] = jnp.zeros((8, 8 * TILE), F32)
    for b in range(have):
        b_at = col * nb - HALO + first + b
        inside = jnp.where(a_ok & (b_at >= 0) & (b_at < n_col * nb), 1.0, 0.0)
        cell = (first + b) // PER_CELL
        value = predicted[b * height : (b + 1) * height, :] + correction[cell * height : (cell + 1) * height, :]
        sensors[8 + b * height : 8 + (b + 1) * height, :] = jnp.where(inside > 0.5, value, 0.0)
    if k < ITERS:
        vectors = sensor_vectors(sensors, 8 + height, (have - 2) * height)
    else:
        vectors = jnp.concatenate(
            [sensor_vectors(sensors, 8 + (b + 1) * height + HALO, na) for b in range(nb)], axis=0
        )
    result = branch(vectors, w1, b1, w2, b2, w3, b3)
    coeffs[...] = result
    send_means(result, pool, mean_trunk, col, cells, payload)


def field_kernel(na, nb, n_row, n_col, cells, gathered, coarse, coeffs, trunk, out, correction, strip):
    step = pl.program_id(0)
    height = na + 2 * HALO

    @pl.when(step == 0)
    def _():
        found = corrections(gathered, coarse, n_row, n_col, cells)
        correction[...] = jnp.broadcast_to(found, correction.shape)

    values = dot(coeffs[...], trunk[...])
    per = trunk.shape[1] // TILE
    low = low_lanes((8, LANES))
    for pair in range(nb // 2):
        for a in range(0, na, 8):
            cell = 1 + 2 * pair // PER_CELL
            at = cell * height + HALO + a
            add = correction[at : at + 8, :]
            even, odd = (2 * pair * na + a, (2 * pair + 1) * na + a)
            for r in range(0, per, 2):
                lanes = slice(r * TILE, r * TILE + LANES)
                x, y = values[even : even + 8, lanes], values[odd : odd + 8, lanes]
                both = jnp.where(low, x, pltpu.roll(y, TILE, 1)) + add
                strip[pl.ds((pair * na + a) * per + r, 8, stride=per), :] = both
                both = jnp.where(low, pltpu.roll(x, TILE, 1), y) + add
                strip[pl.ds((pair * na + a) * per + r + 1, 8, stride=per), :] = both
        done = strip[pair * na * per : (pair + 1) * na * per, :]
        out[:, :, pair * LANES : (pair + 1) * LANES] = done.reshape(na, per, LANES)


def pool_matrix(na, nb, first, trimmed):
    kx, ky = na // PER_CELL, nb // PER_CELL
    height = na if trimmed else na + 2 * HALO
    skip_a = 0 if trimmed else HALO
    skip_b = HALO - first
    wide = nb + 2 * skip_b
    pool = np.zeros((16, wide * height), np.float32)
    for a in range(na):
        for b in range(nb):
            cell = (a // PER_CELL) * ky + b // PER_CELL
            pool[cell, (b + skip_b) * height + a + skip_a] = 1.0 / PER_CELL**2
    return jnp.asarray(pool, BF16)


def body(
    field_start,
    w_sensor,
    bias_sensor,
    w_middle,
    bias_middle,
    w_latent,
    bias_latent,
    trunk_basis,
    coarse_matrix,
):
    rows_here, cols_here = field_start.shape
    n_row, n_col = lax.axis_size("row"), lax.axis_size("col")
    na, nb = rows_here // TILE, cols_here // TILE
    height = na + 2 * HALO
    kx, ky = na // PER_CELL, nb // PER_CELL
    cells = kx * ky
    devices = n_row * n_col
    latent, points = trunk_basis.shape
    hid = w_sensor.shape[1]
    tile_values, places = 4 * TILE, 8 * TILE
    whole = pl.BlockSpec(memory_space=pltpu.VMEM)
    shape = jax.ShapeDtypeStruct

    def shift(x, axis, forward):
        count = lax.axis_size(axis)
        pairs = [(i, i + 1) if forward else (i + 1, i) for i in range(count - 1)]
        return lax.ppermute(x, axis, pairs)

    spread_np, order = sensor_layout()
    spread = jnp.asarray(spread_np, BF16)
    half = TILE // 2
    blocks = tuple((int(order[i]), half) for i in range(0, places, half))

    steps = 2
    own, up, down = call(
        functools.partial(extract_kernel, na, nb),
        (
            shape((nb * na, tile_values), BF16),
            shape((nb * HALO, tile_values), BF16),
            shape((nb * HALO, tile_values), BF16),
        ),
        field_start.reshape(na, TILE, cols_here),
        grid=(steps,),
        in_specs=[pl.BlockSpec((na // steps, TILE, cols_here), lambda i: (i, 0, 0))],
        out_specs=(
            pl.BlockSpec((nb * na, tile_values), lambda i: (0, 0)),
            pl.BlockSpec((nb * HALO, tile_values), lambda i: (0, 0)),
            pl.BlockSpec((nb * HALO, tile_values), lambda i: (0, 0)),
        ),
        scratch=[pltpu.VMEM((nb * na, LANES), F32)] * 2,
    )
    above, below = shift(down, "row", True), shift(up, "row", False)
    c_above = shift(coarse_matrix[cells - ky :], "row", True)
    c_below = shift(coarse_matrix[:ky], "row", False)

    steps = 4
    width = points // steps
    fixed = lambda i: (0, 0)
    sensor_trunk, mean_trunk, w_first = call(
        lambda t, w, s, *rest: trunk_kernel(t, w, s, blocks, *rest),
        (shape((latent, places), BF16), shape((latent, LANES), F32), shape(w_sensor.shape, BF16)),
        trunk_basis,
        w_sensor,
        spread,
        grid=(steps,),
        in_specs=[
            pl.BlockSpec((latent, width), lambda i: (0, i)),
            pl.BlockSpec(w_sensor.shape, fixed),
            pl.BlockSpec(spread.shape, fixed),
        ],
        out_specs=(
            pl.BlockSpec((latent, places), fixed),
            pl.BlockSpec((latent, LANES), fixed),
            pl.BlockSpec(w_sensor.shape, fixed),
        ),
        scratch=[pltpu.VMEM((latent, 2 * LANES), F32), pltpu.VMEM((latent, 2 * LANES), F32)],
    )

    c_shape = shape((kx + 2, coarse_matrix.shape[1]), F32)
    mid, to_left, to_right, c_to_left, c_to_right = call(
        functools.partial(columns_kernel, na, nb),
        (
            shape((nb * height, tile_values), BF16),
            shape((HALO * height, tile_values), BF16),
            shape((HALO * height, tile_values), BF16),
            c_shape,
            c_shape,
        ),
        own,
        above,
        below,
        coarse_matrix,
        c_above,
        c_below,
    )
    left, right = shift(to_right, "col", True), shift(to_left, "col", False)
    c_left, c_right = shift(c_to_right, "col", True), shift(c_to_left, "col", False)

    net = (
        w_first,
        bias_sensor.reshape(1, hid),
        w_middle,
        bias_middle.reshape(1, hid),
        w_latent,
        bias_latent.reshape(1, latent),
    )
    payload_shape = shape((devices, LANES), F32)
    coarse_shape = shape(((ky + 2) * height, coarse_matrix.shape[1]), F32)
    count = (nb + 2 * HALO - 2) * height
    coeffs, payload, coarse = call(
        functools.partial(first_kernel, na, nb, cells),
        (shape((count, latent), BF16), payload_shape, coarse_shape),
        mid,
        left,
        right,
        coarse_matrix,
        c_above,
        c_below,
        c_left,
        c_right,
        spread,
        *net,
        pool_matrix(na, nb, 1, False),
        mean_trunk,
        scratch=[pltpu.VMEM(((nb + 2 * HALO) * height + 16, places), F32)],
    )
    for k in range(2, ITERS + 1):
        gathered = lax.all_to_all(payload, ("row", "col"), 0, 0, tiled=True)
        have = nb + 2 * HALO - 2 * (k - 1)
        count = nb * na if k == ITERS else (have - 2) * height
        coeffs, payload = call(
            functools.partial(next_kernel, k, na, nb, n_row, n_col, cells),
            (shape((count, latent), BF16), payload_shape),
            gathered,
            coeffs,
            sensor_trunk,
            coarse,
            *net,
            pool_matrix(na, nb, k, k == ITERS),
            mean_trunk,
            scratch=[pltpu.VMEM((have * height + 16, places), F32)],
        )
    gathered = lax.all_to_all(payload, ("row", "col"), 0, 0, tiled=True)
    steps = 8
    out = call(
        functools.partial(field_kernel, na, nb, n_row, n_col, cells),
        shape((na, TILE, cols_here), F32),
        gathered,
        coarse,
        coeffs,
        trunk_basis,
        grid=(steps,),
        in_specs=[
            pl.BlockSpec(payload_shape.shape, fixed),
            pl.BlockSpec(coarse_shape.shape, fixed),
            pl.BlockSpec(coeffs.shape, fixed),
            pl.BlockSpec((latent, points // steps), lambda i: (0, i)),
        ],
        out_specs=pl.BlockSpec((na, TILE // steps, cols_here), lambda i: (0, i, 0)),
        scratch=[
            pltpu.VMEM(((ky + 2) * height, LANES), F32),
            pltpu.VMEM((rows_here * cols_here // steps // LANES, LANES), F32),
        ],
    )
    return out.reshape(rows_here, cols_here)


def solution(mesh):
    placed = (P("row", "col"), P(), P(), P(), P(), P(), P(), P(), P(("row", "col"), None))
    return jax.shard_map(
        body, mesh=mesh, in_specs=placed, out_specs=P("row", "col"), check_vma=False
    )
```

```python
import functools

import jax
import jax.numpy as jnp
import numpy as np
from jax import lax
from jax.experimental import pallas as pl
from jax.experimental.pallas import tpu as pltpu
from jax.sharding import PartitionSpec as P

TILE = 64
ITERS = 4
CELL = 256
PER_CELL = CELL // TILE
HALO = ITERS
LANES = 128
F32 = jnp.float32
BF16 = jnp.bfloat16
VMEM_LIMIT = 48 * 1024 * 1024


def dot(a, b, **kw):
    return jnp.dot(a, b, preferred_element_type=F32, **kw)


def nt_dot(a, b):
    return lax.dot_general(a, b, (((1,), (1,)), ((), ())), preferred_element_type=F32)


def low_lanes(shape):
    return lax.broadcasted_iota(jnp.int32, shape, 1) < TILE


def call(kernel, out_shape, *args, grid=(), in_specs=None, out_specs=None, scratch=(), flops=0):
    whole = pl.BlockSpec(memory_space=pltpu.VMEM)
    specs = {}
    if grid:
        specs["grid"] = grid
    return pl.pallas_call(
        kernel,
        out_shape=out_shape,
        in_specs=in_specs or [whole] * len(args),
        out_specs=out_specs or jax.tree.map(lambda _: whole, out_shape),
        scratch_shapes=list(scratch),
        compiler_params=pltpu.CompilerParams(vmem_limit_bytes=VMEM_LIMIT),
        cost_estimate=pl.CostEstimate(flops=flops, bytes_accessed=1 << 20, transcendentals=0),
        **specs,
    )(*args)


def sensor_layout():
    half = TILE // 2
    row31, row32, col31, col32 = (np.arange(TILE) + TILE * i for i in range(4))
    top, bottom, left, right = (np.arange(2 * TILE) + 2 * TILE * i for i in range(4))
    mid = slice(half, half + TILE)
    groups = [
        (row32, top[mid]),
        (row31, bottom[mid]),
        (np.r_[row32[half:], col32[half:]], np.r_[top[:half], left[:half]]),
        (np.r_[row31[half:], col32[:half]], np.r_[bottom[:half], left[-half:]]),
        (np.r_[row32[:half], col31[half:]], np.r_[top[-half:], right[:half]]),
        (np.r_[row31[:half], col31[:half]], np.r_[bottom[-half:], right[-half:]]),
        (col32, left[mid]),
        (col31, right[mid]),
    ]
    source = np.concatenate([g[0] for g in groups])
    order = np.concatenate([g[1] for g in groups])
    spread = np.zeros((4 * TILE, 8 * TILE), np.float32)
    spread[source, np.arange(8 * TILE)] = 1.0
    return spread, order


def extract_kernel(na, nb, ky, field, coarse, own, up, down, cells, arrived, row_part, col_part, packed):
    cols = field.shape[2]
    here = na // arrived.shape[0]
    copies = [
        pltpu.make_async_copy(field.at[pl.ds(i * here, here)], cells.at[pl.ds(i * here, here)], arrived.at[i])
        for i in range(arrived.shape[0])
    ]
    for copy in copies:
        copy.start()
    sel_row = lax.broadcasted_iota(jnp.int32, (2 * 16, cols), 0)
    sel_col = lax.broadcasted_iota(jnp.int32, (2 * 16, cols), 1)
    side, b_of = sel_row // 16, sel_row % 16
    pick = jnp.where(sel_col == b_of * TILE + (TILE // 2 - 1) + side, 1.0, 0.0).astype(BF16)
    low_row, low_col = low_lanes((here, LANES)), low_lanes((16, LANES))
    for i, copy in enumerate(copies):
        copy.wait()
        base = i * here
        chunk = cells[base : base + here]
        picked = nt_dot(pick, chunk.reshape(here * TILE, cols).astype(BF16))
        r31 = cells[base : base + here, TILE // 2 - 1, :]
        r32 = cells[base : base + here, TILE // 2, :]
        for pair in range(nb // 2):
            lanes = slice(pair * LANES, (pair + 1) * LANES)
            x, y = r31[:, lanes], r32[:, lanes]
            even, odd = 2 * pair * na + base, (2 * pair + 1) * na + base
            row_part[even : even + here, :] = jnp.where(low_row, x, pltpu.roll(y, TILE, 1))
            row_part[odd : odd + here, :] = jnp.where(low_row, pltpu.roll(x, TILE, 1), y)
        for pair in range(here // 2):
            lanes = slice(pair * LANES, (pair + 1) * LANES)
            x, y = picked[0:16, lanes], picked[16:32, lanes]
            even = jnp.where(low_col, x, pltpu.roll(y, TILE, 1))
            odd = jnp.where(low_col, pltpu.roll(x, TILE, 1), y)
            col_part[pl.ds(base + 2 * pair, nb, stride=na), :] = even[0:nb]
            col_part[pl.ds(base + 2 * pair + 1, nb, stride=na), :] = odd[0:nb]
    own[:, 0:LANES] = row_part[...].astype(BF16)
    own[:, LANES : 2 * LANES] = col_part[...].astype(BF16)
    for target, first, line in ((up, 0, 0), (down, na - HALO, coarse.shape[0] - ky)):
        packed[...] = jnp.zeros(packed.shape, F32)
        for b in range(nb):
            rows = slice(b * na + first, b * na + first + HALO)
            packed[0:HALO, 2 * b * LANES : (2 * b + 1) * LANES] = row_part[rows, :]
            packed[0:HALO, (2 * b + 1) * LANES : (2 * b + 2) * LANES] = col_part[rows, :]
        packed[HALO : HALO + ky, :] = coarse[line : line + ky, :]
        target[...] = packed[...].astype(BF16)


def columns_kernel(na, nb, own, above, below, coarse, both, left, right, tall, packed):
    height, values = na + 2 * HALO, 4 * TILE
    kx, ky = na // PER_CELL, nb // PER_CELL
    over, under = above[...].astype(F32), below[...].astype(F32)
    for b in range(nb):
        at = b * height
        tall[at : at + HALO, :] = over[0:HALO, b * values : (b + 1) * values]
        tall[at + HALO : at + HALO + na, :] = own[b * na : (b + 1) * na, :].astype(F32)
        tall[at + HALO + na : at + height, :] = under[0:HALO, b * values : (b + 1) * values]
    both[...] = tall[...].astype(BF16)
    packed[...] = jnp.zeros(packed.shape, F32)
    for target, first, j in ((left, 0, 0), (right, nb - HALO, ky - 1)):
        for b in range(HALO):
            for g in range(height // 8):
                lanes = slice((b * (height // 8) + g) * values, (b * (height // 8) + g + 1) * values)
                at = (first + b) * height + 8 * g
                packed[0:8, lanes] = tall[at : at + 8, :]
        packed[8:9, :] = over[HALO + j : HALO + j + 1, :]
        for i in range(kx):
            packed[9 + i : 10 + i, :] = coarse[i * ky + j : i * ky + j + 1, :]
        packed[9 + kx : 10 + kx, :] = under[HALO + j : HALO + j + 1, :]
        target[...] = packed[...].astype(BF16)


def mean_kernel(trunk, mean_trunk):
    share = jnp.full((trunk.shape[1], LANES), 1.0 / (TILE * TILE), BF16)
    mean_trunk[...] = dot(trunk[...], share)


def trunk_sensors(trunk, spread):
    width = 1024
    per = width // TILE
    point = lax.broadcasted_iota(jnp.int32, (width, LANES), 0)
    lane = lax.broadcasted_iota(jnp.int32, (width, LANES), 1)
    column = point % TILE == TILE // 2 - 1 + lane // TILE
    total = None
    for step in range(trunk.shape[1] // width):
        hit = column & (step * per + point // TILE == lane % TILE)
        part = dot(trunk[:, step * width : (step + 1) * width], jnp.where(hit, 1.0, 0.0).astype(BF16))
        total = part if total is None else total + part
    middle = trunk.shape[1] // 2
    row31 = pltpu.roll(trunk[:, middle - LANES : middle].astype(F32), TILE, 1)
    row32 = pltpu.roll(trunk[:, middle : middle + LANES].astype(F32), TILE, 1)
    rows = jnp.where(low_lanes(row31.shape), row31, row32)
    unique = jnp.concatenate([rows, total], axis=1).astype(BF16)
    return dot(unique, spread[...]).astype(BF16)


def sensor_vectors(sensors, base, count):
    height = HALO * 2 + 16
    low = low_lanes((count, LANES))

    def part(shift, group):
        return sensors[base + shift : base + shift + count, group * LANES : (group + 1) * LANES]

    parts = [
        jnp.where(low, part(-1, 0), part(1, 0)),
        jnp.where(low, part(-height - 1, 1), part(-height + 1, 1)),
        jnp.where(low, part(height - 1, 2), part(height + 1, 2)),
        jnp.where(low, part(-height, 3), part(height, 3)),
    ]
    return jnp.concatenate([p.astype(BF16) for p in parts], axis=1)


def branch(vectors, w1, b1, w2, b2, w3, b3):
    hidden = jnp.tanh(dot(vectors, w1[...]) + b1[...]).astype(BF16)
    hidden = jnp.tanh(dot(hidden, w2[...]) + b2[...]).astype(BF16)
    return (dot(hidden, w3[...]) + b3[...]).astype(BF16)


def send_means(coeffs, pool, mean_trunk, col, cells, payload):
    pooled = dot(pool[...], coeffs)
    means = dot(pooled, mean_trunk[...], precision=lax.Precision.HIGHEST)
    lane = lax.broadcasted_iota(jnp.int32, means.shape, 1)
    cell = lax.broadcasted_iota(jnp.int32, means.shape, 0)
    mine = ((lane - cells * col) & (LANES - 1)) == cell
    line = jnp.sum(jnp.where(mine, means, 0.0), axis=0, keepdims=True)
    payload[...] = jnp.broadcast_to(line, payload.shape)


def corrections(gathered, coarse, n_row, n_col, cells):
    blocks = n_col * cells // LANES
    lane = lax.broadcasted_iota(jnp.int32, (n_col, LANES), 1)
    source = cells * lax.broadcasted_iota(jnp.int32, (n_col, LANES), 0)
    block = (source + ((lane - source) & (LANES - 1))) // LANES
    total = None
    for r in range(n_row):
        values = gathered[r * n_col : (r + 1) * n_col, :]
        for k in range(blocks):
            line = jnp.sum(jnp.where(block == k, values, 0.0), axis=0, keepdims=True)
            at = (r * blocks + k) * LANES
            term = coarse[:, at : at + LANES] * line
            total = term if total is None else total + term
    return jnp.sum(total, axis=1, keepdims=True)


def own_vectors(na, nb, sensors, base):
    height = na + 2 * HALO
    return jnp.concatenate(
        [sensor_vectors(sensors, base + b * height + HALO, na) for b in range(nb)], axis=0
    )


def zero_ends(sensors):
    rows = sensors.shape[0]
    sensors[0:8, :] = jnp.zeros((8, sensors.shape[1]), F32)
    sensors[rows - 8 : rows, :] = jnp.zeros((8, sensors.shape[1]), F32)


def first_kernel(
    na, nb, cells, mid, left, right, spread, w1, b1, w2, b2, w3, b3, pool, mean_trunk, payload, sensors, tiles
):
    height, values = na + 2 * HALO, 4 * TILE
    side = HALO * height
    wide = nb * height
    tiles[side : side + wide, :] = mid[...].astype(F32)
    for source, first in ((left, 0), (right, side + wide)):
        lines = source[...].astype(F32)
        for g in range(side // 8):
            tiles[first + 8 * g : first + 8 * (g + 1), :] = lines[0:8, g * values : (g + 1) * values]
    zero_ends(sensors)
    sensors[8 : 8 + 2 * side + wide, :] = dot(tiles[...].astype(BF16), spread[...])
    result = branch(own_vectors(na, nb, sensors, 8 + side), w1, b1, w2, b2, w3, b3)
    send_means(result, pool, mean_trunk, lax.axis_index("col"), cells, payload)


def first_halo_kernel(
    na, nb, sensors, trunk, spread, c_own, above, below, left, right, w1, b1, w2, b2, w3, b3,
    predicted, sensor_trunk, coarse,
):
    height = na + 2 * HALO
    columns = trunk_sensors(trunk, spread)
    sensor_trunk[...] = columns
    vectors = sensor_vectors(sensors, 8 + height, predicted.shape[0])
    predicted[...] = dot(branch(vectors, w1, b1, w2, b2, w3, b3), columns)
    kx, ky = na // PER_CELL, nb // PER_CELL
    edge = [x[...].astype(F32) for x in (above, below, left, right)]
    for j in range(ky + 2):
        for i in range(kx + 2):
            if j == 0:
                line = edge[2][8 + i : 9 + i, :]
            elif j == ky + 1:
                line = edge[3][8 + i : 9 + i, :]
            elif i == 0:
                line = edge[0][HALO + j - 1 : HALO + j, :]
            elif i == kx + 1:
                line = edge[1][HALO + j - 1 : HALO + j, :]
            else:
                at = (i - 1) * ky + j - 1
                line = c_own[at : at + 1, :]
            at = j * height + i * PER_CELL
            coarse[at : at + PER_CELL, :] = jnp.broadcast_to(line, (PER_CELL, line.shape[1]))


def fill_sensors(na, nb, n_row, n_col, first, columns, predicted, correction, sensors):
    height = na + 2 * HALO
    row, col = lax.axis_index("row"), lax.axis_index("col")
    a_at = row * na - HALO + lax.broadcasted_iota(jnp.int32, (height, 1), 0)
    a_ok = (a_at >= 0) & (a_at < n_row * na)
    zero_ends(sensors)
    for i, b in enumerate(columns):
        b_at = col * nb - HALO + b
        inside = jnp.where(a_ok & (b_at >= 0) & (b_at < n_col * nb), 1.0, 0.0)
        cell = b // PER_CELL
        at = (b - first) * height
        value = predicted[at : at + height, :] + correction[cell * height : (cell + 1) * height, 0:1]
        sensors[8 + i * height : 8 + (i + 1) * height, :] = jnp.where(inside > 0.5, value, 0.0)


def next_kernel(
    k, na, nb, n_row, n_col, cells, gathered, predicted, coarse, w1, b1, w2, b2, w3, b3,
    pool, mean_trunk, payload, extra, sensors,
):
    height = na + 2 * HALO
    found = corrections(gathered, coarse, n_row, n_col, cells)
    columns = range(HALO - 1, HALO + nb + 1)
    fill_sensors(na, nb, n_row, n_col, k - 1, columns, predicted, found, sensors)
    result = branch(own_vectors(na, nb, sensors, 8 + height), w1, b1, w2, b2, w3, b3)
    send_means(result, pool, mean_trunk, lax.axis_index("col"), cells, payload)
    if k < ITERS:
        extra[...] = jnp.broadcast_to(found, extra.shape)
    else:
        extra[...] = result


def halo_kernel(
    k, na, nb, n_row, n_col, before, correction, sensor_trunk, w1, b1, w2, b2, w3, b3, predicted, sensors
):
    columns = range(k - 1, nb + 2 * HALO - (k - 1))
    fill_sensors(na, nb, n_row, n_col, k - 1, columns, before, correction, sensors)
    vectors = sensor_vectors(sensors, 8 + na + 2 * HALO, predicted.shape[0])
    predicted[...] = dot(branch(vectors, w1, b1, w2, b2, w3, b3), sensor_trunk[...])


def predict_kernel(na, nb, steps, coeffs, trunk, out, strip):
    width = trunk.shape[1] // steps
    per = width // TILE
    low = low_lanes((8, LANES))
    for step in range(steps):
        values = dot(coeffs[...], trunk[:, step * width : (step + 1) * width])
        for pair in range(nb // 2):
            for a in range(0, na, 8):
                even, odd = (2 * pair * na + a, (2 * pair + 1) * na + a)
                for r in range(0, per, 2):
                    lanes = slice(r * TILE, r * TILE + LANES)
                    x, y = values[even : even + 8, lanes], values[odd : odd + 8, lanes]
                    at = (pair * na + a) * per + r
                    strip[pl.ds(at, 8, stride=per), :] = jnp.where(low, x, pltpu.roll(y, TILE, 1))
                    strip[pl.ds(at + 1, 8, stride=per), :] = jnp.where(low, pltpu.roll(x, TILE, 1), y)
            done = strip[pair * na * per : (pair + 1) * na * per, :].reshape(na, per, LANES)
            out[:, step * per : (step + 1) * per, pair * LANES : (pair + 1) * LANES] = done


def field_kernel(ky, n_row, n_col, cells, gathered, coarse, prediction, out, correction):
    step = pl.program_id(0)

    @pl.when(step == 0)
    def _():
        found = corrections(gathered, coarse, n_row, n_col, cells)
        correction[...] = jnp.broadcast_to(found, correction.shape)

    here = out.shape[0]
    for j in range(ky):
        add = correction[pl.ds(step * ky + j, 1), :].reshape(1, 1, LANES)
        for lane in range(j * CELL, (j + 1) * CELL, LANES):
            lanes = slice(lane, lane + LANES)
            out[:, :, lanes] = prediction[pl.ds(step * here, here), :, lanes] + add


def pool_matrix(na, nb):
    ky = nb // PER_CELL
    pool = np.zeros((16, nb * na), np.float32)
    for a in range(na):
        for b in range(nb):
            pool[(a // PER_CELL) * ky + b // PER_CELL, b * na + a] = 1.0 / PER_CELL**2
    return jnp.asarray(pool, BF16)


def body(
    field_start,
    w_sensor,
    bias_sensor,
    w_middle,
    bias_middle,
    w_latent,
    bias_latent,
    trunk_basis,
    coarse_matrix,
):
    rows_here, cols_here = field_start.shape
    n_row, n_col = lax.axis_size("row"), lax.axis_size("col")
    na, nb = rows_here // TILE, cols_here // TILE
    height = na + 2 * HALO
    kx, ky = na // PER_CELL, nb // PER_CELL
    cells = kx * ky
    devices = n_row * n_col
    latent = trunk_basis.shape[0]
    hid = w_sensor.shape[1]
    tile_values, places = 4 * TILE, 8 * TILE
    total = coarse_matrix.shape[1]
    whole = pl.BlockSpec(memory_space=pltpu.VMEM)
    shape = jax.ShapeDtypeStruct
    part = functools.partial

    def shift(x, axis, forward):
        count = lax.axis_size(axis)
        pairs = [(i, i + 1) if forward else (i + 1, i) for i in range(count - 1)]
        return lax.ppermute(x, axis, pairs)

    def exchange(x):
        return lax.all_to_all(x, ("row", "col"), 0, 0, tiled=True)

    spread_np, order = sensor_layout()
    spread = jnp.asarray(spread_np, BF16)
    half = TILE // 2
    w_first = jnp.concatenate([w_sensor[at : at + half] for at in order[::half].tolist()], axis=0)
    net = (
        w_first,
        bias_sensor.reshape(1, hid),
        w_middle,
        bias_middle.reshape(1, hid),
        w_latent,
        bias_latent.reshape(1, latent),
    )
    pool = pool_matrix(na, nb)

    own, up, down = call(
        part(extract_kernel, na, nb, ky),
        (shape((nb * na, tile_values), BF16), shape((8, total), BF16), shape((8, total), BF16)),
        field_start.reshape(na, TILE, cols_here),
        coarse_matrix,
        in_specs=[pl.BlockSpec(memory_space=pltpu.HBM), whole],
        scratch=[
            pltpu.VMEM((na, TILE, cols_here), F32),
            pltpu.SemaphoreType.DMA((4,)),
            pltpu.VMEM((nb * na, LANES), F32),
            pltpu.VMEM((nb * na, LANES), F32),
            pltpu.VMEM((8, total), F32),
        ],
    )
    above, below = shift(down, "row", True), shift(up, "row", False)
    mean_trunk = call(mean_kernel, shape((latent, LANES), F32), trunk_basis, flops=1 << 28)
    mid, to_left, to_right = call(
        part(columns_kernel, na, nb),
        (shape((nb * height, tile_values), BF16), shape((16, total), BF16), shape((16, total), BF16)),
        own,
        above,
        below,
        coarse_matrix,
        scratch=[pltpu.VMEM((nb * height, tile_values), F32), pltpu.VMEM((16, total), F32)],
    )
    left, right = shift(to_right, "col", True), shift(to_left, "col", False)

    def region(k):
        return (nb + 2 * HALO - 2 * k) * height

    payload_shape = shape((devices, LANES), F32)
    payload, sensors = call(
        part(first_kernel, na, nb, cells),
        (payload_shape, shape((region(0) + 16, places), F32)),
        mid,
        left,
        right,
        spread,
        *net,
        pool,
        mean_trunk,
        scratch=[pltpu.VMEM((region(0), tile_values), F32)],
    )
    gathered = exchange(payload)
    predicted, sensor_trunk, coarse = call(
        part(first_halo_kernel, na, nb),
        (
            shape((region(1), places), F32),
            shape((latent, places), BF16),
            shape(((ky + 2) * height, total), F32),
        ),
        sensors,
        trunk_basis,
        spread,
        coarse_matrix,
        above,
        below,
        left,
        right,
        *net,
        flops=1 << 32,
    )
    for k in range(2, ITERS + 1):
        extra = shape((coarse.shape[0], LANES), F32) if k < ITERS else shape((nb * na, latent), BF16)
        payload, extra = call(
            part(next_kernel, k, na, nb, n_row, n_col, cells),
            (payload_shape, extra),
            gathered,
            predicted,
            coarse,
            *net,
            pool,
            mean_trunk,
            scratch=[pltpu.VMEM(((nb + 2) * height + 16, places), F32)],
        )
        gathered = exchange(payload)
        if k < ITERS:
            predicted = call(
                part(halo_kernel, k, na, nb, n_row, n_col),
                shape((region(k), places), F32),
                predicted,
                extra,
                sensor_trunk,
                *net,
                scratch=[pltpu.VMEM((region(k - 1) + 16, places), F32)],
                flops=1 << 31,
            )
    steps = 8
    prediction = call(
        part(predict_kernel, na, nb, steps),
        shape((na, TILE, cols_here), F32),
        extra,
        trunk_basis,
        scratch=[pltpu.VMEM((rows_here * cols_here // steps // LANES, LANES), F32)],
        flops=1 << 32,
    )
    out = call(
        part(field_kernel, ky, n_row, n_col, cells),
        shape((na, TILE, cols_here), F32),
        gathered,
        coarse_matrix,
        prediction,
        grid=(kx,),
        out_specs=pl.BlockSpec((PER_CELL, TILE, cols_here), lambda i: (i, 0, 0)),
        scratch=[pltpu.VMEM((cells, LANES), F32)],
    )
    return out.reshape(rows_here, cols_here)


def solution(mesh):
    placed = (P("row", "col"), P(), P(), P(), P(), P(), P(), P(), P(("row", "col"), None))
    return jax.shard_map(
        body, mesh=mesh, in_specs=placed, out_specs=P("row", "col"), check_vma=False
    )
```

```python
import functools

import jax
import jax.numpy as jnp
import numpy as np
from jax import lax
from jax.experimental import pallas as pl
from jax.experimental.pallas import tpu as pltpu
from jax.sharding import PartitionSpec as P

TILE = 64
ITERS = 4
CELL = 256
PER_CELL = CELL // TILE
HALO = ITERS
LANES = 128
F32 = jnp.float32
BF16 = jnp.bfloat16
VMEM_LIMIT = 48 * 1024 * 1024
VMEM_LIMIT_FIRST = 52 * 1024 * 1024


def dot(a, b, **kw):
    return jnp.dot(a, b, preferred_element_type=F32, **kw)


def nt_dot(a, b):
    return lax.dot_general(a, b, (((1,), (1,)), ((), ())), preferred_element_type=F32)


def low_lanes(shape):
    return lax.broadcasted_iota(jnp.int32, shape, 1) < TILE


def call(kernel, out_shape, *args, grid=(), in_specs=None, out_specs=None, scratch=(), flops=0, vmem=VMEM_LIMIT):
    whole = pl.BlockSpec(memory_space=pltpu.VMEM)
    specs = {}
    if grid:
        specs["grid"] = grid
    return pl.pallas_call(
        kernel,
        out_shape=out_shape,
        in_specs=in_specs or [whole] * len(args),
        out_specs=out_specs or jax.tree.map(lambda _: whole, out_shape),
        scratch_shapes=list(scratch),
        compiler_params=pltpu.CompilerParams(vmem_limit_bytes=vmem),
        cost_estimate=pl.CostEstimate(flops=flops, bytes_accessed=1 << 20, transcendentals=0),
        **specs,
    )(*args)


def sensor_layout():
    half = TILE // 2
    row31, row32, col31, col32 = (np.arange(TILE) + TILE * i for i in range(4))
    top, bottom, left, right = (np.arange(2 * TILE) + 2 * TILE * i for i in range(4))
    mid = slice(half, half + TILE)
    groups = [
        (row32, top[mid]),
        (row31, bottom[mid]),
        (np.r_[row32[half:], col32[half:]], np.r_[top[:half], left[:half]]),
        (np.r_[row31[half:], col32[:half]], np.r_[bottom[:half], left[-half:]]),
        (np.r_[row32[:half], col31[half:]], np.r_[top[-half:], right[:half]]),
        (np.r_[row31[:half], col31[:half]], np.r_[bottom[-half:], right[-half:]]),
        (col32, left[mid]),
        (col31, right[mid]),
    ]
    source = np.concatenate([g[0] for g in groups])
    order = np.concatenate([g[1] for g in groups])
    spread = np.zeros((4 * TILE, 8 * TILE), np.float32)
    spread[source, np.arange(8 * TILE)] = 1.0
    return spread, order


def extract_kernel(
    na, nb, ky, field, coarse_hbm, own, up, down, cells, coarse, arrived, coarse_arrived, row_part, col_part, packed
):
    cols = field.shape[2]
    here = na // arrived.shape[0]
    copies = [
        pltpu.make_async_copy(field.at[pl.ds(i * here, here)], cells.at[pl.ds(i * here, here)], arrived.at[i])
        for i in range(arrived.shape[0])
    ]
    for copy in copies:
        copy.start()
    coarse_copy = pltpu.make_async_copy(coarse_hbm, coarse, coarse_arrived)
    coarse_copy.start()
    sel_row = lax.broadcasted_iota(jnp.int32, (2 * 16, cols), 0)
    sel_col = lax.broadcasted_iota(jnp.int32, (2 * 16, cols), 1)
    side, b_of = sel_row // 16, sel_row % 16
    pick = jnp.where(sel_col == b_of * TILE + (TILE // 2 - 1) + side, 1.0, 0.0).astype(BF16)
    low_row, low_col = low_lanes((here, LANES)), low_lanes((16, LANES))
    for i, copy in enumerate(copies):
        copy.wait()
        base = i * here
        chunk = cells[base : base + here]
        picked = nt_dot(pick, chunk.reshape(here * TILE, cols).astype(BF16))
        r31 = cells[base : base + here, TILE // 2 - 1, :]
        r32 = cells[base : base + here, TILE // 2, :]
        for pair in range(nb // 2):
            lanes = slice(pair * LANES, (pair + 1) * LANES)
            x, y = r31[:, lanes], r32[:, lanes]
            even, odd = 2 * pair * na + base, (2 * pair + 1) * na + base
            row_part[even : even + here, :] = jnp.where(low_row, x, pltpu.roll(y, TILE, 1))
            row_part[odd : odd + here, :] = jnp.where(low_row, pltpu.roll(x, TILE, 1), y)
        for pair in range(here // 2):
            lanes = slice(pair * LANES, (pair + 1) * LANES)
            x, y = picked[0:16, lanes], picked[16:32, lanes]
            even = jnp.where(low_col, x, pltpu.roll(y, TILE, 1))
            odd = jnp.where(low_col, pltpu.roll(x, TILE, 1), y)
            col_part[pl.ds(base + 2 * pair, nb, stride=na), :] = even[0:nb]
            col_part[pl.ds(base + 2 * pair + 1, nb, stride=na), :] = odd[0:nb]
    own[:, 0:LANES] = row_part[...].astype(BF16)
    own[:, LANES : 2 * LANES] = col_part[...].astype(BF16)
    coarse_copy.wait()
    for target, first, line in ((up, 0, 0), (down, na - HALO, coarse.shape[0] - ky)):
        packed[...] = jnp.zeros(packed.shape, F32)
        for b in range(nb):
            rows = slice(b * na + first, b * na + first + HALO)
            packed[0:HALO, 2 * b * LANES : (2 * b + 1) * LANES] = row_part[rows, :]
            packed[0:HALO, (2 * b + 1) * LANES : (2 * b + 2) * LANES] = col_part[rows, :]
        packed[HALO : HALO + ky, :] = coarse[line : line + ky, :]
        target[...] = packed[...].astype(BF16)


def columns_kernel(na, nb, own, above, below, coarse, both, left, right, tall, packed):
    height, values = na + 2 * HALO, 4 * TILE
    kx, ky = na // PER_CELL, nb // PER_CELL
    over, under = above[...].astype(F32), below[...].astype(F32)
    for b in range(nb):
        at = b * height
        tall[at : at + HALO, :] = over[0:HALO, b * values : (b + 1) * values]
        tall[at + HALO : at + HALO + na, :] = own[b * na : (b + 1) * na, :].astype(F32)
        tall[at + HALO + na : at + height, :] = under[0:HALO, b * values : (b + 1) * values]
    both[...] = tall[...].astype(BF16)
    packed[...] = jnp.zeros(packed.shape, F32)
    for target, first, j in ((left, 0, 0), (right, nb - HALO, ky - 1)):
        for b in range(HALO):
            for g in range(height // 8):
                lanes = slice((b * (height // 8) + g) * values, (b * (height // 8) + g + 1) * values)
                at = (first + b) * height + 8 * g
                packed[0:8, lanes] = tall[at : at + 8, :]
        packed[8:9, :] = over[HALO + j : HALO + j + 1, :]
        for i in range(kx):
            packed[9 + i : 10 + i, :] = coarse[i * ky + j : i * ky + j + 1, :]
        packed[9 + kx : 10 + kx, :] = under[HALO + j : HALO + j + 1, :]
        target[...] = packed[...].astype(BF16)


def trunk_kernel(blocks, trunk_hbm, w_sensor, spread, sensor_trunk, mean_trunk, w_out, trunk, arrived):
    steps = arrived.shape[0]
    width = trunk.shape[1] // steps
    per = width // TILE
    copies = [
        pltpu.make_async_copy(
            trunk_hbm.at[:, pl.ds(i * width, width)], trunk.at[:, pl.ds(i * width, width)], arrived.at[i]
        )
        for i in range(steps)
    ]
    for copy in copies:
        copy.start()
    at = 0
    for start, size in blocks:
        w_out[at : at + size, :] = w_sensor[start : start + size, :]
        at += size
    point = lax.broadcasted_iota(jnp.int32, (width, LANES), 0)
    lane = lax.broadcasted_iota(jnp.int32, (width, LANES), 1)
    column = point % TILE == TILE // 2 - 1 + lane // TILE
    away = jnp.where(column, lane % TILE - point // TILE, -1)
    share = jnp.full((width, LANES), 1.0 / (TILE * TILE), BF16)
    total = None
    for step, copy in enumerate(copies):
        copy.wait()
        pick = jnp.where(away == step * per, 1.0, 0.0).astype(BF16)
        part = dot(trunk[:, step * width : (step + 1) * width], jnp.concatenate([pick, share], axis=1))
        total = part if total is None else total + part
    middle = trunk.shape[1] // 2
    row31 = pltpu.roll(trunk[:, middle - LANES : middle].astype(F32), TILE, 1)
    row32 = pltpu.roll(trunk[:, middle : middle + LANES].astype(F32), TILE, 1)
    rows = jnp.where(low_lanes(row31.shape), row31, row32)
    unique = jnp.concatenate([rows, total[:, 0:LANES]], axis=1).astype(BF16)
    sensor_trunk[...] = dot(unique, spread[...]).astype(BF16)
    mean_trunk[...] = total[:, LANES : 2 * LANES]


def sensor_vectors(sensors, base, count):
    height = HALO * 2 + 16
    low = low_lanes((count, LANES))

    def part(shift, group):
        return sensors[base + shift : base + shift + count, group * LANES : (group + 1) * LANES]

    parts = [
        jnp.where(low, part(-1, 0), part(1, 0)),
        jnp.where(low, part(-height - 1, 1), part(-height + 1, 1)),
        jnp.where(low, part(height - 1, 2), part(height + 1, 2)),
        jnp.where(low, part(-height, 3), part(height, 3)),
    ]
    return jnp.concatenate([p.astype(BF16) for p in parts], axis=1)


def branch(vectors, w1, b1, w2, b2, w3, b3):
    hidden = jnp.tanh(dot(vectors, w1[...]) + b1[...]).astype(BF16)
    hidden = jnp.tanh(dot(hidden, w2[...]) + b2[...]).astype(BF16)
    return (dot(hidden, w3[...]) + b3[...]).astype(BF16)


def send_means(coeffs, pool, mean_trunk, col, cells, payload):
    pooled = dot(pool[...], coeffs)
    means = dot(pooled, mean_trunk[...], precision=lax.Precision.HIGHEST)
    lane = lax.broadcasted_iota(jnp.int32, means.shape, 1)
    cell = lax.broadcasted_iota(jnp.int32, means.shape, 0)
    mine = ((lane - cells * col) & (LANES - 1)) == cell
    line = jnp.sum(jnp.where(mine, means, 0.0), axis=0, keepdims=True)
    payload[...] = jnp.broadcast_to(line, payload.shape)


def corrections(gathered, coarse, n_row, n_col, cells):
    blocks = n_col * cells // LANES
    lane = lax.broadcasted_iota(jnp.int32, (n_col, LANES), 1)
    source = cells * lax.broadcasted_iota(jnp.int32, (n_col, LANES), 0)
    block = (source + ((lane - source) & (LANES - 1))) // LANES
    total = None
    for r in range(n_row):
        values = gathered[r * n_col : (r + 1) * n_col, :]
        for k in range(blocks):
            line = jnp.sum(jnp.where(block == k, values, 0.0), axis=0, keepdims=True)
            at = (r * blocks + k) * LANES
            term = coarse[:, at : at + LANES] * line
            total = term if total is None else total + term
    return jnp.sum(total, axis=1, keepdims=True)


def own_vectors(na, nb, sensors, base):
    height = na + 2 * HALO
    return jnp.concatenate(
        [sensor_vectors(sensors, base + b * height + HALO, na) for b in range(nb)], axis=0
    )


def zero_ends(sensors):
    rows = sensors.shape[0]
    sensors[0:8, :] = jnp.zeros((8, sensors.shape[1]), F32)
    sensors[rows - 8 : rows, :] = jnp.zeros((8, sensors.shape[1]), F32)


def first_kernel(
    na, nb, cells, mid, left, right, above, below, c_own, spread, w1, b1, w2, b2, w3, b3, pool, mean_trunk,
    coeffs, payload, coarse, sensors, tiles,
):
    height, values = na + 2 * HALO, 4 * TILE
    side = HALO * height
    wide = nb * height
    tiles[side : side + wide, :] = mid[...].astype(F32)
    edge = [x[...].astype(F32) for x in (above, below, left, right)]
    for lines, first in ((edge[2], 0), (edge[3], side + wide)):
        for g in range(side // 8):
            tiles[first + 8 * g : first + 8 * (g + 1), :] = lines[0:8, g * values : (g + 1) * values]
    zero_ends(sensors)
    sensors[8 : 8 + 2 * side + wide, :] = dot(tiles[...].astype(BF16), spread[...])
    vectors = sensor_vectors(sensors, 8 + height, coeffs.shape[0])
    result = branch(vectors, w1, b1, w2, b2, w3, b3)
    coeffs[...] = result
    send_means(result, pool, mean_trunk, lax.axis_index("col"), cells, payload)
    kx, ky = na // PER_CELL, nb // PER_CELL
    coarse[0 : kx + 2, :] = edge[2][8 : 10 + kx, :]
    coarse[8 * (ky + 1) : 8 * (ky + 1) + kx + 2, :] = edge[3][8 : 10 + kx, :]
    for j in range(ky):
        at = 8 * (j + 1)
        coarse[at : at + 1, :] = edge[0][HALO + j : HALO + j + 1, :]
        for i in range(kx):
            coarse[at + 1 + i : at + 2 + i, :] = c_own[i * ky + j : i * ky + j + 1, :]
        coarse[at + 1 + kx : at + 2 + kx, :] = edge[1][HALO + j : HALO + j + 1, :]
    for j in range(ky + 2):
        at = 8 * j + kx + 2
        coarse[at : 8 * (j + 1), :] = jnp.zeros((6 - kx, coarse.shape[1]), F32)


def next_kernel(
    k, na, nb, n_row, n_col, cells, gathered, before, sensor_trunk, coarse, w1, b1, w2, b2, w3, b3,
    pool, mean_trunk, coeffs, payload, sensors, lines,
):
    height = na + 2 * HALO
    predicted = dot(before[...], sensor_trunk[...])
    found = corrections(gathered, coarse, n_row, n_col, cells)
    found = jnp.broadcast_to(found, (found.shape[0], sensors.shape[1]))
    row, col = lax.axis_index("row"), lax.axis_index("col")
    a_at = row * na - HALO + lax.broadcasted_iota(jnp.int32, (height, 1), 0)
    a_ok = (a_at >= 0) & (a_at < n_row * na)
    for j in range(nb // PER_CELL + 2):
        for i in range(height // PER_CELL):
            at = j * height + i * PER_CELL
            lines[at : at + PER_CELL, :] = jnp.broadcast_to(
                found[8 * j + i : 8 * j + i + 1, :], (PER_CELL, found.shape[1])
            )
    zero_ends(sensors)
    first = k - 1
    have = nb + 2 * HALO - 2 * first
    for i in range(have):
        b = first + i
        b_at = col * nb - HALO + b
        inside = jnp.where(a_ok & (b_at >= 0) & (b_at < n_col * nb), 1.0, 0.0)
        cell = b // PER_CELL
        value = predicted[i * height : (i + 1) * height, :] + lines[cell * height : (cell + 1) * height, :]
        sensors[8 + i * height : 8 + (i + 1) * height, :] = jnp.where(inside > 0.5, value, 0.0)
    if k < ITERS:
        vectors = sensor_vectors(sensors, 8 + height, coeffs.shape[0])
    else:
        vectors = own_vectors(na, nb, sensors, 8 + height)
    result = branch(vectors, w1, b1, w2, b2, w3, b3)
    coeffs[...] = result
    send_means(result, pool, mean_trunk, col, cells, payload)


def field_kernel(na, nb, n_row, n_col, cells, gathered, coarse, coeffs, trunk, out, correction, strip, ready, sent):
    steps = ready.shape[0]
    width = trunk.shape[1] // steps
    per = width // TILE
    ky = nb // PER_CELL
    found = corrections(gathered, coarse, n_row, n_col, cells)
    correction[...] = jnp.broadcast_to(found, correction.shape)
    upper = lax.broadcasted_iota(jnp.int32, (8, LANES), 0) < PER_CELL
    adds = {}
    for a in range(0, na, 8):
        for j in range(ky):
            at = a // PER_CELL * ky + j
            adds[a, j] = jnp.where(upper, correction[at : at + 1, :], correction[at + ky : at + ky + 1, :])
    low = low_lanes((8, LANES))
    copies = []
    for step in range(steps):
        values = dot(coeffs[...], trunk[:, step * width : (step + 1) * width])
        for pair in range(nb // 2):
            for a in range(0, na, 8):
                add = adds[a, 2 * pair // PER_CELL]
                even, odd = (2 * pair * na + a, (2 * pair + 1) * na + a)
                for r in range(0, per, 2):
                    lanes = slice(r * TILE, r * TILE + LANES)
                    x, y = values[even : even + 8, lanes], values[odd : odd + 8, lanes]
                    at = (pair * na + a) * per + r
                    strip[pl.ds(at, 8, stride=per), :] = jnp.where(low, x, pltpu.roll(y, TILE, 1)) + add
                    strip[pl.ds(at + 1, 8, stride=per), :] = jnp.where(low, pltpu.roll(x, TILE, 1), y) + add
            done = strip[pair * na * per : (pair + 1) * na * per, :].reshape(na, per, LANES)
            ready[step, :, :, pair * LANES : (pair + 1) * LANES] = done
        copies.append(
            pltpu.make_async_copy(ready.at[step], out.at[:, pl.ds(step * per, per), :], sent.at[step])
        )
        copies[-1].start()
    for copy in copies:
        copy.wait()


def pool_matrix(na, nb, first, trimmed):
    kx, ky = na // PER_CELL, nb // PER_CELL
    height = na if trimmed else na + 2 * HALO
    skip_a = 0 if trimmed else HALO
    skip_b = HALO - first
    wide = nb + 2 * skip_b
    pool = np.zeros((16, wide * height), np.float32)
    for a in range(na):
        for b in range(nb):
            cell = (a // PER_CELL) * ky + b // PER_CELL
            pool[cell, (b + skip_b) * height + a + skip_a] = 1.0 / PER_CELL**2
    return jnp.asarray(pool, BF16)


def body(
    field_start,
    w_sensor,
    bias_sensor,
    w_middle,
    bias_middle,
    w_latent,
    bias_latent,
    trunk_basis,
    coarse_matrix,
):
    rows_here, cols_here = field_start.shape
    n_row, n_col = lax.axis_size("row"), lax.axis_size("col")
    na, nb = rows_here // TILE, cols_here // TILE
    height = na + 2 * HALO
    kx, ky = na // PER_CELL, nb // PER_CELL
    cells = kx * ky
    devices = n_row * n_col
    latent = trunk_basis.shape[0]
    hid = w_sensor.shape[1]
    tile_values, places = 4 * TILE, 8 * TILE
    total = coarse_matrix.shape[1]
    whole = pl.BlockSpec(memory_space=pltpu.VMEM)
    shape = jax.ShapeDtypeStruct
    part = functools.partial

    def shift(x, axis, forward):
        count = lax.axis_size(axis)
        pairs = [(i, i + 1) if forward else (i + 1, i) for i in range(count - 1)]
        return lax.ppermute(x, axis, pairs)

    def exchange(x):
        return lax.all_to_all(x, ("row", "col"), 0, 0, tiled=True)

    spread_np, order = sensor_layout()
    spread = jnp.asarray(spread_np, BF16)
    half = TILE // 2
    blocks = tuple((int(at), half) for at in order[::half])
    hbm = pl.BlockSpec(memory_space=pltpu.HBM)

    own, up, down = call(
        part(extract_kernel, na, nb, ky),
        (shape((nb * na, tile_values), BF16), shape((8, total), BF16), shape((8, total), BF16)),
        field_start.reshape(na, TILE, cols_here),
        coarse_matrix,
        in_specs=[hbm, hbm],
        scratch=[
            pltpu.VMEM((na, TILE, cols_here), F32),
            pltpu.VMEM(coarse_matrix.shape, F32),
            pltpu.SemaphoreType.DMA((4,)),
            pltpu.SemaphoreType.DMA,
            pltpu.VMEM((nb * na, LANES), F32),
            pltpu.VMEM((nb * na, LANES), F32),
            pltpu.VMEM((8, total), F32),
        ],
        vmem=VMEM_LIMIT_FIRST,
    )
    above, below = shift(down, "row", True), shift(up, "row", False)
    sensor_trunk, mean_trunk, w_first = call(
        part(trunk_kernel, blocks),
        (shape((latent, places), BF16), shape((latent, LANES), F32), shape(w_sensor.shape, BF16)),
        trunk_basis,
        w_sensor,
        spread,
        in_specs=[hbm, whole, whole],
        scratch=[pltpu.VMEM(trunk_basis.shape, BF16), pltpu.SemaphoreType.DMA((4,))],
        flops=1 << 30,
    )
    above, below, w_first = lax.optimization_barrier((above, below, w_first))
    net = (
        w_first,
        bias_sensor.reshape(1, hid),
        w_middle,
        bias_middle.reshape(1, hid),
        w_latent,
        bias_latent.reshape(1, latent),
    )
    mid, to_left, to_right = call(
        part(columns_kernel, na, nb),
        (shape((nb * height, tile_values), BF16), shape((16, total), BF16), shape((16, total), BF16)),
        own,
        above,
        below,
        coarse_matrix,
        scratch=[pltpu.VMEM((nb * height, tile_values), F32), pltpu.VMEM((16, total), F32)],
    )
    left, right = shift(to_right, "col", True), shift(to_left, "col", False)

    def region(k):
        return (nb + 2 * HALO - 2 * k) * height

    payload_shape = shape((devices, LANES), F32)
    coeffs, payload, coarse = call(
        part(first_kernel, na, nb, cells),
        (shape((region(1), latent), BF16), payload_shape, shape((8 * (ky + 2), total), F32)),
        mid,
        left,
        right,
        above,
        below,
        coarse_matrix,
        spread,
        *net,
        pool_matrix(na, nb, 1, False),
        mean_trunk,
        scratch=[pltpu.VMEM((region(0) + 16, places), F32), pltpu.VMEM((region(0), tile_values), F32)],
    )
    for k in range(2, ITERS + 1):
        gathered = exchange(payload)
        coeffs, payload = call(
            part(next_kernel, k, na, nb, n_row, n_col, cells),
            (shape((region(k) if k < ITERS else nb * na, latent), BF16), payload_shape),
            gathered,
            coeffs,
            sensor_trunk,
            coarse,
            *net,
            pool_matrix(na, nb, k, k == ITERS),
            mean_trunk,
            scratch=[
                pltpu.VMEM((region(k - 1) + 16, places), F32),
                pltpu.VMEM(((ky + 2) * height, places), F32),
            ],
        )
    gathered = exchange(payload)
    steps = 8
    out = call(
        part(field_kernel, na, nb, n_row, n_col, cells),
        shape((na, TILE, cols_here), F32),
        gathered,
        coarse_matrix,
        coeffs,
        trunk_basis,
        out_specs=hbm,
        scratch=[
            pltpu.VMEM((cells, LANES), F32),
            pltpu.VMEM((rows_here * cols_here // steps // LANES, LANES), F32),
            pltpu.VMEM((steps, na, TILE // steps, cols_here), F32),
            pltpu.SemaphoreType.DMA((steps,)),
        ],
    )
    return out.reshape(rows_here, cols_here)


def solution(mesh):
    placed = (P("row", "col"), P(), P(), P(), P(), P(), P(), P(), P(("row", "col"), None))
    return jax.shard_map(
        body, mesh=mesh, in_specs=placed, out_specs=P("row", "col"), check_vma=False
    )
```

```python
import functools

import jax
import jax.numpy as jnp
import numpy as np
from jax import lax
from jax.experimental import pallas as pl
from jax.experimental.pallas import tpu as pltpu
from jax.sharding import PartitionSpec as P

TILE = 64
ITERS = 4
CELL = 256
PER_CELL = CELL // TILE
HALO = ITERS
LANES = 128
F32 = jnp.float32
BF16 = jnp.bfloat16
VMEM_LIMIT = 48 * 1024 * 1024


def dot(a, b, **kw):
    return jnp.dot(a, b, preferred_element_type=F32, **kw)


def nt_dot(a, b):
    return lax.dot_general(a, b, (((1,), (1,)), ((), ())), preferred_element_type=F32)


def low_lanes(shape):
    return lax.broadcasted_iota(jnp.int32, shape, 1) < TILE


def call(kernel, out_shape, *args, grid=(), in_specs=None, out_specs=None, scratch=(), flops=1 << 31, vmem=VMEM_LIMIT):
    whole = pl.BlockSpec(memory_space=pltpu.VMEM)
    specs = {}
    if grid:
        specs["grid"] = grid
    return pl.pallas_call(
        kernel,
        out_shape=out_shape,
        in_specs=in_specs or [whole] * len(args),
        out_specs=out_specs or jax.tree.map(lambda _: whole, out_shape),
        scratch_shapes=list(scratch),
        compiler_params=pltpu.CompilerParams(vmem_limit_bytes=vmem),
        cost_estimate=pl.CostEstimate(flops=flops, bytes_accessed=1 << 20, transcendentals=0),
        **specs,
    )(*args)


def sensor_layout():
    half = TILE // 2
    row31, row32, col31, col32 = (np.arange(TILE) + TILE * i for i in range(4))
    top, bottom, left, right = (np.arange(2 * TILE) + 2 * TILE * i for i in range(4))
    mid = slice(half, half + TILE)
    groups = [
        (row32, top[mid]),
        (row31, bottom[mid]),
        (np.r_[row32[half:], col32[half:]], np.r_[top[:half], left[:half]]),
        (np.r_[row31[half:], col32[:half]], np.r_[bottom[:half], left[-half:]]),
        (np.r_[row32[:half], col31[half:]], np.r_[top[-half:], right[:half]]),
        (np.r_[row31[:half], col31[:half]], np.r_[bottom[-half:], right[-half:]]),
        (col32, left[mid]),
        (col31, right[mid]),
    ]
    source = np.concatenate([g[0] for g in groups])
    order = np.concatenate([g[1] for g in groups])
    spread = np.zeros((4 * TILE, 8 * TILE), np.float32)
    spread[source, np.arange(8 * TILE)] = 1.0
    return spread, order


def extract_kernel(na, nb, cells, row_part, col_part):
    cols = cells.shape[2]
    here = 8
    sel_row = lax.broadcasted_iota(jnp.int32, (2 * 16, cols), 0)
    sel_col = lax.broadcasted_iota(jnp.int32, (2 * 16, cols), 1)
    side, b_of = sel_row // 16, sel_row % 16
    pick = jnp.where(sel_col == b_of * TILE + (TILE // 2 - 1) + side, 1.0, 0.0).astype(BF16)
    low_row, low_col = low_lanes((here, LANES)), low_lanes((16, LANES))
    for base in range(0, na, here):
        chunk = cells[base : base + here]
        picked = nt_dot(pick, chunk.reshape(here * TILE, cols).astype(BF16))
        r31 = cells[base : base + here, TILE // 2 - 1, :]
        r32 = cells[base : base + here, TILE // 2, :]
        for pair in range(nb // 2):
            lanes = slice(pair * LANES, (pair + 1) * LANES)
            x, y = r31[:, lanes], r32[:, lanes]
            even, odd = 2 * pair * na + base, (2 * pair + 1) * na + base
            row_part[even : even + here, :] = jnp.where(low_row, x, pltpu.roll(y, TILE, 1))
            row_part[odd : odd + here, :] = jnp.where(low_row, pltpu.roll(x, TILE, 1), y)
        for pair in range(here // 2):
            lanes = slice(pair * LANES, (pair + 1) * LANES)
            x, y = picked[0:16, lanes], picked[16:32, lanes]
            even = jnp.where(low_col, x, pltpu.roll(y, TILE, 1))
            odd = jnp.where(low_col, pltpu.roll(x, TILE, 1), y)
            col_part[pl.ds(base + 2 * pair, nb, stride=na), :] = even[0:nb]
            col_part[pl.ds(base + 2 * pair + 1, nb, stride=na), :] = odd[0:nb]


def pack_kernel(na, nb, ky, row_part, col_part, coarse, up, down, packed):
    packed[...] = jnp.zeros(packed.shape, F32)
    for target, first, line in ((up, 0, 0), (down, na - HALO, coarse.shape[0] - ky)):
        for b in range(nb):
            rows = slice(b * na + first, b * na + first + HALO)
            packed[0:HALO, 2 * b * LANES : (2 * b + 1) * LANES] = row_part[rows, :]
            packed[0:HALO, (2 * b + 1) * LANES : (2 * b + 2) * LANES] = col_part[rows, :]
        packed[HALO : HALO + ky, :] = coarse[line : line + ky, :]
        target[...] = packed[...].astype(BF16)


def columns_kernel(na, nb, row_part, col_part, above, below, coarse, both, left, right, tall, packed):
    height, values = na + 2 * HALO, 4 * TILE
    kx, ky = na // PER_CELL, nb // PER_CELL
    over, under = above[...].astype(F32), below[...].astype(F32)
    for b in range(nb):
        at = b * height
        tall[at : at + HALO, :] = over[0:HALO, b * values : (b + 1) * values]
        tall[at + HALO : at + HALO + na, 0:LANES] = row_part[b * na : (b + 1) * na, :]
        tall[at + HALO : at + HALO + na, LANES : 2 * LANES] = col_part[b * na : (b + 1) * na, :]
        tall[at + HALO + na : at + height, :] = under[0:HALO, b * values : (b + 1) * values]
    both[...] = tall[...].astype(BF16)
    packed[...] = jnp.zeros(packed.shape, F32)
    for target, first, j in ((left, 0, 0), (right, nb - HALO, ky - 1)):
        for b in range(HALO):
            for g in range(height // 8):
                lanes = slice((b * (height // 8) + g) * values, (b * (height // 8) + g + 1) * values)
                at = (first + b) * height + 8 * g
                packed[0:8, lanes] = tall[at : at + 8, :]
        packed[8:9, :] = over[HALO + j : HALO + j + 1, :]
        for i in range(kx):
            packed[9 + i : 10 + i, :] = coarse[i * ky + j : i * ky + j + 1, :]
        packed[9 + kx : 10 + kx, :] = under[HALO + j : HALO + j + 1, :]
        target[...] = packed[...].astype(BF16)


def trunk_kernel(blocks, trunk_hbm, w_sensor, trunk, mean_trunk, w_out, arrived):
    steps = arrived.shape[0]
    depth = trunk.shape[0] // steps
    copies = [
        pltpu.make_async_copy(trunk_hbm.at[pl.ds(i * depth, depth)], trunk.at[pl.ds(i * depth, depth)], arrived.at[i])
        for i in range(steps)
    ]
    for copy in copies:
        copy.start()
    at = 0
    for start, size in blocks:
        w_out[at : at + size, :] = w_sensor[start : start + size, :]
        at += size
    share = jnp.full((trunk.shape[1], LANES), 1.0 / (TILE * TILE), BF16)
    for i, copy in enumerate(copies):
        copy.wait()
        rows = slice(i * depth, (i + 1) * depth)
        mean_trunk[rows, :] = dot(trunk[rows, :], share)


def sensor_trunk_kernel(trunk, spread, sensor_trunk):
    width = 1024
    per = width // TILE
    point = lax.broadcasted_iota(jnp.int32, (width, LANES), 0)
    lane = lax.broadcasted_iota(jnp.int32, (width, LANES), 1)
    column = (point & (TILE - 1)) == TILE // 2 - 1 + (lane >> 6)
    away = jnp.where(column, (lane & (TILE - 1)) - (point >> 6), -1)
    total = None
    for step in range(trunk.shape[1] // width):
        pick = jnp.where(away == step * per, 1.0, 0.0).astype(BF16)
        part = dot(trunk[:, step * width : (step + 1) * width], pick)
        total = part if total is None else total + part
    middle = trunk.shape[1] // 2
    row31 = pltpu.roll(trunk[:, middle - LANES : middle].astype(F32), TILE, 1)
    row32 = pltpu.roll(trunk[:, middle : middle + LANES].astype(F32), TILE, 1)
    rows = jnp.where(low_lanes(row31.shape), row31, row32)
    unique = jnp.concatenate([rows, total], axis=1).astype(BF16)
    sensor_trunk[...] = dot(unique, spread[...]).astype(BF16)


def sensor_vectors(sensors, base, count):
    height = HALO * 2 + 16
    low = low_lanes((count, LANES))

    def part(shift, group):
        return sensors[base + shift : base + shift + count, group * LANES : (group + 1) * LANES]

    parts = [
        jnp.where(low, part(-1, 0), part(1, 0)),
        jnp.where(low, part(-height - 1, 1), part(-height + 1, 1)),
        jnp.where(low, part(height - 1, 2), part(height + 1, 2)),
        jnp.where(low, part(-height, 3), part(height, 3)),
    ]
    return jnp.concatenate([p.astype(BF16) for p in parts], axis=1)


def branch(vectors, w1, b1, w2, b2, w3, b3):
    hidden = jnp.tanh(dot(vectors, w1[...]) + b1[...]).astype(BF16)
    hidden = jnp.tanh(dot(hidden, w2[...]) + b2[...]).astype(BF16)
    return (dot(hidden, w3[...]) + b3[...]).astype(BF16)


def send_means(coeffs, pool, mean_trunk, col, cells, payload):
    pooled = dot(pool[...], coeffs)
    means = dot(pooled, mean_trunk[...], precision=lax.Precision.HIGHEST)
    lane = lax.broadcasted_iota(jnp.int32, means.shape, 1)
    cell = lax.broadcasted_iota(jnp.int32, means.shape, 0)
    mine = ((lane - cells * col) & (LANES - 1)) == cell
    line = jnp.sum(jnp.where(mine, means, 0.0), axis=0, keepdims=True)
    payload[...] = jnp.broadcast_to(line, payload.shape)


def corrections(gathered, coarse, n_row, n_col, cells):
    blocks = n_col * cells // LANES
    lane = lax.broadcasted_iota(jnp.int32, (n_col, LANES), 1)
    source = cells * lax.broadcasted_iota(jnp.int32, (n_col, LANES), 0)
    block = (source + ((lane - source) & (LANES - 1))) // LANES
    total = None
    for r in range(n_row):
        values = gathered[r * n_col : (r + 1) * n_col, :]
        for k in range(blocks):
            line = jnp.sum(jnp.where(block == k, values, 0.0), axis=0, keepdims=True)
            at = (r * blocks + k) * LANES
            term = coarse[:, at : at + LANES] * line
            total = term if total is None else total + term
    return jnp.sum(total, axis=1, keepdims=True)


def own_vectors(na, nb, sensors, base):
    height = na + 2 * HALO
    return jnp.concatenate(
        [sensor_vectors(sensors, base + b * height + HALO, na) for b in range(nb)], axis=0
    )


def zero_ends(sensors):
    rows = sensors.shape[0]
    sensors[0:8, :] = jnp.zeros((8, sensors.shape[1]), F32)
    sensors[rows - 8 : rows, :] = jnp.zeros((8, sensors.shape[1]), F32)


def first_kernel(
    na, nb, cells, mid, left, right, above, below, c_own, spread, w1, b1, w2, b2, w3, b3, pool, mean_trunk,
    coeffs, payload, coarse, sensors, tiles,
):
    height, values = na + 2 * HALO, 4 * TILE
    side = HALO * height
    wide = nb * height
    tiles[side : side + wide, :] = mid[...].astype(F32)
    edge = [x[...].astype(F32) for x in (above, below, left, right)]
    for lines, first in ((edge[2], 0), (edge[3], side + wide)):
        for g in range(side // 8):
            tiles[first + 8 * g : first + 8 * (g + 1), :] = lines[0:8, g * values : (g + 1) * values]
    zero_ends(sensors)
    sensors[8 : 8 + 2 * side + wide, :] = dot(tiles[...].astype(BF16), spread[...])
    vectors = sensor_vectors(sensors, 8 + height, coeffs.shape[0])
    result = branch(vectors, w1, b1, w2, b2, w3, b3)
    coeffs[...] = result
    send_means(result, pool, mean_trunk, lax.axis_index("col"), cells, payload)
    kx, ky = na // PER_CELL, nb // PER_CELL
    coarse[0 : kx + 2, :] = edge[2][8 : 10 + kx, :]
    coarse[8 * (ky + 1) : 8 * (ky + 1) + kx + 2, :] = edge[3][8 : 10 + kx, :]
    for j in range(ky):
        at = 8 * (j + 1)
        coarse[at : at + 1, :] = edge[0][HALO + j : HALO + j + 1, :]
        for i in range(kx):
            coarse[at + 1 + i : at + 2 + i, :] = c_own[i * ky + j : i * ky + j + 1, :]
        coarse[at + 1 + kx : at + 2 + kx, :] = edge[1][HALO + j : HALO + j + 1, :]
    for j in range(ky + 2):
        at = 8 * j + kx + 2
        coarse[at : 8 * (j + 1), :] = jnp.zeros((6 - kx, coarse.shape[1]), F32)


def next_kernel(
    k, na, nb, n_row, n_col, cells, gathered, before, sensor_trunk, coarse, w1, b1, w2, b2, w3, b3,
    pool, mean_trunk, coeffs, payload, sensors, lines,
):
    height = na + 2 * HALO
    predicted = dot(before[...], sensor_trunk[...])
    found = corrections(gathered, coarse, n_row, n_col, cells)
    found = jnp.broadcast_to(found, (found.shape[0], sensors.shape[1]))
    row, col = lax.axis_index("row"), lax.axis_index("col")
    a_at = row * na - HALO + lax.broadcasted_iota(jnp.int32, (height, 1), 0)
    a_ok = (a_at >= 0) & (a_at < n_row * na)
    for j in range(nb // PER_CELL + 2):
        for i in range(height // PER_CELL):
            at = j * height + i * PER_CELL
            lines[at : at + PER_CELL, :] = jnp.broadcast_to(
                found[8 * j + i : 8 * j + i + 1, :], (PER_CELL, found.shape[1])
            )
    zero_ends(sensors)
    first = k - 1
    have = nb + 2 * HALO - 2 * first
    for i in range(have):
        b = first + i
        b_at = col * nb - HALO + b
        inside = jnp.where(a_ok & (b_at >= 0) & (b_at < n_col * nb), 1.0, 0.0)
        cell = b // PER_CELL
        value = predicted[i * height : (i + 1) * height, :] + lines[cell * height : (cell + 1) * height, :]
        sensors[8 + i * height : 8 + (i + 1) * height, :] = jnp.where(inside > 0.5, value, 0.0)
    if k < ITERS:
        vectors = sensor_vectors(sensors, 8 + height, coeffs.shape[0])
    else:
        vectors = own_vectors(na, nb, sensors, 8 + height)
    result = branch(vectors, w1, b1, w2, b2, w3, b3)
    coeffs[...] = result
    send_means(result, pool, mean_trunk, col, cells, payload)


def field_kernel(na, nb, n_row, n_col, cells, gathered, coarse, coeffs, trunk, out, correction, strip, ready, sent):
    steps = ready.shape[0]
    width = trunk.shape[1] // steps
    per = width // TILE
    ky = nb // PER_CELL
    found = corrections(gathered, coarse, n_row, n_col, cells)
    correction[...] = jnp.broadcast_to(found, correction.shape)
    upper = lax.broadcasted_iota(jnp.int32, (8, LANES), 0) < PER_CELL
    adds = {}
    for a in range(0, na, 8):
        for j in range(ky):
            at = a // PER_CELL * ky + j
            adds[a, j] = jnp.where(upper, correction[at : at + 1, :], correction[at + ky : at + ky + 1, :])
    low = low_lanes((8, LANES))
    copies = []
    for step in range(steps):
        values = dot(coeffs[...], trunk[:, step * width : (step + 1) * width])
        for pair in range(nb // 2):
            for a in range(0, na, 8):
                add = adds[a, 2 * pair // PER_CELL]
                even, odd = (2 * pair * na + a, (2 * pair + 1) * na + a)
                for r in range(0, per, 2):
                    lanes = slice(r * TILE, r * TILE + LANES)
                    x, y = values[even : even + 8, lanes], values[odd : odd + 8, lanes]
                    at = (pair * na + a) * per + r
                    strip[pl.ds(at, 8, stride=per), :] = jnp.where(low, x, pltpu.roll(y, TILE, 1)) + add
                    strip[pl.ds(at + 1, 8, stride=per), :] = jnp.where(low, pltpu.roll(x, TILE, 1), y) + add
            done = strip[pair * na * per : (pair + 1) * na * per, :].reshape(na, per, LANES)
            ready[step, :, :, pair * LANES : (pair + 1) * LANES] = done
        copies.append(
            pltpu.make_async_copy(ready.at[step], out.at[:, pl.ds(step * per, per), :], sent.at[step])
        )
        copies[-1].start()
    for copy in copies:
        copy.wait()


def pool_matrix(na, nb, first, trimmed):
    kx, ky = na // PER_CELL, nb // PER_CELL
    height = na if trimmed else na + 2 * HALO
    skip_a = 0 if trimmed else HALO
    skip_b = HALO - first
    wide = nb + 2 * skip_b
    pool = np.zeros((16, wide * height), np.float32)
    for a in range(na):
        for b in range(nb):
            cell = (a // PER_CELL) * ky + b // PER_CELL
            pool[cell, (b + skip_b) * height + a + skip_a] = 1.0 / PER_CELL**2
    return jnp.asarray(pool, BF16)


def body(
    field_start,
    w_sensor,
    bias_sensor,
    w_middle,
    bias_middle,
    w_latent,
    bias_latent,
    trunk_basis,
    coarse_matrix,
):
    rows_here, cols_here = field_start.shape
    n_row, n_col = lax.axis_size("row"), lax.axis_size("col")
    na, nb = rows_here // TILE, cols_here // TILE
    height = na + 2 * HALO
    kx, ky = na // PER_CELL, nb // PER_CELL
    cells = kx * ky
    devices = n_row * n_col
    latent = trunk_basis.shape[0]
    hid = w_sensor.shape[1]
    tile_values, places = 4 * TILE, 8 * TILE
    total = coarse_matrix.shape[1]
    whole = pl.BlockSpec(memory_space=pltpu.VMEM)
    shape = jax.ShapeDtypeStruct
    part = functools.partial

    def shift(x, axis, forward):
        count = lax.axis_size(axis)
        pairs = [(i, i + 1) if forward else (i + 1, i) for i in range(count - 1)]
        return lax.ppermute(x, axis, pairs)

    def exchange(x):
        return lax.all_to_all(x, ("row", "col"), 0, 0, tiled=True)

    spread_np, order = sensor_layout()
    spread = jnp.asarray(spread_np, BF16)
    half = TILE // 2
    blocks = tuple((int(at), half) for at in order[::half])
    hbm = pl.BlockSpec(memory_space=pltpu.HBM)

    row_part, col_part = call(
        part(extract_kernel, na, nb),
        (shape((nb * na, LANES), F32), shape((nb * na, LANES), F32)),
        field_start.reshape(na, TILE, cols_here),
    )
    up, down = call(
        part(pack_kernel, na, nb, ky),
        (shape((8, total), BF16), shape((8, total), BF16)),
        row_part,
        col_part,
        coarse_matrix,
        scratch=[pltpu.VMEM((8, total), F32)],
    )
    above, below = shift(down, "row", True), shift(up, "row", False)
    trunk, mean_trunk, w_first = call(
        part(trunk_kernel, blocks),
        (shape(trunk_basis.shape, BF16), shape((latent, LANES), F32), shape(w_sensor.shape, BF16)),
        trunk_basis,
        w_sensor,
        in_specs=[hbm, whole],
        scratch=[pltpu.SemaphoreType.DMA((4,))],
        flops=1 << 32,
    )
    above, below, w_first = lax.optimization_barrier((above, below, w_first))
    mid, to_left, to_right = call(
        part(columns_kernel, na, nb),
        (shape((nb * height, tile_values), BF16), shape((16, total), BF16), shape((16, total), BF16)),
        row_part,
        col_part,
        above,
        below,
        coarse_matrix,
        scratch=[pltpu.VMEM((nb * height, tile_values), F32), pltpu.VMEM((16, total), F32)],
    )
    to_left, to_right, mean_trunk = lax.optimization_barrier((to_left, to_right, mean_trunk))
    left, right = shift(to_right, "col", True), shift(to_left, "col", False)

    net = (
        w_first,
        bias_sensor.reshape(1, hid),
        w_middle,
        bias_middle.reshape(1, hid),
        w_latent,
        bias_latent.reshape(1, latent),
    )

    sensor_trunk = call(
        sensor_trunk_kernel, shape((latent, places), BF16), trunk, spread, flops=1 << 30
    )
    left, right, sensor_trunk = lax.optimization_barrier((left, right, sensor_trunk))

    def region(k):
        return (nb + 2 * HALO - 2 * k) * height

    payload_shape = shape((devices, LANES), F32)
    coeffs, payload, coarse = call(
        part(first_kernel, na, nb, cells),
        (shape((region(1), latent), BF16), payload_shape, shape((8 * (ky + 2), total), F32)),
        mid,
        left,
        right,
        above,
        below,
        coarse_matrix,
        spread,
        *net,
        pool_matrix(na, nb, 1, False),
        mean_trunk,
        scratch=[pltpu.VMEM((region(0) + 16, places), F32), pltpu.VMEM((region(0), tile_values), F32)],
    )
    for k in range(2, ITERS + 1):
        gathered = exchange(payload)
        coeffs, payload = call(
            part(next_kernel, k, na, nb, n_row, n_col, cells),
            (shape((region(k) if k < ITERS else nb * na, latent), BF16), payload_shape),
            gathered,
            coeffs,
            sensor_trunk,
            coarse,
            *net,
            pool_matrix(na, nb, k, k == ITERS),
            mean_trunk,
            scratch=[
                pltpu.VMEM((region(k - 1) + 16, places), F32),
                pltpu.VMEM(((ky + 2) * height, places), F32),
            ],
        )
    gathered = exchange(payload)
    steps = 8
    out = call(
        part(field_kernel, na, nb, n_row, n_col, cells),
        shape((na, TILE, cols_here), F32),
        gathered,
        coarse_matrix,
        coeffs,
        trunk,
        out_specs=hbm,
        scratch=[
            pltpu.VMEM((cells, LANES), F32),
            pltpu.VMEM((rows_here * cols_here // steps // LANES, LANES), F32),
            pltpu.VMEM((steps, na, TILE // steps, cols_here), F32),
            pltpu.SemaphoreType.DMA((steps,)),
        ],
    )
    return out.reshape(rows_here, cols_here)


def solution(mesh):
    placed = (P("row", "col"), P(), P(), P(), P(), P(), P(), P(), P(("row", "col"), None))
    return jax.shard_map(
        body, mesh=mesh, in_specs=placed, out_specs=P("row", "col"), check_vma=False
    )
```

```python
import functools

import jax
import jax.numpy as jnp
import numpy as np
from jax import lax
from jax.experimental import pallas as pl
from jax.experimental.pallas import tpu as pltpu
from jax.sharding import PartitionSpec as P

TILE = 64
ITERS = 4
CELL = 256
PER_CELL = CELL // TILE
HALO = ITERS
LANES = 128
F32 = jnp.float32
BF16 = jnp.bfloat16
VMEM_LIMIT = 48 * 1024 * 1024


def dot(a, b, **kw):
    return jnp.dot(a, b, preferred_element_type=F32, **kw)


def nt_dot(a, b):
    return lax.dot_general(a, b, (((1,), (1,)), ((), ())), preferred_element_type=F32)


def low_lanes(shape):
    return lax.broadcasted_iota(jnp.int32, shape, 1) < TILE


def call(kernel, out_shape, *args, grid=(), in_specs=None, out_specs=None, scratch=(), flops=1 << 31, vmem=VMEM_LIMIT):
    whole = pl.BlockSpec(memory_space=pltpu.VMEM)
    specs = {}
    if grid:
        specs["grid"] = grid
    return pl.pallas_call(
        kernel,
        out_shape=out_shape,
        in_specs=in_specs or [whole] * len(args),
        out_specs=out_specs or jax.tree.map(lambda _: whole, out_shape),
        scratch_shapes=list(scratch),
        compiler_params=pltpu.CompilerParams(vmem_limit_bytes=vmem),
        cost_estimate=pl.CostEstimate(flops=flops, bytes_accessed=1 << 20, transcendentals=0),
        **specs,
    )(*args)


def sensor_layout():
    half = TILE // 2
    row31, row32, col31, col32 = (np.arange(TILE) + TILE * i for i in range(4))
    top, bottom, left, right = (np.arange(2 * TILE) + 2 * TILE * i for i in range(4))
    mid = slice(half, half + TILE)
    groups = [
        (row32, top[mid]),
        (row31, bottom[mid]),
        (np.r_[row32[half:], col32[half:]], np.r_[top[:half], left[:half]]),
        (np.r_[row31[half:], col32[:half]], np.r_[bottom[:half], left[-half:]]),
        (np.r_[row32[:half], col31[half:]], np.r_[top[-half:], right[:half]]),
        (np.r_[row31[:half], col31[:half]], np.r_[bottom[-half:], right[-half:]]),
        (col32, left[mid]),
        (col31, right[mid]),
    ]
    source = np.concatenate([g[0] for g in groups])
    order = np.concatenate([g[1] for g in groups])
    spread = np.zeros((4 * TILE, 8 * TILE), np.float32)
    spread[source, np.arange(8 * TILE)] = 1.0
    return spread, order


def extract_kernel(na, nb, cells, row_part, col_part):
    cols = cells.shape[2]
    here = 8
    sel_row = lax.broadcasted_iota(jnp.int32, (2 * 16, cols), 0)
    sel_col = lax.broadcasted_iota(jnp.int32, (2 * 16, cols), 1)
    side, b_of = sel_row // 16, sel_row % 16
    pick = jnp.where(sel_col == b_of * TILE + (TILE // 2 - 1) + side, 1.0, 0.0).astype(BF16)
    low_row, low_col = low_lanes((here, LANES)), low_lanes((16, LANES))
    for base in range(0, na, here):
        chunk = cells[base : base + here]
        picked = nt_dot(pick, chunk.reshape(here * TILE, cols).astype(BF16))
        r31 = cells[base : base + here, TILE // 2 - 1, :]
        r32 = cells[base : base + here, TILE // 2, :]
        for pair in range(nb // 2):
            lanes = slice(pair * LANES, (pair + 1) * LANES)
            x, y = r31[:, lanes], r32[:, lanes]
            even, odd = 2 * pair * na + base, (2 * pair + 1) * na + base
            row_part[even : even + here, :] = jnp.where(low_row, x, pltpu.roll(y, TILE, 1))
            row_part[odd : odd + here, :] = jnp.where(low_row, pltpu.roll(x, TILE, 1), y)
        for pair in range(here // 2):
            lanes = slice(pair * LANES, (pair + 1) * LANES)
            x, y = picked[0:16, lanes], picked[16:32, lanes]
            even = jnp.where(low_col, x, pltpu.roll(y, TILE, 1))
            odd = jnp.where(low_col, pltpu.roll(x, TILE, 1), y)
            col_part[pl.ds(base + 2 * pair, nb, stride=na), :] = even[0:nb]
            col_part[pl.ds(base + 2 * pair + 1, nb, stride=na), :] = odd[0:nb]


def pack_kernel(na, nb, ky, row_part, col_part, coarse, up, down, packed):
    packed[...] = jnp.zeros(packed.shape, F32)
    for target, first, line in ((up, 0, 0), (down, na - HALO, coarse.shape[0] - ky)):
        for b in range(nb):
            rows = slice(b * na + first, b * na + first + HALO)
            packed[0:HALO, 2 * b * LANES : (2 * b + 1) * LANES] = row_part[rows, :]
            packed[0:HALO, (2 * b + 1) * LANES : (2 * b + 2) * LANES] = col_part[rows, :]
        packed[HALO : HALO + ky, :] = coarse[line : line + ky, :]
        target[...] = packed[...].astype(BF16)


def columns_kernel(na, nb, row_part, col_part, above, below, both, left, right, tall, packed):
    height, values = na + 2 * HALO, 4 * TILE
    over, under = above[...].astype(F32), below[...].astype(F32)
    for b in range(nb):
        at = b * height
        tall[at : at + HALO, :] = over[0:HALO, b * values : (b + 1) * values]
        tall[at + HALO : at + HALO + na, 0:LANES] = row_part[b * na : (b + 1) * na, :]
        tall[at + HALO : at + HALO + na, LANES : 2 * LANES] = col_part[b * na : (b + 1) * na, :]
        tall[at + HALO + na : at + height, :] = under[0:HALO, b * values : (b + 1) * values]
    both[...] = tall[...].astype(BF16)
    for target, first in ((left, 0), (right, nb - HALO)):
        for b in range(HALO):
            for g in range(height // 8):
                lanes = slice((b * (height // 8) + g) * values, (b * (height // 8) + g + 1) * values)
                at = (first + b) * height + 8 * g
                packed[:, lanes] = tall[at : at + 8, :]
        target[...] = packed[...].astype(BF16)


def trunk_kernel(blocks, trunk_hbm, w_sensor, trunk, mean_trunk, w_out, arrived):
    steps = arrived.shape[0]
    depth = trunk.shape[0] // steps
    copies = [
        pltpu.make_async_copy(trunk_hbm.at[pl.ds(i * depth, depth)], trunk.at[pl.ds(i * depth, depth)], arrived.at[i])
        for i in range(steps)
    ]
    for copy in copies:
        copy.start()
    at = 0
    for start, size in blocks:
        w_out[at : at + size, :] = w_sensor[start : start + size, :]
        at += size
    share = jnp.full((trunk.shape[1], LANES), 1.0 / (TILE * TILE), BF16)
    for i, copy in enumerate(copies):
        copy.wait()
        rows = slice(i * depth, (i + 1) * depth)
        mean_trunk[rows, :] = dot(trunk[rows, :], share)


def sensor_trunk_kernel(kx, ky, trunk, spread, above, below, coarse, sensor_trunk, left, right, packed):
    over, under = above[...].astype(F32), below[...].astype(F32)
    packed[...] = jnp.zeros(packed.shape, F32)
    for target, j in ((left, 0), (right, ky - 1)):
        packed[0:1, :] = over[HALO + j : HALO + j + 1, :]
        for i in range(kx):
            packed[1 + i : 2 + i, :] = coarse[i * ky + j : i * ky + j + 1, :]
        packed[1 + kx : 2 + kx, :] = under[HALO + j : HALO + j + 1, :]
        target[...] = packed[...].astype(BF16)
    width = 1024
    per = width // TILE
    point = lax.broadcasted_iota(jnp.int32, (width, LANES), 0)
    lane = lax.broadcasted_iota(jnp.int32, (width, LANES), 1)
    column = (point & (TILE - 1)) == TILE // 2 - 1 + (lane >> 6)
    away = jnp.where(column, (lane & (TILE - 1)) - (point >> 6), -1)
    total = None
    for step in range(trunk.shape[1] // width):
        pick = jnp.where(away == step * per, 1.0, 0.0).astype(BF16)
        part = dot(trunk[:, step * width : (step + 1) * width], pick)
        total = part if total is None else total + part
    middle = trunk.shape[1] // 2
    row31 = pltpu.roll(trunk[:, middle - LANES : middle].astype(F32), TILE, 1)
    row32 = pltpu.roll(trunk[:, middle : middle + LANES].astype(F32), TILE, 1)
    rows = jnp.where(low_lanes(row31.shape), row31, row32)
    unique = jnp.concatenate([rows, total], axis=1).astype(BF16)
    sensor_trunk[...] = dot(unique, spread[...]).astype(BF16)


def sensor_vectors(sensors, base, count):
    height = HALO * 2 + 16
    low = low_lanes((count, LANES))

    def part(shift, group):
        return sensors[base + shift : base + shift + count, group * LANES : (group + 1) * LANES]

    parts = [
        jnp.where(low, part(-1, 0), part(1, 0)),
        jnp.where(low, part(-height - 1, 1), part(-height + 1, 1)),
        jnp.where(low, part(height - 1, 2), part(height + 1, 2)),
        jnp.where(low, part(-height, 3), part(height, 3)),
    ]
    return jnp.concatenate([p.astype(BF16) for p in parts], axis=1)


def branch(vectors, w1, b1, w2, b2, w3, b3):
    hidden = jnp.tanh(dot(vectors, w1[...]) + b1[...]).astype(BF16)
    hidden = jnp.tanh(dot(hidden, w2[...]) + b2[...]).astype(BF16)
    return (dot(hidden, w3[...]) + b3[...]).astype(BF16)


def send_means(coeffs, pool, mean_trunk, col, cells, payload):
    pooled = dot(pool[...], coeffs)
    means = dot(pooled, mean_trunk[...], precision=lax.Precision.HIGHEST)
    lane = lax.broadcasted_iota(jnp.int32, means.shape, 1)
    cell = lax.broadcasted_iota(jnp.int32, means.shape, 0)
    mine = ((lane - cells * col) & (LANES - 1)) == cell
    line = jnp.sum(jnp.where(mine, means, 0.0), axis=0, keepdims=True)
    payload[...] = jnp.broadcast_to(line, payload.shape)


def corrections(gathered, coarse, n_row, n_col, cells):
    blocks = n_col * cells // LANES
    lane = lax.broadcasted_iota(jnp.int32, (n_col, LANES), 1)
    source = cells * lax.broadcasted_iota(jnp.int32, (n_col, LANES), 0)
    block = (source + ((lane - source) & (LANES - 1))) // LANES
    total = None
    for r in range(n_row):
        values = gathered[r * n_col : (r + 1) * n_col, :]
        for k in range(blocks):
            line = jnp.sum(jnp.where(block == k, values, 0.0), axis=0, keepdims=True)
            at = (r * blocks + k) * LANES
            term = coarse[:, at : at + LANES] * line
            total = term if total is None else total + term
    return jnp.sum(total, axis=1, keepdims=True)


def own_vectors(na, nb, sensors, base):
    height = na + 2 * HALO
    return jnp.concatenate(
        [sensor_vectors(sensors, base + b * height + HALO, na) for b in range(nb)], axis=0
    )


def zero_ends(sensors):
    rows = sensors.shape[0]
    sensors[0:8, :] = jnp.zeros((8, sensors.shape[1]), F32)
    sensors[rows - 8 : rows, :] = jnp.zeros((8, sensors.shape[1]), F32)


def first_kernel(
    na, nb, cells, mid, left, right, spread, w1, b1, w2, b2, w3, b3, pool, mean_trunk,
    coeffs, payload, sensors, tiles,
):
    height, values = na + 2 * HALO, 4 * TILE
    side = HALO * height
    wide = nb * height
    tiles[side : side + wide, :] = mid[...].astype(F32)
    for source, first in ((left, 0), (right, side + wide)):
        lines = source[...].astype(F32)
        for g in range(side // 8):
            tiles[first + 8 * g : first + 8 * (g + 1), :] = lines[:, g * values : (g + 1) * values]
    zero_ends(sensors)
    sensors[8 : 8 + 2 * side + wide, :] = dot(tiles[...].astype(BF16), spread[...])
    vectors = sensor_vectors(sensors, 8 + height, coeffs.shape[0])
    result = branch(vectors, w1, b1, w2, b2, w3, b3)
    coeffs[...] = result
    send_means(result, pool, mean_trunk, lax.axis_index("col"), cells, payload)


def gather_coarse(kx, ky, c_own, above, below, left, right, coarse):
    edge = [x[...].astype(F32) for x in (above, below, left, right)]
    coarse[0:8, :] = edge[2]
    coarse[8 * (ky + 1) : 8 * (ky + 2), :] = edge[3]
    for j in range(ky):
        at = 8 * (j + 1)
        coarse[at : at + 1, :] = edge[0][HALO + j : HALO + j + 1, :]
        for i in range(kx):
            coarse[at + 1 + i : at + 2 + i, :] = c_own[i * ky + j : i * ky + j + 1, :]
        coarse[at + 1 + kx : at + 2 + kx, :] = edge[1][HALO + j : HALO + j + 1, :]
        coarse[at + kx + 2 : at + 8, :] = jnp.zeros((6 - kx, coarse.shape[1]), F32)


def second_kernel(
    na, nb, n_row, n_col, cells, c_own, above, below, left, right, gathered, before, sensor_trunk, *rest
):
    *net, coeffs, payload, coarse, sensors, lines = rest
    gather_coarse(na // PER_CELL, nb // PER_CELL, c_own, above, below, left, right, coarse)
    next_kernel(
        2, na, nb, n_row, n_col, cells, gathered, before, sensor_trunk, coarse, *net, coeffs, payload, sensors, lines
    )


def next_kernel(
    k, na, nb, n_row, n_col, cells, gathered, before, sensor_trunk, coarse, w1, b1, w2, b2, w3, b3,
    pool, mean_trunk, coeffs, payload, sensors, lines,
):
    height = na + 2 * HALO
    predicted = dot(before[...], sensor_trunk[...])
    found = corrections(gathered, coarse, n_row, n_col, cells)
    found = jnp.broadcast_to(found, (found.shape[0], sensors.shape[1]))
    row, col = lax.axis_index("row"), lax.axis_index("col")
    a_at = row * na - HALO + lax.broadcasted_iota(jnp.int32, (height, 1), 0)
    a_ok = (a_at >= 0) & (a_at < n_row * na)
    for j in range(nb // PER_CELL + 2):
        for i in range(height // PER_CELL):
            at = j * height + i * PER_CELL
            lines[at : at + PER_CELL, :] = jnp.broadcast_to(
                found[8 * j + i : 8 * j + i + 1, :], (PER_CELL, found.shape[1])
            )
    zero_ends(sensors)
    first = k - 1
    have = nb + 2 * HALO - 2 * first
    for i in range(have):
        b = first + i
        b_at = col * nb - HALO + b
        inside = jnp.where(a_ok & (b_at >= 0) & (b_at < n_col * nb), 1.0, 0.0)
        cell = b // PER_CELL
        value = predicted[i * height : (i + 1) * height, :] + lines[cell * height : (cell + 1) * height, :]
        sensors[8 + i * height : 8 + (i + 1) * height, :] = jnp.where(inside > 0.5, value, 0.0)
    if k < ITERS:
        vectors = sensor_vectors(sensors, 8 + height, coeffs.shape[0])
    else:
        vectors = own_vectors(na, nb, sensors, 8 + height)
    result = branch(vectors, w1, b1, w2, b2, w3, b3)
    coeffs[...] = result
    send_means(result, pool, mean_trunk, col, cells, payload)


def field_kernel(na, nb, n_row, n_col, cells, gathered, coarse, coeffs, trunk, out, correction, strip, ready, sent):
    steps = ready.shape[0]
    width = trunk.shape[1] // steps
    per = width // TILE
    ky = nb // PER_CELL
    found = corrections(gathered, coarse, n_row, n_col, cells)
    correction[...] = jnp.broadcast_to(found, correction.shape)
    upper = lax.broadcasted_iota(jnp.int32, (8, LANES), 0) < PER_CELL
    adds = {}
    for a in range(0, na, 8):
        for j in range(ky):
            at = a // PER_CELL * ky + j
            adds[a, j] = jnp.where(upper, correction[at : at + 1, :], correction[at + ky : at + ky + 1, :])
    low = low_lanes((8, LANES))
    copies = []
    for step in range(steps):
        values = dot(coeffs[...], trunk[:, step * width : (step + 1) * width])
        for pair in range(nb // 2):
            for a in range(0, na, 8):
                add = adds[a, 2 * pair // PER_CELL]
                even, odd = (2 * pair * na + a, (2 * pair + 1) * na + a)
                for r in range(0, per, 2):
                    lanes = slice(r * TILE, r * TILE + LANES)
                    x, y = values[even : even + 8, lanes], values[odd : odd + 8, lanes]
                    at = (pair * na + a) * per + r
                    strip[pl.ds(at, 8, stride=per), :] = jnp.where(low, x, pltpu.roll(y, TILE, 1)) + add
                    strip[pl.ds(at + 1, 8, stride=per), :] = jnp.where(low, pltpu.roll(x, TILE, 1), y) + add
            done = strip[pair * na * per : (pair + 1) * na * per, :].reshape(na, per, LANES)
            ready[step, :, :, pair * LANES : (pair + 1) * LANES] = done
        copies.append(
            pltpu.make_async_copy(ready.at[step], out.at[:, pl.ds(step * per, per), :], sent.at[step])
        )
        copies[-1].start()
    for copy in copies:
        copy.wait()


def pool_matrix(na, nb, first, trimmed):
    kx, ky = na // PER_CELL, nb // PER_CELL
    height = na if trimmed else na + 2 * HALO
    skip_a = 0 if trimmed else HALO
    skip_b = HALO - first
    wide = nb + 2 * skip_b
    pool = np.zeros((16, wide * height), np.float32)
    for a in range(na):
        for b in range(nb):
            cell = (a // PER_CELL) * ky + b // PER_CELL
            pool[cell, (b + skip_b) * height + a + skip_a] = 1.0 / PER_CELL**2
    return jnp.asarray(pool, BF16)


def body(
    field_start,
    w_sensor,
    bias_sensor,
    w_middle,
    bias_middle,
    w_latent,
    bias_latent,
    trunk_basis,
    coarse_matrix,
):
    rows_here, cols_here = field_start.shape
    n_row, n_col = lax.axis_size("row"), lax.axis_size("col")
    na, nb = rows_here // TILE, cols_here // TILE
    height = na + 2 * HALO
    kx, ky = na // PER_CELL, nb // PER_CELL
    cells = kx * ky
    devices = n_row * n_col
    latent = trunk_basis.shape[0]
    hid = w_sensor.shape[1]
    tile_values, places = 4 * TILE, 8 * TILE
    total = coarse_matrix.shape[1]
    whole = pl.BlockSpec(memory_space=pltpu.VMEM)
    shape = jax.ShapeDtypeStruct
    part = functools.partial

    def shift(x, axis, forward):
        count = lax.axis_size(axis)
        pairs = [(i, i + 1) if forward else (i + 1, i) for i in range(count - 1)]
        return lax.ppermute(x, axis, pairs)

    def exchange(x):
        return lax.all_to_all(x, ("row", "col"), 0, 0, tiled=True)

    spread_np, order = sensor_layout()
    spread = jnp.asarray(spread_np, BF16)
    half = TILE // 2
    blocks = tuple((int(at), half) for at in order[::half])
    hbm = pl.BlockSpec(memory_space=pltpu.HBM)

    row_part, col_part = call(
        part(extract_kernel, na, nb),
        (shape((nb * na, LANES), F32), shape((nb * na, LANES), F32)),
        field_start.reshape(na, TILE, cols_here),
    )
    up, down = call(
        part(pack_kernel, na, nb, ky),
        (shape((8, total), BF16), shape((8, total), BF16)),
        row_part,
        col_part,
        coarse_matrix,
        scratch=[pltpu.VMEM((8, total), F32)],
    )
    above, below = shift(down, "row", True), shift(up, "row", False)
    trunk, mean_trunk, w_first = call(
        part(trunk_kernel, blocks),
        (shape(trunk_basis.shape, BF16), shape((latent, LANES), F32), shape(w_sensor.shape, BF16)),
        trunk_basis,
        w_sensor,
        in_specs=[hbm, whole],
        scratch=[pltpu.SemaphoreType.DMA((4,))],
        flops=1 << 32,
    )
    above, below, w_first = lax.optimization_barrier((above, below, w_first))
    mid, to_left, to_right = call(
        part(columns_kernel, na, nb),
        (shape((nb * height, tile_values), BF16), shape((8, total), BF16), shape((8, total), BF16)),
        row_part,
        col_part,
        above,
        below,
        scratch=[pltpu.VMEM((nb * height, tile_values), F32), pltpu.VMEM((8, total), F32)],
    )
    to_left, to_right, mean_trunk = lax.optimization_barrier((to_left, to_right, mean_trunk))
    left, right = shift(to_right, "col", True), shift(to_left, "col", False)

    net = (
        w_first,
        bias_sensor.reshape(1, hid),
        w_middle,
        bias_middle.reshape(1, hid),
        w_latent,
        bias_latent.reshape(1, latent),
    )

    sensor_trunk, c_to_left, c_to_right = call(
        part(sensor_trunk_kernel, kx, ky),
        (shape((latent, places), BF16), shape((8, total), BF16), shape((8, total), BF16)),
        trunk,
        spread,
        above,
        below,
        coarse_matrix,
        scratch=[pltpu.VMEM((8, total), F32)],
        flops=1 << 30,
    )
    mid, c_to_left, c_to_right = lax.optimization_barrier((mid, c_to_left, c_to_right))
    c_left, c_right = shift(c_to_right, "col", True), shift(c_to_left, "col", False)

    def region(k):
        return (nb + 2 * HALO - 2 * k) * height

    payload_shape = shape((devices, LANES), F32)
    coeffs, payload = call(
        part(first_kernel, na, nb, cells),
        (shape((region(1), latent), BF16), payload_shape),
        mid,
        left,
        right,
        spread,
        *net,
        pool_matrix(na, nb, 1, False),
        mean_trunk,
        scratch=[pltpu.VMEM((region(0) + 16, places), F32), pltpu.VMEM((region(0), tile_values), F32)],
    )
    coarse = None
    for k in range(2, ITERS + 1):
        gathered = exchange(payload)
        rest = (*net, pool_matrix(na, nb, k, k == ITERS), mean_trunk)
        shapes = (shape((region(k) if k < ITERS else nb * na, latent), BF16), payload_shape)
        scratch = [
            pltpu.VMEM((region(k - 1) + 16, places), F32),
            pltpu.VMEM(((ky + 2) * height, places), F32),
        ]
        if k == 2:
            coeffs, payload, coarse = call(
                part(second_kernel, na, nb, n_row, n_col, cells),
                (*shapes, shape((8 * (ky + 2), total), F32)),
                coarse_matrix,
                above,
                below,
                c_left,
                c_right,
                gathered,
                coeffs,
                sensor_trunk,
                *rest,
                scratch=scratch,
            )
        else:
            coeffs, payload = call(
                part(next_kernel, k, na, nb, n_row, n_col, cells),
                shapes,
                gathered,
                coeffs,
                sensor_trunk,
                coarse,
                *rest,
                scratch=scratch,
            )
    gathered = exchange(payload)
    steps = 8
    out = call(
        part(field_kernel, na, nb, n_row, n_col, cells),
        shape((na, TILE, cols_here), F32),
        gathered,
        coarse_matrix,
        coeffs,
        trunk,
        out_specs=hbm,
        scratch=[
            pltpu.VMEM((cells, LANES), F32),
            pltpu.VMEM((rows_here * cols_here // steps // LANES, LANES), F32),
            pltpu.VMEM((steps, na, TILE // steps, cols_here), F32),
            pltpu.SemaphoreType.DMA((steps,)),
        ],
    )
    return out.reshape(rows_here, cols_here)


def solution(mesh):
    placed = (P("row", "col"), P(), P(), P(), P(), P(), P(), P(), P(("row", "col"), None))
    return jax.shard_map(
        body, mesh=mesh, in_specs=placed, out_specs=P("row", "col"), check_vma=False
    )
```

```python
import functools

import jax
import jax.numpy as jnp
import numpy as np
from jax import lax
from jax.experimental import pallas as pl
from jax.experimental.pallas import tpu as pltpu
from jax.sharding import PartitionSpec as P

TILE = 64
ITERS = 4
CELL = 256
PER_CELL = CELL // TILE
HALO = ITERS
LANES = 128
F32 = jnp.float32
BF16 = jnp.bfloat16
VMEM_LIMIT = 48 * 1024 * 1024


def dot(a, b, **kw):
    return jnp.dot(a, b, preferred_element_type=F32, **kw)


def nt_dot(a, b):
    return lax.dot_general(a, b, (((1,), (1,)), ((), ())), preferred_element_type=F32)


def low_lanes(shape):
    return lax.broadcasted_iota(jnp.int32, shape, 1) < TILE


def call(kernel, out_shape, *args, grid=(), in_specs=None, out_specs=None, scratch=(), flops=1 << 31, vmem=VMEM_LIMIT):
    whole = pl.BlockSpec(memory_space=pltpu.VMEM)
    specs = {}
    if grid:
        specs["grid"] = grid
    return pl.pallas_call(
        kernel,
        out_shape=out_shape,
        in_specs=in_specs or [whole] * len(args),
        out_specs=out_specs or jax.tree.map(lambda _: whole, out_shape),
        scratch_shapes=list(scratch),
        compiler_params=pltpu.CompilerParams(vmem_limit_bytes=vmem),
        cost_estimate=pl.CostEstimate(flops=flops, bytes_accessed=1 << 20, transcendentals=0),
        **specs,
    )(*args)


def sensor_layout():
    half = TILE // 2
    row31, row32, col31, col32 = (np.arange(TILE) + TILE * i for i in range(4))
    top, bottom, left, right = (np.arange(2 * TILE) + 2 * TILE * i for i in range(4))
    mid = slice(half, half + TILE)
    groups = [
        (row32, top[mid]),
        (row31, bottom[mid]),
        (np.r_[row32[half:], col32[half:]], np.r_[top[:half], left[:half]]),
        (np.r_[row31[half:], col32[:half]], np.r_[bottom[:half], left[-half:]]),
        (np.r_[row32[:half], col31[half:]], np.r_[top[-half:], right[:half]]),
        (np.r_[row31[:half], col31[:half]], np.r_[bottom[-half:], right[-half:]]),
        (col32, left[mid]),
        (col31, right[mid]),
    ]
    source = np.concatenate([g[0] for g in groups])
    order = np.concatenate([g[1] for g in groups])
    spread = np.zeros((4 * TILE, 8 * TILE), np.float32)
    spread[source, np.arange(8 * TILE)] = 1.0
    return spread, order


def extract_kernel(na, nb, cells, row_part, col_part):
    cols = cells.shape[2]
    here = 8
    sel_row = lax.broadcasted_iota(jnp.int32, (2 * 16, cols), 0)
    sel_col = lax.broadcasted_iota(jnp.int32, (2 * 16, cols), 1)
    side, b_of = sel_row // 16, sel_row % 16
    pick = jnp.where(sel_col == b_of * TILE + (TILE // 2 - 1) + side, 1.0, 0.0).astype(BF16)
    low_row, low_col = low_lanes((here, LANES)), low_lanes((16, LANES))
    for base in range(0, na, here):
        chunk = cells[base : base + here]
        picked = nt_dot(pick, chunk.reshape(here * TILE, cols).astype(BF16))
        r31 = cells[base : base + here, TILE // 2 - 1, :]
        r32 = cells[base : base + here, TILE // 2, :]
        for pair in range(nb // 2):
            lanes = slice(pair * LANES, (pair + 1) * LANES)
            x, y = r31[:, lanes], r32[:, lanes]
            even, odd = 2 * pair * na + base, (2 * pair + 1) * na + base
            row_part[even : even + here, :] = jnp.where(low_row, x, pltpu.roll(y, TILE, 1))
            row_part[odd : odd + here, :] = jnp.where(low_row, pltpu.roll(x, TILE, 1), y)
        for pair in range(here // 2):
            lanes = slice(pair * LANES, (pair + 1) * LANES)
            x, y = picked[0:16, lanes], picked[16:32, lanes]
            even = jnp.where(low_col, x, pltpu.roll(y, TILE, 1))
            odd = jnp.where(low_col, pltpu.roll(x, TILE, 1), y)
            col_part[pl.ds(base + 2 * pair, nb, stride=na), :] = even[0:nb]
            col_part[pl.ds(base + 2 * pair + 1, nb, stride=na), :] = odd[0:nb]


def pack_kernel(na, nb, ky, row_part, col_part, coarse, up, down, packed):
    packed[...] = jnp.zeros(packed.shape, F32)
    for target, first, line in ((up, 0, 0), (down, na - HALO, coarse.shape[0] - ky)):
        for b in range(nb):
            rows = slice(b * na + first, b * na + first + HALO)
            packed[0:HALO, 2 * b * LANES : (2 * b + 1) * LANES] = row_part[rows, :]
            packed[0:HALO, (2 * b + 1) * LANES : (2 * b + 2) * LANES] = col_part[rows, :]
        packed[HALO : HALO + ky, :] = coarse[line : line + ky, :]
        target[...] = packed[...].astype(BF16)


def columns_kernel(na, nb, n_row, row_part, col_part, above, below, coarse, both, first, second, tall, left, right):
    height, values = na + 2 * HALO, 4 * TILE
    kx, ky = na // PER_CELL, nb // PER_CELL
    row, even = lax.axis_index("row"), lax.axis_index("col") % 2 == 0
    over = jnp.where(row == 0, 0.0, above[...].astype(F32))
    under = jnp.where(row == n_row - 1, 0.0, below[...].astype(F32))
    for b in range(nb):
        at = b * height
        tall[at : at + HALO, :] = over[0:HALO, b * values : (b + 1) * values]
        tall[at + HALO : at + HALO + na, 0:LANES] = row_part[b * na : (b + 1) * na, :]
        tall[at + HALO : at + HALO + na, LANES : 2 * LANES] = col_part[b * na : (b + 1) * na, :]
        tall[at + HALO + na : at + height, :] = under[0:HALO, b * values : (b + 1) * values]
    both[...] = tall[...].astype(BF16)
    for packed, start, j in ((left, 0, 0), (right, nb - HALO, ky - 1)):
        packed[...] = jnp.zeros(packed.shape, F32)
        for b in range(HALO):
            for g in range(height // 8):
                lanes = slice((b * (height // 8) + g) * values, (b * (height // 8) + g + 1) * values)
                at = (start + b) * height + 8 * g
                packed[0:8, lanes] = tall[at : at + 8, :]
        packed[8:9, :] = over[HALO + j : HALO + j + 1, :]
        for i in range(kx):
            packed[9 + i : 10 + i, :] = coarse[i * ky + j : i * ky + j + 1, :]
        packed[9 + kx : 10 + kx, :] = under[HALO + j : HALO + j + 1, :]
    first[...] = jnp.where(even, right[...], left[...]).astype(BF16)
    second[...] = jnp.where(even, left[...], right[...]).astype(BF16)


def trunk_kernel(blocks, trunk_hbm, w_sensor, trunk, mean_trunk, w_out, arrived):
    steps = arrived.shape[0]
    depth = trunk.shape[0] // steps
    copies = [
        pltpu.make_async_copy(trunk_hbm.at[pl.ds(i * depth, depth)], trunk.at[pl.ds(i * depth, depth)], arrived.at[i])
        for i in range(steps)
    ]
    for copy in copies:
        copy.start()
    at = 0
    for start, size in blocks:
        w_out[at : at + size, :] = w_sensor[start : start + size, :]
        at += size
    share = jnp.full((trunk.shape[1], LANES), 1.0 / (TILE * TILE), BF16)
    for i, copy in enumerate(copies):
        copy.wait()
        rows = slice(i * depth, (i + 1) * depth)
        mean_trunk[rows, :] = dot(trunk[rows, :], share)


def sensor_trunk_kernel(trunk, spread, sensor_trunk):
    width = 1024
    per = width // TILE
    point = lax.broadcasted_iota(jnp.int32, (width, LANES), 0)
    lane = lax.broadcasted_iota(jnp.int32, (width, LANES), 1)
    column = (point & (TILE - 1)) == TILE // 2 - 1 + (lane >> 6)
    away = jnp.where(column, (lane & (TILE - 1)) - (point >> 6), -1)
    total = None
    for step in range(trunk.shape[1] // width):
        pick = jnp.where(away == step * per, 1.0, 0.0).astype(BF16)
        part = dot(trunk[:, step * width : (step + 1) * width], pick)
        total = part if total is None else total + part
    middle = trunk.shape[1] // 2
    row31 = pltpu.roll(trunk[:, middle - LANES : middle].astype(F32), TILE, 1)
    row32 = pltpu.roll(trunk[:, middle : middle + LANES].astype(F32), TILE, 1)
    rows = jnp.where(low_lanes(row31.shape), row31, row32)
    unique = jnp.concatenate([rows, total], axis=1).astype(BF16)
    sensor_trunk[...] = dot(unique, spread[...]).astype(BF16)


def sensor_vectors(sensors, base, count):
    height = HALO * 2 + 16
    low = low_lanes((count, LANES))

    def part(shift, group):
        return sensors[base + shift : base + shift + count, group * LANES : (group + 1) * LANES]

    parts = [
        jnp.where(low, part(-1, 0), part(1, 0)),
        jnp.where(low, part(-height - 1, 1), part(-height + 1, 1)),
        jnp.where(low, part(height - 1, 2), part(height + 1, 2)),
        jnp.where(low, part(-height, 3), part(height, 3)),
    ]
    return jnp.concatenate([p.astype(BF16) for p in parts], axis=1)


def branch(vectors, w1, b1, w2, b2, w3, b3):
    hidden = jnp.tanh(dot(vectors, w1[...]) + b1[...]).astype(BF16)
    hidden = jnp.tanh(dot(hidden, w2[...]) + b2[...]).astype(BF16)
    return (dot(hidden, w3[...]) + b3[...]).astype(BF16)


def send_means(coeffs, pool, mean_trunk, col, cells, payload):
    pooled = dot(pool[...], coeffs)
    means = dot(pooled, mean_trunk[...], precision=lax.Precision.HIGHEST)
    lane = lax.broadcasted_iota(jnp.int32, means.shape, 1)
    cell = lax.broadcasted_iota(jnp.int32, means.shape, 0)
    mine = ((lane - cells * col) & (LANES - 1)) == cell
    line = jnp.sum(jnp.where(mine, means, 0.0), axis=0, keepdims=True)
    payload[...] = jnp.broadcast_to(line, payload.shape)


def corrections(gathered, coarse, n_row, n_col, cells):
    blocks = n_col * cells // LANES
    lane = lax.broadcasted_iota(jnp.int32, (n_col, LANES), 1)
    source = cells * lax.broadcasted_iota(jnp.int32, (n_col, LANES), 0)
    block = (source + ((lane - source) & (LANES - 1))) // LANES
    total = None
    for r in range(n_row):
        values = gathered[r * n_col : (r + 1) * n_col, :]
        for k in range(blocks):
            line = jnp.sum(jnp.where(block == k, values, 0.0), axis=0, keepdims=True)
            at = (r * blocks + k) * LANES
            term = coarse[:, at : at + LANES] * line
            total = term if total is None else total + term
    return jnp.sum(total, axis=1, keepdims=True)


def own_vectors(na, nb, sensors, base):
    height = na + 2 * HALO
    return jnp.concatenate(
        [sensor_vectors(sensors, base + b * height + HALO, na) for b in range(nb)], axis=0
    )


def zero_ends(sensors):
    rows = sensors.shape[0]
    sensors[0:8, :] = jnp.zeros((8, sensors.shape[1]), F32)
    sensors[rows - 8 : rows, :] = jnp.zeros((8, sensors.shape[1]), F32)


def first_kernel(
    na, nb, n_col, cells, mid, first, second, above, below, c_own, spread, w1, b1, w2, b2, w3, b3, pool, mean_trunk,
    coeffs, payload, coarse, sensors, tiles,
):
    height, values = na + 2 * HALO, 4 * TILE
    side = HALO * height
    wide = nb * height
    tiles[side : side + wide, :] = mid[...].astype(F32)
    col = lax.axis_index("col")
    even = col % 2 == 0
    one, other = first[...].astype(F32), second[...].astype(F32)
    left = jnp.where(col == 0, 0.0, jnp.where(even, other, one))
    right = jnp.where(col == n_col - 1, 0.0, jnp.where(even, one, other))
    edge = [above[...].astype(F32), below[...].astype(F32), left, right]
    for lines, start in ((left, 0), (right, side + wide)):
        for g in range(side // 8):
            tiles[start + 8 * g : start + 8 * (g + 1), :] = lines[0:8, g * values : (g + 1) * values]
    zero_ends(sensors)
    sensors[8 : 8 + 2 * side + wide, :] = dot(tiles[...].astype(BF16), spread[...])
    vectors = sensor_vectors(sensors, 8 + height, coeffs.shape[0])
    result = branch(vectors, w1, b1, w2, b2, w3, b3)
    coeffs[...] = result
    send_means(result, pool, mean_trunk, lax.axis_index("col"), cells, payload)
    kx, ky = na // PER_CELL, nb // PER_CELL
    coarse[0 : kx + 2, :] = edge[2][8 : 10 + kx, :]
    coarse[8 * (ky + 1) : 8 * (ky + 1) + kx + 2, :] = edge[3][8 : 10 + kx, :]
    for j in range(ky):
        at = 8 * (j + 1)
        coarse[at : at + 1, :] = edge[0][HALO + j : HALO + j + 1, :]
        for i in range(kx):
            coarse[at + 1 + i : at + 2 + i, :] = c_own[i * ky + j : i * ky + j + 1, :]
        coarse[at + 1 + kx : at + 2 + kx, :] = edge[1][HALO + j : HALO + j + 1, :]
    for j in range(ky + 2):
        at = 8 * j + kx + 2
        coarse[at : 8 * (j + 1), :] = jnp.zeros((6 - kx, coarse.shape[1]), F32)


def next_kernel(
    k, na, nb, n_row, n_col, cells, gathered, before, sensor_trunk, coarse, w1, b1, w2, b2, w3, b3,
    pool, mean_trunk, coeffs, payload, sensors, lines,
):
    height = na + 2 * HALO
    predicted = dot(before[...], sensor_trunk[...])
    found = corrections(gathered, coarse, n_row, n_col, cells)
    found = jnp.broadcast_to(found, (found.shape[0], sensors.shape[1]))
    row, col = lax.axis_index("row"), lax.axis_index("col")
    a_at = row * na - HALO + lax.broadcasted_iota(jnp.int32, (height, 1), 0)
    a_ok = (a_at >= 0) & (a_at < n_row * na)
    for j in range(nb // PER_CELL + 2):
        for i in range(height // PER_CELL):
            at = j * height + i * PER_CELL
            lines[at : at + PER_CELL, :] = jnp.broadcast_to(
                found[8 * j + i : 8 * j + i + 1, :], (PER_CELL, found.shape[1])
            )
    zero_ends(sensors)
    first = k - 1
    have = nb + 2 * HALO - 2 * first
    for i in range(have):
        b = first + i
        b_at = col * nb - HALO + b
        inside = jnp.where(a_ok & (b_at >= 0) & (b_at < n_col * nb), 1.0, 0.0)
        cell = b // PER_CELL
        value = predicted[i * height : (i + 1) * height, :] + lines[cell * height : (cell + 1) * height, :]
        sensors[8 + i * height : 8 + (i + 1) * height, :] = jnp.where(inside > 0.5, value, 0.0)
    if k < ITERS:
        vectors = sensor_vectors(sensors, 8 + height, coeffs.shape[0])
    else:
        vectors = own_vectors(na, nb, sensors, 8 + height)
    result = branch(vectors, w1, b1, w2, b2, w3, b3)
    coeffs[...] = result
    send_means(result, pool, mean_trunk, col, cells, payload)


def field_kernel(na, nb, n_row, n_col, cells, gathered, coarse, coeffs, trunk, out, correction, strip, ready, sent):
    steps = ready.shape[0]
    width = trunk.shape[1] // steps
    per = width // TILE
    ky = nb // PER_CELL
    found = corrections(gathered, coarse, n_row, n_col, cells)
    correction[...] = jnp.broadcast_to(found, correction.shape)
    upper = lax.broadcasted_iota(jnp.int32, (8, LANES), 0) < PER_CELL
    adds = {}
    for a in range(0, na, 8):
        for j in range(ky):
            at = a // PER_CELL * ky + j
            adds[a, j] = jnp.where(upper, correction[at : at + 1, :], correction[at + ky : at + ky + 1, :])
    low = low_lanes((8, LANES))
    copies = []
    for step in range(steps):
        values = dot(coeffs[...], trunk[:, step * width : (step + 1) * width])
        for pair in range(nb // 2):
            for a in range(0, na, 8):
                add = adds[a, 2 * pair // PER_CELL]
                even, odd = (2 * pair * na + a, (2 * pair + 1) * na + a)
                for r in range(0, per, 2):
                    lanes = slice(r * TILE, r * TILE + LANES)
                    x, y = values[even : even + 8, lanes], values[odd : odd + 8, lanes]
                    at = (pair * na + a) * per + r
                    strip[pl.ds(at, 8, stride=per), :] = jnp.where(low, x, pltpu.roll(y, TILE, 1)) + add
                    strip[pl.ds(at + 1, 8, stride=per), :] = jnp.where(low, pltpu.roll(x, TILE, 1), y) + add
            done = strip[pair * na * per : (pair + 1) * na * per, :].reshape(na, per, LANES)
            ready[step, :, :, pair * LANES : (pair + 1) * LANES] = done
        copies.append(
            pltpu.make_async_copy(ready.at[step], out.at[:, pl.ds(step * per, per), :], sent.at[step])
        )
        copies[-1].start()
    for copy in copies:
        copy.wait()


def pool_matrix(na, nb, first, trimmed):
    kx, ky = na // PER_CELL, nb // PER_CELL
    height = na if trimmed else na + 2 * HALO
    skip_a = 0 if trimmed else HALO
    skip_b = HALO - first
    wide = nb + 2 * skip_b
    pool = np.zeros((16, wide * height), np.float32)
    for a in range(na):
        for b in range(nb):
            cell = (a // PER_CELL) * ky + b // PER_CELL
            pool[cell, (b + skip_b) * height + a + skip_a] = 1.0 / PER_CELL**2
    return jnp.asarray(pool, BF16)


def body(
    field_start,
    w_sensor,
    bias_sensor,
    w_middle,
    bias_middle,
    w_latent,
    bias_latent,
    trunk_basis,
    coarse_matrix,
):
    rows_here, cols_here = field_start.shape
    n_row, n_col = lax.axis_size("row"), lax.axis_size("col")
    na, nb = rows_here // TILE, cols_here // TILE
    height = na + 2 * HALO
    kx, ky = na // PER_CELL, nb // PER_CELL
    cells = kx * ky
    devices = n_row * n_col
    latent = trunk_basis.shape[0]
    hid = w_sensor.shape[1]
    tile_values, places = 4 * TILE, 8 * TILE
    total = coarse_matrix.shape[1]
    whole = pl.BlockSpec(memory_space=pltpu.VMEM)
    shape = jax.ShapeDtypeStruct
    part = functools.partial

    def shift(x, step):
        return lax.ppermute(x, "row", [(i, (i + step) % n_row) for i in range(n_row)])

    def swap(x, parity):
        pairs = [(i, (i + 1 if i % 2 == parity else i - 1) % n_col) for i in range(n_col)]
        return lax.ppermute(x, "col", pairs)

    def exchange(x):
        return lax.all_to_all(x, ("row", "col"), 0, 0, tiled=True)

    spread_np, order = sensor_layout()
    spread = jnp.asarray(spread_np, BF16)
    half = TILE // 2
    blocks = tuple((int(at), half) for at in order[::half])
    hbm = pl.BlockSpec(memory_space=pltpu.HBM)

    row_part, col_part = call(
        part(extract_kernel, na, nb),
        (shape((nb * na, LANES), F32), shape((nb * na, LANES), F32)),
        field_start.reshape(na, TILE, cols_here),
    )
    up, down = call(
        part(pack_kernel, na, nb, ky),
        (shape((8, total), BF16), shape((8, total), BF16)),
        row_part,
        col_part,
        coarse_matrix,
        scratch=[pltpu.VMEM((8, total), F32)],
    )
    above, below = shift(down, 1), shift(up, -1)
    trunk, mean_trunk, w_first = call(
        part(trunk_kernel, blocks),
        (shape(trunk_basis.shape, BF16), shape((latent, LANES), F32), shape(w_sensor.shape, BF16)),
        trunk_basis,
        w_sensor,
        in_specs=[hbm, whole],
        scratch=[pltpu.SemaphoreType.DMA((4,))],
        flops=1 << 32,
    )
    above, below, w_first = lax.optimization_barrier((above, below, w_first))
    mid, first, second = call(
        part(columns_kernel, na, nb, n_row),
        (shape((nb * height, tile_values), BF16), shape((16, total), BF16), shape((16, total), BF16)),
        row_part,
        col_part,
        above,
        below,
        coarse_matrix,
        scratch=[pltpu.VMEM((nb * height, tile_values), F32)] + [pltpu.VMEM((16, total), F32)] * 2,
    )
    second, first = swap(second, 1), swap(first, 0)

    net = (
        w_first,
        bias_sensor.reshape(1, hid),
        w_middle,
        bias_middle.reshape(1, hid),
        w_latent,
        bias_latent.reshape(1, latent),
    )

    sensor_trunk = call(
        sensor_trunk_kernel, shape((latent, places), BF16), trunk, spread, flops=1 << 30
    )
    mid, sensor_trunk = lax.optimization_barrier((mid, sensor_trunk))

    def region(k):
        return (nb + 2 * HALO - 2 * k) * height

    payload_shape = shape((devices, LANES), F32)
    coeffs, payload, coarse = call(
        part(first_kernel, na, nb, n_col, cells),
        (shape((region(1), latent), BF16), payload_shape, shape((8 * (ky + 2), total), F32)),
        mid,
        first,
        second,
        above,
        below,
        coarse_matrix,
        spread,
        *net,
        pool_matrix(na, nb, 1, False),
        mean_trunk,
        scratch=[pltpu.VMEM((region(0) + 16, places), F32), pltpu.VMEM((region(0), tile_values), F32)],
    )
    for k in range(2, ITERS + 1):
        gathered = exchange(payload)
        coeffs, payload = call(
            part(next_kernel, k, na, nb, n_row, n_col, cells),
            (shape((region(k) if k < ITERS else nb * na, latent), BF16), payload_shape),
            gathered,
            coeffs,
            sensor_trunk,
            coarse,
            *net,
            pool_matrix(na, nb, k, k == ITERS),
            mean_trunk,
            scratch=[
                pltpu.VMEM((region(k - 1) + 16, places), F32),
                pltpu.VMEM(((ky + 2) * height, places), F32),
            ],
        )
    gathered = exchange(payload)
    steps = 8
    out = call(
        part(field_kernel, na, nb, n_row, n_col, cells),
        shape((na, TILE, cols_here), F32),
        gathered,
        coarse_matrix,
        coeffs,
        trunk,
        out_specs=hbm,
        scratch=[
            pltpu.VMEM((cells, LANES), F32),
            pltpu.VMEM((rows_here * cols_here // steps // LANES, LANES), F32),
            pltpu.VMEM((steps, na, TILE // steps, cols_here), F32),
            pltpu.SemaphoreType.DMA((steps,)),
        ],
    )
    return out.reshape(rows_here, cols_here)


def solution(mesh):
    placed = (P("row", "col"), P(), P(), P(), P(), P(), P(), P(), P(("row", "col"), None))
    return jax.shard_map(
        body, mesh=mesh, in_specs=placed, out_specs=P("row", "col"), check_vma=False
    )
```

```python
import functools

import jax
import jax.numpy as jnp
import numpy as np
from jax import lax
from jax.experimental import pallas as pl
from jax.experimental.pallas import tpu as pltpu
from jax.sharding import PartitionSpec as P

TILE = 64
ITERS = 4
CELL = 256
PER_CELL = CELL // TILE
HALO = ITERS
LANES = 128
F32 = jnp.float32
BF16 = jnp.bfloat16
VMEM_LIMIT = 48 * 1024 * 1024


def dot(a, b, **kw):
    return jnp.dot(a, b, preferred_element_type=F32, **kw)


def nt_dot(a, b):
    return lax.dot_general(a, b, (((1,), (1,)), ((), ())), preferred_element_type=F32)


def low_lanes(shape):
    return lax.broadcasted_iota(jnp.int32, shape, 1) < TILE


def call(kernel, out_shape, *args, grid=(), in_specs=None, out_specs=None, scratch=(), flops=1 << 31, vmem=VMEM_LIMIT):
    whole = pl.BlockSpec(memory_space=pltpu.VMEM)
    specs = {}
    if grid:
        specs["grid"] = grid
    return pl.pallas_call(
        kernel,
        out_shape=out_shape,
        in_specs=in_specs or [whole] * len(args),
        out_specs=out_specs or jax.tree.map(lambda _: whole, out_shape),
        scratch_shapes=list(scratch),
        compiler_params=pltpu.CompilerParams(vmem_limit_bytes=vmem),
        cost_estimate=pl.CostEstimate(flops=flops, bytes_accessed=1 << 20, transcendentals=0),
        **specs,
    )(*args)


def sensor_layout():
    half = TILE // 2
    row31, row32, col31, col32 = (np.arange(TILE) + TILE * i for i in range(4))
    top, bottom, left, right = (np.arange(2 * TILE) + 2 * TILE * i for i in range(4))
    mid = slice(half, half + TILE)
    groups = [
        (row32, top[mid]),
        (row31, bottom[mid]),
        (np.r_[row32[half:], col32[half:]], np.r_[top[:half], left[:half]]),
        (np.r_[row31[half:], col32[:half]], np.r_[bottom[:half], left[-half:]]),
        (np.r_[row32[:half], col31[half:]], np.r_[top[-half:], right[:half]]),
        (np.r_[row31[:half], col31[:half]], np.r_[bottom[-half:], right[-half:]]),
        (col32, left[mid]),
        (col31, right[mid]),
    ]
    source = np.concatenate([g[0] for g in groups])
    order = np.concatenate([g[1] for g in groups])
    spread = np.zeros((4 * TILE, 8 * TILE), np.float32)
    spread[source, np.arange(8 * TILE)] = 1.0
    return spread, order


def extract_kernel(na, nb, cells, row_part, col_part):
    cols = cells.shape[2]
    here = 8
    sel_row = lax.broadcasted_iota(jnp.int32, (2 * 16, cols), 0)
    sel_col = lax.broadcasted_iota(jnp.int32, (2 * 16, cols), 1)
    side, b_of = sel_row // 16, sel_row % 16
    pick = jnp.where(sel_col == b_of * TILE + (TILE // 2 - 1) + side, 1.0, 0.0).astype(BF16)
    low_row, low_col = low_lanes((here, LANES)), low_lanes((16, LANES))
    for base in range(0, na, here):
        chunk = cells[base : base + here]
        picked = nt_dot(pick, chunk.reshape(here * TILE, cols).astype(BF16))
        r31 = cells[base : base + here, TILE // 2 - 1, :]
        r32 = cells[base : base + here, TILE // 2, :]
        for pair in range(nb // 2):
            lanes = slice(pair * LANES, (pair + 1) * LANES)
            x, y = r31[:, lanes], r32[:, lanes]
            even, odd = 2 * pair * na + base, (2 * pair + 1) * na + base
            row_part[even : even + here, :] = jnp.where(low_row, x, pltpu.roll(y, TILE, 1))
            row_part[odd : odd + here, :] = jnp.where(low_row, pltpu.roll(x, TILE, 1), y)
        for pair in range(here // 2):
            lanes = slice(pair * LANES, (pair + 1) * LANES)
            x, y = picked[0:16, lanes], picked[16:32, lanes]
            even = jnp.where(low_col, x, pltpu.roll(y, TILE, 1))
            odd = jnp.where(low_col, pltpu.roll(x, TILE, 1), y)
            col_part[pl.ds(base + 2 * pair, nb, stride=na), :] = even[0:nb]
            col_part[pl.ds(base + 2 * pair + 1, nb, stride=na), :] = odd[0:nb]


def pack_kernel(na, nb, ky, row_part, col_part, coarse, up, down, packed):
    packed[...] = jnp.zeros(packed.shape, F32)
    for target, first, line in ((up, 0, 0), (down, na - HALO, coarse.shape[0] - ky)):
        for b in range(nb):
            rows = slice(b * na + first, b * na + first + HALO)
            packed[0:HALO, 2 * b * LANES : (2 * b + 1) * LANES] = row_part[rows, :]
            packed[0:HALO, (2 * b + 1) * LANES : (2 * b + 2) * LANES] = col_part[rows, :]
        packed[HALO : HALO + ky, :] = coarse[line : line + ky, :]
        target[...] = packed[...].astype(BF16)


def columns_kernel(na, nb, n_row, row_part, col_part, above, below, coarse, both, first, second, tall, left, right):
    height, values = na + 2 * HALO, 4 * TILE
    kx, ky = na // PER_CELL, nb // PER_CELL
    row, even = lax.axis_index("row"), lax.axis_index("col") % 2 == 0
    over = jnp.where(row == 0, 0.0, above[...].astype(F32))
    under = jnp.where(row == n_row - 1, 0.0, below[...].astype(F32))
    for b in range(nb):
        at = b * height
        tall[at : at + HALO, :] = over[0:HALO, b * values : (b + 1) * values]
        tall[at + HALO : at + HALO + na, 0:LANES] = row_part[b * na : (b + 1) * na, :]
        tall[at + HALO : at + HALO + na, LANES : 2 * LANES] = col_part[b * na : (b + 1) * na, :]
        tall[at + HALO + na : at + height, :] = under[0:HALO, b * values : (b + 1) * values]
    both[...] = tall[...].astype(BF16)
    for packed, start, j in ((left, 0, 0), (right, nb - HALO, ky - 1)):
        packed[...] = jnp.zeros(packed.shape, F32)
        for b in range(HALO):
            for g in range(height // 8):
                lanes = slice((b * (height // 8) + g) * values, (b * (height // 8) + g + 1) * values)
                at = (start + b) * height + 8 * g
                packed[0:8, lanes] = tall[at : at + 8, :]
        packed[8:9, :] = over[HALO + j : HALO + j + 1, :]
        for i in range(kx):
            packed[9 + i : 10 + i, :] = coarse[i * ky + j : i * ky + j + 1, :]
        packed[9 + kx : 10 + kx, :] = under[HALO + j : HALO + j + 1, :]
    first[...] = jnp.where(even, right[...], left[...]).astype(BF16)
    second[...] = jnp.where(even, left[...], right[...]).astype(BF16)


def trunk_kernel(blocks, trunk_hbm, w_sensor, trunk, mean_trunk, w_out, arrived):
    steps = arrived.shape[0]
    depth = trunk.shape[0] // steps
    copies = [
        pltpu.make_async_copy(trunk_hbm.at[pl.ds(i * depth, depth)], trunk.at[pl.ds(i * depth, depth)], arrived.at[i])
        for i in range(steps)
    ]
    for copy in copies:
        copy.start()
    at = 0
    for start, size in blocks:
        w_out[at : at + size, :] = w_sensor[start : start + size, :]
        at += size
    share = jnp.full((trunk.shape[1], LANES), 1.0 / (TILE * TILE), BF16)
    for i, copy in enumerate(copies):
        copy.wait()
        rows = slice(i * depth, (i + 1) * depth)
        mean_trunk[rows, :] = dot(trunk[rows, :], share)


def sensor_trunk_kernel(trunk, spread, mean_trunk, sensor_trunk, mean_line):
    mean_line[...] = jnp.transpose(mean_trunk[...])[0:8, :]
    width = 1024
    per = width // TILE
    point = lax.broadcasted_iota(jnp.int32, (width, LANES), 0)
    lane = lax.broadcasted_iota(jnp.int32, (width, LANES), 1)
    column = (point & (TILE - 1)) == TILE // 2 - 1 + (lane >> 6)
    away = jnp.where(column, (lane & (TILE - 1)) - (point >> 6), -1)
    total = None
    for step in range(trunk.shape[1] // width):
        pick = jnp.where(away == step * per, 1.0, 0.0).astype(BF16)
        part = dot(trunk[:, step * width : (step + 1) * width], pick)
        total = part if total is None else total + part
    middle = trunk.shape[1] // 2
    row31 = pltpu.roll(trunk[:, middle - LANES : middle].astype(F32), TILE, 1)
    row32 = pltpu.roll(trunk[:, middle : middle + LANES].astype(F32), TILE, 1)
    rows = jnp.where(low_lanes(row31.shape), row31, row32)
    unique = jnp.concatenate([rows, total], axis=1).astype(BF16)
    sensor_trunk[...] = dot(unique, spread[...]).astype(BF16)


def sensor_vectors(sensors, base, count):
    height = HALO * 2 + 16
    low = low_lanes((count, LANES))

    def part(shift, group):
        return sensors[base + shift : base + shift + count, group * LANES : (group + 1) * LANES]

    parts = [
        jnp.where(low, part(-1, 0), part(1, 0)),
        jnp.where(low, part(-height - 1, 1), part(-height + 1, 1)),
        jnp.where(low, part(height - 1, 2), part(height + 1, 2)),
        jnp.where(low, part(-height, 3), part(height, 3)),
    ]
    return jnp.concatenate([p.astype(BF16) for p in parts], axis=1)


def branch(vectors, w1, b1, w2, b2, w3, b3):
    hidden = jnp.tanh(dot(vectors, w1[...]) + b1[...]).astype(BF16)
    hidden = jnp.tanh(dot(hidden, w2[...]) + b2[...]).astype(BF16)
    return (dot(hidden, w3[...]) + b3[...]).astype(BF16)


def send_means(coeffs, columns, na, ky, height, mean_line, col, cells, payload):
    skip = (height - na) // 2
    share = mean_line[0:1, :] * (1.0 / PER_CELL**2)
    lane = lax.broadcasted_iota(jnp.int32, (height, LANES), 1)
    line = lax.broadcasted_iota(jnp.int32, (height, LANES), 0) - skip
    inside = (line >= 0) & (line < na)
    place = jnp.where(inside, (line >> 2) * ky, -LANES)
    total = None
    for j in range(ky):
        tiles = None
        for b in range(PER_CELL * j, PER_CELL * (j + 1)):
            at = (b - columns) * height
            part = coeffs[at : at + height, :].astype(F32)
            tiles = part if tiles is None else tiles + part
        sums = jnp.sum(tiles * share, axis=1, keepdims=True)
        mine = ((lane - cells * col) & (LANES - 1)) == place + j
        part = jnp.where(mine, sums, 0.0)
        total = part if total is None else total + part
    payload[...] = jnp.broadcast_to(jnp.sum(total, axis=0, keepdims=True), payload.shape)


def corrections(gathered, coarse, n_row, n_col, cells):
    blocks = n_col * cells // LANES
    lane = lax.broadcasted_iota(jnp.int32, (n_col, LANES), 1)
    source = cells * lax.broadcasted_iota(jnp.int32, (n_col, LANES), 0)
    block = (source + ((lane - source) & (LANES - 1))) // LANES
    total = None
    for r in range(n_row):
        values = gathered[r * n_col : (r + 1) * n_col, :]
        for k in range(blocks):
            line = jnp.sum(jnp.where(block == k, values, 0.0), axis=0, keepdims=True)
            at = (r * blocks + k) * LANES
            term = coarse[:, at : at + LANES] * line
            total = term if total is None else total + term
    return jnp.sum(total, axis=1, keepdims=True)


def own_vectors(na, nb, sensors, base):
    height = na + 2 * HALO
    return jnp.concatenate(
        [sensor_vectors(sensors, base + b * height + HALO, na) for b in range(nb)], axis=0
    )


def zero_ends(sensors):
    rows = sensors.shape[0]
    sensors[0:8, :] = jnp.zeros((8, sensors.shape[1]), F32)
    sensors[rows - 8 : rows, :] = jnp.zeros((8, sensors.shape[1]), F32)


def first_kernel(
    na, nb, n_col, cells, mid, first, second, above, below, c_own, spread, w1, b1, w2, b2, w3, b3, mean_line,
    coeffs, payload, coarse, sensors, tiles,
):
    height, values = na + 2 * HALO, 4 * TILE
    side = HALO * height
    wide = nb * height
    tiles[side : side + wide, :] = mid[...].astype(F32)
    col = lax.axis_index("col")
    even = col % 2 == 0
    one, other = first[...].astype(F32), second[...].astype(F32)
    left = jnp.where(col == 0, 0.0, jnp.where(even, other, one))
    right = jnp.where(col == n_col - 1, 0.0, jnp.where(even, one, other))
    edge = [above[...].astype(F32), below[...].astype(F32), left, right]
    for lines, start in ((left, 0), (right, side + wide)):
        for g in range(side // 8):
            tiles[start + 8 * g : start + 8 * (g + 1), :] = lines[0:8, g * values : (g + 1) * values]
    zero_ends(sensors)
    sensors[8 : 8 + 2 * side + wide, :] = dot(tiles[...].astype(BF16), spread[...])
    vectors = sensor_vectors(sensors, 8 + height, coeffs.shape[0])
    result = branch(vectors, w1, b1, w2, b2, w3, b3)
    coeffs[...] = result
    send_means(result, 1 - HALO, na, nb // PER_CELL, height, mean_line, col, cells, payload)
    kx, ky = na // PER_CELL, nb // PER_CELL
    coarse[0 : kx + 2, :] = edge[2][8 : 10 + kx, :]
    coarse[8 * (ky + 1) : 8 * (ky + 1) + kx + 2, :] = edge[3][8 : 10 + kx, :]
    for j in range(ky):
        at = 8 * (j + 1)
        coarse[at : at + 1, :] = edge[0][HALO + j : HALO + j + 1, :]
        for i in range(kx):
            coarse[at + 1 + i : at + 2 + i, :] = c_own[i * ky + j : i * ky + j + 1, :]
        coarse[at + 1 + kx : at + 2 + kx, :] = edge[1][HALO + j : HALO + j + 1, :]
    for j in range(ky + 2):
        at = 8 * j + kx + 2
        coarse[at : 8 * (j + 1), :] = jnp.zeros((6 - kx, coarse.shape[1]), F32)


def next_kernel(
    k, na, nb, n_row, n_col, cells, gathered, before, sensor_trunk, coarse, w1, b1, w2, b2, w3, b3,
    mean_line, coeffs, payload, sensors, lines,
):
    height = na + 2 * HALO
    predicted = dot(before[...], sensor_trunk[...])
    found = corrections(gathered, coarse, n_row, n_col, cells)
    found = jnp.broadcast_to(found, (found.shape[0], sensors.shape[1]))
    row, col = lax.axis_index("row"), lax.axis_index("col")
    a_at = row * na - HALO + lax.broadcasted_iota(jnp.int32, (height, 1), 0)
    a_ok = (a_at >= 0) & (a_at < n_row * na)
    for j in range(nb // PER_CELL + 2):
        for i in range(height // PER_CELL):
            at = j * height + i * PER_CELL
            lines[at : at + PER_CELL, :] = jnp.broadcast_to(
                found[8 * j + i : 8 * j + i + 1, :], (PER_CELL, found.shape[1])
            )
    zero_ends(sensors)
    first = k - 1
    have = nb + 2 * HALO - 2 * first
    for i in range(have):
        b = first + i
        b_at = col * nb - HALO + b
        inside = jnp.where(a_ok & (b_at >= 0) & (b_at < n_col * nb), 1.0, 0.0)
        cell = b // PER_CELL
        value = predicted[i * height : (i + 1) * height, :] + lines[cell * height : (cell + 1) * height, :]
        sensors[8 + i * height : 8 + (i + 1) * height, :] = jnp.where(inside > 0.5, value, 0.0)
    if k < ITERS:
        vectors = sensor_vectors(sensors, 8 + height, coeffs.shape[0])
    else:
        vectors = own_vectors(na, nb, sensors, 8 + height)
    result = branch(vectors, w1, b1, w2, b2, w3, b3)
    coeffs[...] = result
    skip = (k - HALO, height) if k < ITERS else (0, na)
    send_means(result, skip[0], na, nb // PER_CELL, skip[1], mean_line, col, cells, payload)


def field_kernel(na, nb, n_row, n_col, cells, gathered, coarse, coeffs, trunk, out, correction, ready, sent):
    steps = ready.shape[0]
    width = trunk.shape[1] // steps
    per = width // TILE
    ky = nb // PER_CELL
    found = corrections(gathered, coarse, n_row, n_col, cells)
    correction[...] = jnp.broadcast_to(found, correction.shape)
    upper = lax.broadcasted_iota(jnp.int32, (8, LANES), 0) < PER_CELL
    adds = {}
    for a in range(0, na, 8):
        for j in range(ky):
            at = a // PER_CELL * ky + j
            adds[a, j] = jnp.where(upper, correction[at : at + 1, :], correction[at + ky : at + ky + 1, :])
    low = low_lanes((8, LANES))
    copies = []
    for step in range(steps):
        values = dot(coeffs[...], trunk[:, step * width : (step + 1) * width])
        for pair in range(nb // 2):
            for a in range(0, na, 8):
                even, odd = (2 * pair * na + a, (2 * pair + 1) * na + a)
                lines = []
                for r in range(0, per, 2):
                    lanes = slice(r * TILE, r * TILE + LANES)
                    x, y = values[even : even + 8, lanes], values[odd : odd + 8, lanes]
                    lines.append(jnp.where(low, x, pltpu.roll(y, TILE, 1)))
                    lines.append(jnp.where(low, pltpu.roll(x, TILE, 1), y))
                block = jnp.stack(lines, axis=0) + adds[a, 2 * pair // PER_CELL][None]
                ready[step, a : a + 8, :, pair * LANES : (pair + 1) * LANES] = jnp.swapaxes(block, 0, 1)
        copies.append(
            pltpu.make_async_copy(ready.at[step], out.at[:, pl.ds(step * per, per), :], sent.at[step])
        )
        copies[-1].start()
    for copy in copies:
        copy.wait()


def body(
    field_start,
    w_sensor,
    bias_sensor,
    w_middle,
    bias_middle,
    w_latent,
    bias_latent,
    trunk_basis,
    coarse_matrix,
):
    rows_here, cols_here = field_start.shape
    n_row, n_col = lax.axis_size("row"), lax.axis_size("col")
    na, nb = rows_here // TILE, cols_here // TILE
    height = na + 2 * HALO
    kx, ky = na // PER_CELL, nb // PER_CELL
    cells = kx * ky
    devices = n_row * n_col
    latent = trunk_basis.shape[0]
    hid = w_sensor.shape[1]
    tile_values, places = 4 * TILE, 8 * TILE
    total = coarse_matrix.shape[1]
    whole = pl.BlockSpec(memory_space=pltpu.VMEM)
    shape = jax.ShapeDtypeStruct
    part = functools.partial

    def shift(x, step):
        return lax.ppermute(x, "row", [(i, (i + step) % n_row) for i in range(n_row)])

    def swap(x, parity):
        pairs = [(i, (i + 1 if i % 2 == parity else i - 1) % n_col) for i in range(n_col)]
        return lax.ppermute(x, "col", pairs)

    def exchange(x):
        return lax.all_to_all(x, ("row", "col"), 0, 0, tiled=True)

    spread_np, order = sensor_layout()
    spread = jnp.asarray(spread_np, BF16)
    half = TILE // 2
    blocks = tuple((int(at), half) for at in order[::half])
    hbm = pl.BlockSpec(memory_space=pltpu.HBM)

    row_part, col_part = call(
        part(extract_kernel, na, nb),
        (shape((nb * na, LANES), F32), shape((nb * na, LANES), F32)),
        field_start.reshape(na, TILE, cols_here),
    )
    up, down = call(
        part(pack_kernel, na, nb, ky),
        (shape((8, total), BF16), shape((8, total), BF16)),
        row_part,
        col_part,
        coarse_matrix,
        scratch=[pltpu.VMEM((8, total), F32)],
    )
    above, below = shift(down, 1), shift(up, -1)
    trunk, mean_trunk, w_first = call(
        part(trunk_kernel, blocks),
        (shape(trunk_basis.shape, BF16), shape((latent, LANES), F32), shape(w_sensor.shape, BF16)),
        trunk_basis,
        w_sensor,
        in_specs=[hbm, whole],
        scratch=[pltpu.SemaphoreType.DMA((4,))],
        flops=1 << 32,
    )
    above, below, w_first = lax.optimization_barrier((above, below, w_first))
    mid, first, second = call(
        part(columns_kernel, na, nb, n_row),
        (shape((nb * height, tile_values), BF16), shape((16, total), BF16), shape((16, total), BF16)),
        row_part,
        col_part,
        above,
        below,
        coarse_matrix,
        scratch=[pltpu.VMEM((nb * height, tile_values), F32)] + [pltpu.VMEM((16, total), F32)] * 2,
    )
    second, first = swap(second, 1), swap(first, 0)

    net = (
        w_first,
        bias_sensor.reshape(1, hid),
        w_middle,
        bias_middle.reshape(1, hid),
        w_latent,
        bias_latent.reshape(1, latent),
    )

    sensor_trunk, mean_line = call(
        sensor_trunk_kernel,
        (shape((latent, places), BF16), shape((8, latent), F32)),
        trunk,
        spread,
        mean_trunk,
        flops=1 << 30,
    )
    mid, sensor_trunk = lax.optimization_barrier((mid, sensor_trunk))

    def region(k):
        return (nb + 2 * HALO - 2 * k) * height

    payload_shape = shape((devices, LANES), F32)
    coeffs, payload, coarse = call(
        part(first_kernel, na, nb, n_col, cells),
        (shape((region(1), latent), BF16), payload_shape, shape((8 * (ky + 2), total), F32)),
        mid,
        first,
        second,
        above,
        below,
        coarse_matrix,
        spread,
        *net,
        mean_line,
        scratch=[pltpu.VMEM((region(0) + 16, places), F32), pltpu.VMEM((region(0), tile_values), F32)],
    )
    for k in range(2, ITERS + 1):
        gathered = exchange(payload)
        coeffs, payload = call(
            part(next_kernel, k, na, nb, n_row, n_col, cells),
            (shape((region(k) if k < ITERS else nb * na, latent), BF16), payload_shape),
            gathered,
            coeffs,
            sensor_trunk,
            coarse,
            *net,
            mean_line,
            scratch=[
                pltpu.VMEM((region(k - 1) + 16, places), F32),
                pltpu.VMEM(((ky + 2) * height, places), F32),
            ],
        )
    gathered = exchange(payload)
    steps = 8
    out = call(
        part(field_kernel, na, nb, n_row, n_col, cells),
        shape((na, TILE, cols_here), F32),
        gathered,
        coarse_matrix,
        coeffs,
        trunk,
        out_specs=hbm,
        scratch=[
            pltpu.VMEM((cells, LANES), F32),
            pltpu.VMEM((steps, na, TILE // steps, cols_here), F32),
            pltpu.SemaphoreType.DMA((steps,)),
        ],
    )
    return out.reshape(rows_here, cols_here)


def solution(mesh):
    placed = (P("row", "col"), P(), P(), P(), P(), P(), P(), P(), P(("row", "col"), None))
    return jax.shard_map(
        body, mesh=mesh, in_specs=placed, out_specs=P("row", "col"), check_vma=False
    )
```

```python
import functools

import jax
import jax.numpy as jnp
import numpy as np
from jax import lax
from jax.experimental import pallas as pl
from jax.experimental.pallas import tpu as pltpu
from jax.sharding import PartitionSpec as P

TILE = 64
ITERS = 4
CELL = 256
PER_CELL = CELL // TILE
HALO = ITERS
LANES = 128
F32 = jnp.float32
BF16 = jnp.bfloat16
VMEM_LIMIT = 48 * 1024 * 1024


def dot(a, b, **kw):
    return jnp.dot(a, b, preferred_element_type=F32, **kw)


def nt_dot(a, b):
    return lax.dot_general(a, b, (((1,), (1,)), ((), ())), preferred_element_type=F32)


def low_lanes(shape):
    return lax.broadcasted_iota(jnp.int32, shape, 1) < TILE


def call(kernel, out_shape, *args, grid=(), in_specs=None, out_specs=None, scratch=(), flops=1 << 31, vmem=VMEM_LIMIT):
    whole = pl.BlockSpec(memory_space=pltpu.VMEM)
    specs = {}
    if grid:
        specs["grid"] = grid
    return pl.pallas_call(
        kernel,
        out_shape=out_shape,
        in_specs=in_specs or [whole] * len(args),
        out_specs=out_specs or jax.tree.map(lambda _: whole, out_shape),
        scratch_shapes=list(scratch),
        compiler_params=pltpu.CompilerParams(vmem_limit_bytes=vmem),
        cost_estimate=pl.CostEstimate(flops=flops, bytes_accessed=1 << 20, transcendentals=0),
        **specs,
    )(*args)


def sensor_layout():
    half = TILE // 2
    row31, row32, col31, col32 = (np.arange(TILE) + TILE * i for i in range(4))
    top, bottom, left, right = (np.arange(2 * TILE) + 2 * TILE * i for i in range(4))
    mid = slice(half, half + TILE)
    groups = [
        (row32, top[mid]),
        (row31, bottom[mid]),
        (np.r_[row32[half:], col32[half:]], np.r_[top[:half], left[:half]]),
        (np.r_[row31[half:], col32[:half]], np.r_[bottom[:half], left[-half:]]),
        (np.r_[row32[:half], col31[half:]], np.r_[top[-half:], right[:half]]),
        (np.r_[row31[:half], col31[:half]], np.r_[bottom[-half:], right[-half:]]),
        (col32, left[mid]),
        (col31, right[mid]),
    ]
    source = np.concatenate([g[0] for g in groups])
    order = np.concatenate([g[1] for g in groups])
    spread = np.zeros((4 * TILE, 8 * TILE), np.float32)
    spread[source, np.arange(8 * TILE)] = 1.0
    return spread, order


def extract_tiles(nb, cells, row_part, col_part):
    here, _, cols = cells.shape
    sel_row = lax.broadcasted_iota(jnp.int32, (2 * 16, cols), 0)
    sel_col = lax.broadcasted_iota(jnp.int32, (2 * 16, cols), 1)
    side, b_of = sel_row >> 4, sel_row & 15
    pick = jnp.where(sel_col == b_of * TILE + (TILE // 2 - 1) + side, 1.0, 0.0).astype(BF16)
    low_row, low_col = low_lanes((here, LANES)), low_lanes((16, LANES))
    picked = nt_dot(pick, cells[...].reshape(here * TILE, cols).astype(BF16))
    r31 = cells[:, TILE // 2 - 1, :]
    r32 = cells[:, TILE // 2, :]
    for pair in range(nb // 2):
        lanes = slice(pair * LANES, (pair + 1) * LANES)
        x, y = r31[:, lanes], r32[:, lanes]
        even, odd = 2 * pair * here, (2 * pair + 1) * here
        row_part[even : even + here, :] = jnp.where(low_row, x, pltpu.roll(y, TILE, 1))
        row_part[odd : odd + here, :] = jnp.where(low_row, pltpu.roll(x, TILE, 1), y)
    for pair in range(here // 2):
        lanes = slice(pair * LANES, (pair + 1) * LANES)
        x, y = picked[0:16, lanes], picked[16:32, lanes]
        even = jnp.where(low_col, x, pltpu.roll(y, TILE, 1))
        odd = jnp.where(low_col, pltpu.roll(x, TILE, 1), y)
        col_part[pl.ds(2 * pair, nb, stride=here), :] = even[0:nb]
        col_part[pl.ds(2 * pair + 1, nb, stride=here), :] = odd[0:nb]


def outer_kernel(nb, ky, top, bottom, coarse, up, down, top_rows, top_cols, bottom_rows, bottom_cols, packed):
    packed[...] = jnp.zeros(packed.shape, F32)
    for target, cells, rows, cols, line in (
        (up, top, top_rows, top_cols, 0),
        (down, bottom, bottom_rows, bottom_cols, coarse.shape[0] - ky),
    ):
        extract_tiles(nb, cells, rows, cols)
        for b in range(nb):
            part = slice(b * HALO, (b + 1) * HALO)
            packed[0:HALO, 2 * b * LANES : (2 * b + 1) * LANES] = rows[part, :]
            packed[0:HALO, (2 * b + 1) * LANES : (2 * b + 2) * LANES] = cols[part, :]
        packed[HALO : HALO + ky, :] = coarse[line : line + ky, :]
        target[...] = packed[...].astype(BF16)


def columns_kernel(
    na, nb, n_row, top_rows, top_cols, mid_rows, mid_cols, bottom_rows, bottom_cols, above, below, coarse,
    both, first, second, tall, left, right,
):
    height, values = na + 2 * HALO, 4 * TILE
    kx, ky = na // PER_CELL, nb // PER_CELL
    row, even = lax.axis_index("row"), lax.axis_index("col") % 2 == 0
    over = jnp.where(row == 0, 0.0, above[...].astype(F32))
    under = jnp.where(row == n_row - 1, 0.0, below[...].astype(F32))
    for b in range(nb):
        at = b * height
        tall[at : at + HALO, :] = over[0:HALO, b * values : (b + 1) * values]
        to = at + HALO
        for rows, cols in ((top_rows, top_cols), (mid_rows, mid_cols), (bottom_rows, bottom_cols)):
            size = rows.shape[0] // nb
            tall[to : to + size, 0:LANES] = rows[b * size : (b + 1) * size, :]
            tall[to : to + size, LANES : 2 * LANES] = cols[b * size : (b + 1) * size, :]
            to += size
        tall[at + HALO + na : at + height, :] = under[0:HALO, b * values : (b + 1) * values]
    both[...] = tall[...].astype(BF16)
    for packed, start, j in ((left, 0, 0), (right, nb - HALO, ky - 1)):
        packed[...] = jnp.zeros(packed.shape, F32)
        for b in range(HALO):
            for g in range(height // 8):
                lanes = slice((b * (height // 8) + g) * values, (b * (height // 8) + g + 1) * values)
                at = (start + b) * height + 8 * g
                packed[0:8, lanes] = tall[at : at + 8, :]
        packed[8:9, :] = over[HALO + j : HALO + j + 1, :]
        for i in range(kx):
            packed[9 + i : 10 + i, :] = coarse[i * ky + j : i * ky + j + 1, :]
        packed[9 + kx : 10 + kx, :] = under[HALO + j : HALO + j + 1, :]
    first[...] = jnp.where(even, right[...], left[...]).astype(BF16)
    second[...] = jnp.where(even, left[...], right[...]).astype(BF16)


def trunk_kernel(blocks, trunk_hbm, w_sensor, trunk, mean_trunk, w_out, arrived):
    steps = arrived.shape[0]
    depth = trunk.shape[0] // steps
    copies = [
        pltpu.make_async_copy(trunk_hbm.at[pl.ds(i * depth, depth)], trunk.at[pl.ds(i * depth, depth)], arrived.at[i])
        for i in range(steps)
    ]
    for copy in copies:
        copy.start()
    at = 0
    for start, size in blocks:
        w_out[at : at + size, :] = w_sensor[start : start + size, :]
        at += size
    share = jnp.full((trunk.shape[1], LANES), 1.0 / (TILE * TILE), BF16)
    for i, copy in enumerate(copies):
        copy.wait()
        rows = slice(i * depth, (i + 1) * depth)
        mean_trunk[rows, :] = dot(trunk[rows, :], share)


def sensor_trunk_kernel(trunk, spread, mean_trunk, sensor_trunk, mean_line):
    mean_line[...] = jnp.transpose(mean_trunk[...])[0:8, :]
    width = 1024
    per = width // TILE
    point = lax.broadcasted_iota(jnp.int32, (width, LANES), 0)
    lane = lax.broadcasted_iota(jnp.int32, (width, LANES), 1)
    column = (point & (TILE - 1)) == TILE // 2 - 1 + (lane >> 6)
    away = jnp.where(column, (lane & (TILE - 1)) - (point >> 6), -1)
    total = None
    for step in range(trunk.shape[1] // width):
        pick = jnp.where(away == step * per, 1.0, 0.0).astype(BF16)
        part = dot(trunk[:, step * width : (step + 1) * width], pick)
        total = part if total is None else total + part
    middle = trunk.shape[1] // 2
    row31 = pltpu.roll(trunk[:, middle - LANES : middle].astype(F32), TILE, 1)
    row32 = pltpu.roll(trunk[:, middle : middle + LANES].astype(F32), TILE, 1)
    rows = jnp.where(low_lanes(row31.shape), row31, row32)
    unique = jnp.concatenate([rows, total], axis=1).astype(BF16)
    sensor_trunk[...] = dot(unique, spread[...]).astype(BF16)


def sensor_vectors(sensors, base, count):
    height = HALO * 2 + 16
    low = low_lanes((count, LANES))

    def part(shift, group):
        return sensors[base + shift : base + shift + count, group * LANES : (group + 1) * LANES]

    parts = [
        jnp.where(low, part(-1, 0), part(1, 0)),
        jnp.where(low, part(-height - 1, 1), part(-height + 1, 1)),
        jnp.where(low, part(height - 1, 2), part(height + 1, 2)),
        jnp.where(low, part(-height, 3), part(height, 3)),
    ]
    return jnp.concatenate([p.astype(BF16) for p in parts], axis=1)


def branch(vectors, w1, b1, w2, b2, w3, b3):
    hidden = jnp.tanh(dot(vectors, w1[...]) + b1[...]).astype(BF16)
    hidden = jnp.tanh(dot(hidden, w2[...]) + b2[...]).astype(BF16)
    return (dot(hidden, w3[...]) + b3[...]).astype(BF16)


def send_means(coeffs, columns, na, ky, height, mean_line, col, cells, payload):
    skip = (height - na) // 2
    share = mean_line[0:1, :] * (1.0 / PER_CELL**2)
    lane = lax.broadcasted_iota(jnp.int32, (height, LANES), 1)
    line = lax.broadcasted_iota(jnp.int32, (height, LANES), 0) - skip
    inside = (line >= 0) & (line < na)
    place = jnp.where(inside, (line >> 2) * ky, -LANES)
    total = None
    for j in range(ky):
        tiles = None
        for b in range(PER_CELL * j, PER_CELL * (j + 1)):
            at = (b - columns) * height
            part = coeffs[at : at + height, :].astype(F32)
            tiles = part if tiles is None else tiles + part
        sums = jnp.sum(tiles * share, axis=1, keepdims=True)
        mine = ((lane - cells * col) & (LANES - 1)) == place + j
        part = jnp.where(mine, sums, 0.0)
        total = part if total is None else total + part
    payload[...] = jnp.broadcast_to(jnp.sum(total, axis=0, keepdims=True), payload.shape)


def corrections(gathered, coarse, n_row, n_col, cells):
    blocks = n_col * cells // LANES
    lane = lax.broadcasted_iota(jnp.int32, (n_col, LANES), 1)
    source = cells * lax.broadcasted_iota(jnp.int32, (n_col, LANES), 0)
    block = (source + ((lane - source) & (LANES - 1))) // LANES
    total = None
    for r in range(n_row):
        values = gathered[r * n_col : (r + 1) * n_col, :]
        for k in range(blocks):
            line = jnp.sum(jnp.where(block == k, values, 0.0), axis=0, keepdims=True)
            at = (r * blocks + k) * LANES
            term = coarse[:, at : at + LANES] * line
            total = term if total is None else total + term
    return jnp.sum(total, axis=1, keepdims=True)


def own_vectors(na, nb, sensors, base):
    height = na + 2 * HALO
    return jnp.concatenate(
        [sensor_vectors(sensors, base + b * height + HALO, na) for b in range(nb)], axis=0
    )


def zero_ends(sensors):
    rows = sensors.shape[0]
    sensors[0:8, :] = jnp.zeros((8, sensors.shape[1]), F32)
    sensors[rows - 8 : rows, :] = jnp.zeros((8, sensors.shape[1]), F32)


def first_kernel(
    na, nb, n_col, cells, mid, first, second, above, below, c_own, spread, w1, b1, w2, b2, w3, b3, mean_line,
    coeffs, payload, coarse, sensors, tiles,
):
    height, values = na + 2 * HALO, 4 * TILE
    side = HALO * height
    wide = nb * height
    tiles[side : side + wide, :] = mid[...].astype(F32)
    col = lax.axis_index("col")
    even = col % 2 == 0
    one, other = first[...].astype(F32), second[...].astype(F32)
    left = jnp.where(col == 0, 0.0, jnp.where(even, other, one))
    right = jnp.where(col == n_col - 1, 0.0, jnp.where(even, one, other))
    edge = [above[...].astype(F32), below[...].astype(F32), left, right]
    for lines, start in ((left, 0), (right, side + wide)):
        for g in range(side // 8):
            tiles[start + 8 * g : start + 8 * (g + 1), :] = lines[0:8, g * values : (g + 1) * values]
    zero_ends(sensors)
    sensors[8 : 8 + 2 * side + wide, :] = dot(tiles[...].astype(BF16), spread[...])
    vectors = sensor_vectors(sensors, 8 + height, coeffs.shape[0])
    result = branch(vectors, w1, b1, w2, b2, w3, b3)
    coeffs[...] = result
    send_means(result, 1 - HALO, na, nb // PER_CELL, height, mean_line, col, cells, payload)
    kx, ky = na // PER_CELL, nb // PER_CELL
    coarse[0 : kx + 2, :] = edge[2][8 : 10 + kx, :]
    coarse[8 * (ky + 1) : 8 * (ky + 1) + kx + 2, :] = edge[3][8 : 10 + kx, :]
    for j in range(ky):
        at = 8 * (j + 1)
        coarse[at : at + 1, :] = edge[0][HALO + j : HALO + j + 1, :]
        for i in range(kx):
            coarse[at + 1 + i : at + 2 + i, :] = c_own[i * ky + j : i * ky + j + 1, :]
        coarse[at + 1 + kx : at + 2 + kx, :] = edge[1][HALO + j : HALO + j + 1, :]
    for j in range(ky + 2):
        at = 8 * j + kx + 2
        coarse[at : 8 * (j + 1), :] = jnp.zeros((6 - kx, coarse.shape[1]), F32)


def next_kernel(
    k, na, nb, n_row, n_col, cells, gathered, before, sensor_trunk, coarse, w1, b1, w2, b2, w3, b3,
    mean_line, coeffs, payload, sensors, lines,
):
    height = na + 2 * HALO
    predicted = dot(before[...], sensor_trunk[...])
    found = corrections(gathered, coarse, n_row, n_col, cells)
    found = jnp.broadcast_to(found, (found.shape[0], sensors.shape[1]))
    row, col = lax.axis_index("row"), lax.axis_index("col")
    a_at = row * na - HALO + lax.broadcasted_iota(jnp.int32, (height, 1), 0)
    a_ok = (a_at >= 0) & (a_at < n_row * na)
    for j in range(nb // PER_CELL + 2):
        for i in range(height // PER_CELL):
            at = j * height + i * PER_CELL
            lines[at : at + PER_CELL, :] = jnp.broadcast_to(
                found[8 * j + i : 8 * j + i + 1, :], (PER_CELL, found.shape[1])
            )
    zero_ends(sensors)
    first = k - 1
    have = nb + 2 * HALO - 2 * first
    for i in range(have):
        b = first + i
        b_at = col * nb - HALO + b
        inside = jnp.where(a_ok & (b_at >= 0) & (b_at < n_col * nb), 1.0, 0.0)
        cell = b // PER_CELL
        value = predicted[i * height : (i + 1) * height, :] + lines[cell * height : (cell + 1) * height, :]
        sensors[8 + i * height : 8 + (i + 1) * height, :] = jnp.where(inside > 0.5, value, 0.0)
    if k < ITERS:
        vectors = sensor_vectors(sensors, 8 + height, coeffs.shape[0])
    else:
        vectors = own_vectors(na, nb, sensors, 8 + height)
    result = branch(vectors, w1, b1, w2, b2, w3, b3)
    coeffs[...] = result
    skip = (k - HALO, height) if k < ITERS else (0, na)
    send_means(result, skip[0], na, nb // PER_CELL, skip[1], mean_line, col, cells, payload)


def field_kernel(na, nb, n_row, n_col, cells, gathered, coarse, coeffs, trunk, out, correction, ready, sent):
    steps = ready.shape[0]
    width = trunk.shape[1] // steps
    per = width // TILE
    ky = nb // PER_CELL
    found = corrections(gathered, coarse, n_row, n_col, cells)
    correction[...] = jnp.broadcast_to(found, correction.shape)
    upper = lax.broadcasted_iota(jnp.int32, (8, LANES), 0) < PER_CELL
    adds = {}
    for a in range(0, na, 8):
        for j in range(ky):
            at = a // PER_CELL * ky + j
            adds[a, j] = jnp.where(upper, correction[at : at + 1, :], correction[at + ky : at + ky + 1, :])
    low = low_lanes((8, LANES))
    copies = []
    for step in range(steps):
        values = dot(coeffs[...], trunk[:, step * width : (step + 1) * width])
        for pair in range(nb // 2):
            for a in range(0, na, 8):
                even, odd = (2 * pair * na + a, (2 * pair + 1) * na + a)
                lines = []
                for r in range(0, per, 2):
                    lanes = slice(r * TILE, r * TILE + LANES)
                    x, y = values[even : even + 8, lanes], values[odd : odd + 8, lanes]
                    lines.append(jnp.where(low, x, pltpu.roll(y, TILE, 1)))
                    lines.append(jnp.where(low, pltpu.roll(x, TILE, 1), y))
                block = jnp.stack(lines, axis=0) + adds[a, 2 * pair // PER_CELL][None]
                ready[step, a : a + 8, :, pair * LANES : (pair + 1) * LANES] = jnp.swapaxes(block, 0, 1)
        copies.append(
            pltpu.make_async_copy(ready.at[step], out.at[:, pl.ds(step * per, per), :], sent.at[step])
        )
        copies[-1].start()
    for copy in copies:
        copy.wait()


def body(
    field_start,
    w_sensor,
    bias_sensor,
    w_middle,
    bias_middle,
    w_latent,
    bias_latent,
    trunk_basis,
    coarse_matrix,
):
    rows_here, cols_here = field_start.shape
    n_row, n_col = lax.axis_size("row"), lax.axis_size("col")
    na, nb = rows_here // TILE, cols_here // TILE
    height = na + 2 * HALO
    kx, ky = na // PER_CELL, nb // PER_CELL
    cells = kx * ky
    devices = n_row * n_col
    latent = trunk_basis.shape[0]
    hid = w_sensor.shape[1]
    tile_values, places = 4 * TILE, 8 * TILE
    total = coarse_matrix.shape[1]
    whole = pl.BlockSpec(memory_space=pltpu.VMEM)
    shape = jax.ShapeDtypeStruct
    part = functools.partial

    def shift(x, step):
        return lax.ppermute(x, "row", [(i, (i + step) % n_row) for i in range(n_row)])

    def swap(x, parity):
        pairs = [(i, (i + 1 if i % 2 == parity else i - 1) % n_col) for i in range(n_col)]
        return lax.ppermute(x, "col", pairs)

    def exchange(x):
        return lax.all_to_all(x, ("row", "col"), 0, 0, tiled=True)

    spread_np, order = sensor_layout()
    spread = jnp.asarray(spread_np, BF16)
    half = TILE // 2
    blocks = tuple((int(at), half) for at in order[::half])
    hbm = pl.BlockSpec(memory_space=pltpu.HBM)

    side, inner = shape((nb * HALO, LANES), F32), shape((nb * (na - 2 * HALO), LANES), F32)
    field_rows = field_start.reshape(na, TILE, cols_here)
    up, down, *outer = call(
        part(outer_kernel, nb, ky),
        (shape((8, total), BF16), shape((8, total), BF16), side, side, side, side),
        field_rows[0:HALO],
        field_rows[na - HALO :],
        coarse_matrix,
        scratch=[pltpu.VMEM((8, total), F32)],
    )
    above, below = shift(down, 1), shift(up, -1)
    trunk, mean_trunk, w_first = call(
        part(trunk_kernel, blocks),
        (shape(trunk_basis.shape, BF16), shape((latent, LANES), F32), shape(w_sensor.shape, BF16)),
        trunk_basis,
        w_sensor,
        in_specs=[hbm, whole],
        scratch=[pltpu.SemaphoreType.DMA((4,))],
        flops=1 << 32,
    )
    middle = call(part(extract_tiles, nb), (inner, inner), field_rows[HALO : na - HALO])
    above, below, w_first = lax.optimization_barrier((above, below, w_first))
    mid, first, second = call(
        part(columns_kernel, na, nb, n_row),
        (shape((nb * height, tile_values), BF16), shape((16, total), BF16), shape((16, total), BF16)),
        *outer[:2],
        *middle,
        *outer[2:],
        above,
        below,
        coarse_matrix,
        scratch=[pltpu.VMEM((nb * height, tile_values), F32)] + [pltpu.VMEM((16, total), F32)] * 2,
    )
    second, first = swap(second, 1), swap(first, 0)

    net = (
        w_first,
        bias_sensor.reshape(1, hid),
        w_middle,
        bias_middle.reshape(1, hid),
        w_latent,
        bias_latent.reshape(1, latent),
    )

    sensor_trunk, mean_line = call(
        sensor_trunk_kernel,
        (shape((latent, places), BF16), shape((8, latent), F32)),
        trunk,
        spread,
        mean_trunk,
        flops=1 << 30,
    )
    mid, sensor_trunk = lax.optimization_barrier((mid, sensor_trunk))

    def region(k):
        return (nb + 2 * HALO - 2 * k) * height

    payload_shape = shape((devices, LANES), F32)
    coeffs, payload, coarse = call(
        part(first_kernel, na, nb, n_col, cells),
        (shape((region(1), latent), BF16), payload_shape, shape((8 * (ky + 2), total), F32)),
        mid,
        first,
        second,
        above,
        below,
        coarse_matrix,
        spread,
        *net,
        mean_line,
        scratch=[pltpu.VMEM((region(0) + 16, places), F32), pltpu.VMEM((region(0), tile_values), F32)],
    )
    for k in range(2, ITERS + 1):
        gathered = exchange(payload)
        coeffs, payload = call(
            part(next_kernel, k, na, nb, n_row, n_col, cells),
            (shape((region(k) if k < ITERS else nb * na, latent), BF16), payload_shape),
            gathered,
            coeffs,
            sensor_trunk,
            coarse,
            *net,
            mean_line,
            scratch=[
                pltpu.VMEM((region(k - 1) + 16, places), F32),
                pltpu.VMEM(((ky + 2) * height, places), F32),
            ],
        )
    gathered = exchange(payload)
    steps = 8
    out = call(
        part(field_kernel, na, nb, n_row, n_col, cells),
        shape((na, TILE, cols_here), F32),
        gathered,
        coarse_matrix,
        coeffs,
        trunk,
        out_specs=hbm,
        scratch=[
            pltpu.VMEM((cells, LANES), F32),
            pltpu.VMEM((steps, na, TILE // steps, cols_here), F32),
            pltpu.SemaphoreType.DMA((steps,)),
        ],
    )
    return out.reshape(rows_here, cols_here)


def solution(mesh):
    placed = (P("row", "col"), P(), P(), P(), P(), P(), P(), P(), P(("row", "col"), None))
    return jax.shard_map(
        body, mesh=mesh, in_specs=placed, out_specs=P("row", "col"), check_vma=False
    )
```

```python
import functools

import jax
import jax.numpy as jnp
import numpy as np
from jax import lax
from jax.experimental import pallas as pl
from jax.experimental.pallas import tpu as pltpu
from jax.sharding import PartitionSpec as P

TILE = 64
ITERS = 4
CELL = 256
PER_CELL = CELL // TILE
HALO = ITERS
LANES = 128
F32 = jnp.float32
BF16 = jnp.bfloat16
VMEM_LIMIT = 48 * 1024 * 1024


def dot(a, b, **kw):
    return jnp.dot(a, b, preferred_element_type=F32, **kw)


def nt_dot(a, b):
    return lax.dot_general(a, b, (((1,), (1,)), ((), ())), preferred_element_type=F32)


def low_lanes(shape):
    return lax.broadcasted_iota(jnp.int32, shape, 1) < TILE


def call(kernel, out_shape, *args, grid=(), in_specs=None, out_specs=None, scratch=(), flops=1 << 31, vmem=VMEM_LIMIT):
    whole = pl.BlockSpec(memory_space=pltpu.VMEM)
    specs = {}
    if grid:
        specs["grid"] = grid
    return pl.pallas_call(
        kernel,
        out_shape=out_shape,
        in_specs=in_specs or [whole] * len(args),
        out_specs=out_specs or jax.tree.map(lambda _: whole, out_shape),
        scratch_shapes=list(scratch),
        compiler_params=pltpu.CompilerParams(vmem_limit_bytes=vmem),
        cost_estimate=pl.CostEstimate(flops=flops, bytes_accessed=1 << 20, transcendentals=0),
        **specs,
    )(*args)


def sensor_layout():
    half = TILE // 2
    row31, row32, col31, col32 = (np.arange(TILE) + TILE * i for i in range(4))
    top, bottom, left, right = (np.arange(2 * TILE) + 2 * TILE * i for i in range(4))
    mid = slice(half, half + TILE)
    groups = [
        (row32, top[mid]),
        (row31, bottom[mid]),
        (np.r_[row32[half:], col32[half:]], np.r_[top[:half], left[:half]]),
        (np.r_[row31[half:], col32[:half]], np.r_[bottom[:half], left[-half:]]),
        (np.r_[row32[:half], col31[half:]], np.r_[top[-half:], right[:half]]),
        (np.r_[row31[:half], col31[:half]], np.r_[bottom[-half:], right[-half:]]),
        (col32, left[mid]),
        (col31, right[mid]),
    ]
    source = np.concatenate([g[0] for g in groups])
    order = np.concatenate([g[1] for g in groups])
    spread = np.zeros((4 * TILE, 8 * TILE), np.float32)
    spread[source, np.arange(8 * TILE)] = 1.0
    return spread, order


def extract_tiles(nb, cells, row_part, col_part):
    here, _, cols = cells.shape
    sel_row = lax.broadcasted_iota(jnp.int32, (2 * 16, cols), 0)
    sel_col = lax.broadcasted_iota(jnp.int32, (2 * 16, cols), 1)
    side, b_of = sel_row >> 4, sel_row & 15
    pick = jnp.where(sel_col == b_of * TILE + (TILE // 2 - 1) + side, 1.0, 0.0).astype(BF16)
    low_row, low_col = low_lanes((here, LANES)), low_lanes((16, LANES))
    picked = nt_dot(pick, cells[...].reshape(here * TILE, cols).astype(BF16))
    r31 = cells[:, TILE // 2 - 1, :]
    r32 = cells[:, TILE // 2, :]
    for pair in range(nb // 2):
        lanes = slice(pair * LANES, (pair + 1) * LANES)
        x, y = r31[:, lanes], r32[:, lanes]
        even, odd = 2 * pair * here, (2 * pair + 1) * here
        row_part[even : even + here, :] = jnp.where(low_row, x, pltpu.roll(y, TILE, 1))
        row_part[odd : odd + here, :] = jnp.where(low_row, pltpu.roll(x, TILE, 1), y)
    for pair in range(here // 2):
        lanes = slice(pair * LANES, (pair + 1) * LANES)
        x, y = picked[0:16, lanes], picked[16:32, lanes]
        even = jnp.where(low_col, x, pltpu.roll(y, TILE, 1))
        odd = jnp.where(low_col, pltpu.roll(x, TILE, 1), y)
        col_part[pl.ds(2 * pair, nb, stride=here), :] = even[0:nb]
        col_part[pl.ds(2 * pair + 1, nb, stride=here), :] = odd[0:nb]


def outer_kernel(nb, ky, top, bottom, coarse, up, down, top_rows, top_cols, bottom_rows, bottom_cols, packed):
    packed[...] = jnp.zeros(packed.shape, F32)
    for target, cells, rows, cols, line in (
        (up, top, top_rows, top_cols, 0),
        (down, bottom, bottom_rows, bottom_cols, coarse.shape[0] - ky),
    ):
        extract_tiles(nb, cells, rows, cols)
        for b in range(nb):
            part = slice(b * HALO, (b + 1) * HALO)
            packed[0:HALO, 2 * b * LANES : (2 * b + 1) * LANES] = rows[part, :]
            packed[0:HALO, (2 * b + 1) * LANES : (2 * b + 2) * LANES] = cols[part, :]
        packed[HALO : HALO + ky, :] = coarse[line : line + ky, :]
        target[...] = packed[...].astype(BF16)


def columns_kernel(
    na, nb, n_row, top_rows, top_cols, mid_rows, mid_cols, bottom_rows, bottom_cols, above, below, coarse,
    both, first, second, tall, left, right,
):
    height, values = na + 2 * HALO, 4 * TILE
    kx, ky = na // PER_CELL, nb // PER_CELL
    row, even = lax.axis_index("row"), lax.axis_index("col") % 2 == 0
    over = jnp.where(row == 0, 0.0, above[...].astype(F32))
    under = jnp.where(row == n_row - 1, 0.0, below[...].astype(F32))
    for b in range(nb):
        at = b * height
        tall[at : at + HALO, :] = over[0:HALO, b * values : (b + 1) * values]
        to = at + HALO
        for rows, cols in ((top_rows, top_cols), (mid_rows, mid_cols), (bottom_rows, bottom_cols)):
            size = rows.shape[0] // nb
            tall[to : to + size, 0:LANES] = rows[b * size : (b + 1) * size, :]
            tall[to : to + size, LANES : 2 * LANES] = cols[b * size : (b + 1) * size, :]
            to += size
        tall[at + HALO + na : at + height, :] = under[0:HALO, b * values : (b + 1) * values]
    both[...] = tall[...].astype(BF16)
    for packed, start, j in ((left, 0, 0), (right, nb - HALO, ky - 1)):
        packed[...] = jnp.zeros(packed.shape, F32)
        for b in range(HALO):
            for g in range(height // 8):
                lanes = slice((b * (height // 8) + g) * values, (b * (height // 8) + g + 1) * values)
                at = (start + b) * height + 8 * g
                packed[0:8, lanes] = tall[at : at + 8, :]
        packed[8:9, :] = over[HALO + j : HALO + j + 1, :]
        for i in range(kx):
            packed[9 + i : 10 + i, :] = coarse[i * ky + j : i * ky + j + 1, :]
        packed[9 + kx : 10 + kx, :] = under[HALO + j : HALO + j + 1, :]
    first[...] = jnp.where(even, right[...], left[...]).astype(BF16)
    second[...] = jnp.where(even, left[...], right[...]).astype(BF16)


def trunk_kernel(blocks, trunk_hbm, w_sensor, trunk, mean_trunk, w_out, arrived):
    steps = arrived.shape[0]
    depth = trunk.shape[0] // steps
    copies = [
        pltpu.make_async_copy(trunk_hbm.at[pl.ds(i * depth, depth)], trunk.at[pl.ds(i * depth, depth)], arrived.at[i])
        for i in range(steps)
    ]
    for copy in copies:
        copy.start()
    at = 0
    for start, size in blocks:
        w_out[at : at + size, :] = w_sensor[start : start + size, :]
        at += size
    share = jnp.full((trunk.shape[1], LANES), 1.0 / (TILE * TILE), BF16)
    for i, copy in enumerate(copies):
        copy.wait()
        rows = slice(i * depth, (i + 1) * depth)
        mean_trunk[rows, :] = dot(trunk[rows, :], share)


def three_parts(line):
    high = line.astype(BF16).astype(F32)
    middle = (line - high).astype(BF16).astype(F32)
    low = line - high - middle
    at = lax.broadcasted_iota(jnp.int32, (16, line.shape[1]), 0)
    parts = jnp.where(at == 0, high, jnp.where(at == 1, middle, jnp.where(at == 2, low, 0.0)))
    return parts.astype(BF16)


def sensor_trunk_kernel(trunk, spread, mean_trunk, w3, b3, w_sensors, b_sensors, mean_line, mean_bias):
    mean = jnp.transpose(mean_trunk[...])[0:8, :]
    line = jnp.sum(nt_dot(three_parts(mean[0:1, :]), w3[...]), axis=0, keepdims=True)
    mean_line[...] = jnp.broadcast_to(line, mean_line.shape)
    mean_bias[...] = jnp.broadcast_to(jnp.sum(mean * b3[...], axis=1, keepdims=True), mean_bias.shape)
    width = 1024
    per = width // TILE
    point = lax.broadcasted_iota(jnp.int32, (width, LANES), 0)
    lane = lax.broadcasted_iota(jnp.int32, (width, LANES), 1)
    column = (point & (TILE - 1)) == TILE // 2 - 1 + (lane >> 6)
    away = jnp.where(column, (lane & (TILE - 1)) - (point >> 6), -1)
    total = None
    for step in range(trunk.shape[1] // width):
        pick = jnp.where(away == step * per, 1.0, 0.0).astype(BF16)
        part = dot(trunk[:, step * width : (step + 1) * width], pick)
        total = part if total is None else total + part
    middle = trunk.shape[1] // 2
    row31 = pltpu.roll(trunk[:, middle - LANES : middle].astype(F32), TILE, 1)
    row32 = pltpu.roll(trunk[:, middle : middle + LANES].astype(F32), TILE, 1)
    rows = jnp.where(low_lanes(row31.shape), row31, row32)
    unique = jnp.concatenate([rows, total], axis=1).astype(BF16)
    columns = dot(unique, spread[...]).astype(BF16)
    both = dot(jnp.concatenate([w3[...], three_parts(b3[...])], axis=0), columns)
    depth = w_sensors.shape[0]
    w_sensors[...] = both[0:depth, :].astype(BF16)
    b_sensors[...] = jnp.broadcast_to(jnp.sum(both[depth:, :], axis=0, keepdims=True), b_sensors.shape)


def sensor_vectors(sensors, base, count):
    height = HALO * 2 + 16
    low = low_lanes((count, LANES))

    def part(shift, group):
        return sensors[base + shift : base + shift + count, group * LANES : (group + 1) * LANES]

    parts = [
        jnp.where(low, part(-1, 0), part(1, 0)),
        jnp.where(low, part(-height - 1, 1), part(-height + 1, 1)),
        jnp.where(low, part(height - 1, 2), part(height + 1, 2)),
        jnp.where(low, part(-height, 3), part(height, 3)),
    ]
    return jnp.concatenate([p.astype(BF16) for p in parts], axis=1)


def hidden_two(vectors, w1, b1, w2, b2):
    hidden = jnp.tanh(dot(vectors, w1[...]) + b1[...]).astype(BF16)
    return jnp.tanh(dot(hidden, w2[...]) + b2[...]).astype(BF16)


def send_means(hidden, columns, na, ky, height, mean_line, mean_bias, col, cells, payload):
    skip = (height - na) // 2
    share = mean_line[0:1, :] * (1.0 / PER_CELL**2)
    lane = lax.broadcasted_iota(jnp.int32, (height, LANES), 1)
    line = lax.broadcasted_iota(jnp.int32, (height, LANES), 0) - skip
    inside = (line >= 0) & (line < na)
    place = jnp.where(inside, (line >> 2) * ky, -LANES)
    total = None
    for j in range(ky):
        tiles = None
        for b in range(PER_CELL * j, PER_CELL * (j + 1)):
            at = (b - columns) * height
            part = hidden[at : at + height, :].astype(F32)
            tiles = part if tiles is None else tiles + part
        sums = jnp.sum(tiles * share, axis=1, keepdims=True) + mean_bias[0:1, 0:1] * (1.0 / PER_CELL)
        mine = ((lane - cells * col) & (LANES - 1)) == place + j
        part = jnp.where(mine, sums, 0.0)
        total = part if total is None else total + part
    payload[...] = jnp.broadcast_to(jnp.sum(total, axis=0, keepdims=True), payload.shape)


def corrections(gathered, coarse, n_row, n_col, cells):
    blocks = n_col * cells // LANES
    lane = lax.broadcasted_iota(jnp.int32, (n_col, LANES), 1)
    source = cells * lax.broadcasted_iota(jnp.int32, (n_col, LANES), 0)
    block = (source + ((lane - source) & (LANES - 1))) // LANES
    total = None
    for r in range(n_row):
        values = gathered[r * n_col : (r + 1) * n_col, :]
        for k in range(blocks):
            line = jnp.sum(jnp.where(block == k, values, 0.0), axis=0, keepdims=True)
            at = (r * blocks + k) * LANES
            term = coarse[:, at : at + LANES] * line
            total = term if total is None else total + term
    return jnp.sum(total, axis=1, keepdims=True)


def own_vectors(na, nb, sensors, base):
    height = na + 2 * HALO
    return jnp.concatenate(
        [sensor_vectors(sensors, base + b * height + HALO, na) for b in range(nb)], axis=0
    )


def zero_ends(sensors):
    rows = sensors.shape[0]
    sensors[0:8, :] = jnp.zeros((8, sensors.shape[1]), F32)
    sensors[rows - 8 : rows, :] = jnp.zeros((8, sensors.shape[1]), F32)


def first_kernel(
    na, nb, n_col, cells, mid, first, second, above, below, c_own, spread, w1, b1, w2, b2, mean_line, mean_bias,
    hidden, payload, coarse, sensors, tiles,
):
    height, values = na + 2 * HALO, 4 * TILE
    side = HALO * height
    wide = nb * height
    tiles[side : side + wide, :] = mid[...].astype(F32)
    col = lax.axis_index("col")
    even = col % 2 == 0
    one, other = first[...].astype(F32), second[...].astype(F32)
    left = jnp.where(col == 0, 0.0, jnp.where(even, other, one))
    right = jnp.where(col == n_col - 1, 0.0, jnp.where(even, one, other))
    edge = [above[...].astype(F32), below[...].astype(F32), left, right]
    for lines, start in ((left, 0), (right, side + wide)):
        for g in range(side // 8):
            tiles[start + 8 * g : start + 8 * (g + 1), :] = lines[0:8, g * values : (g + 1) * values]
    zero_ends(sensors)
    sensors[8 : 8 + 2 * side + wide, :] = dot(tiles[...].astype(BF16), spread[...])
    vectors = sensor_vectors(sensors, 8 + height, hidden.shape[0])
    result = hidden_two(vectors, w1, b1, w2, b2)
    hidden[...] = result
    send_means(result, 1 - HALO, na, nb // PER_CELL, height, mean_line, mean_bias, col, cells, payload)
    kx, ky = na // PER_CELL, nb // PER_CELL
    coarse[0 : kx + 2, :] = edge[2][8 : 10 + kx, :]
    coarse[8 * (ky + 1) : 8 * (ky + 1) + kx + 2, :] = edge[3][8 : 10 + kx, :]
    for j in range(ky):
        at = 8 * (j + 1)
        coarse[at : at + 1, :] = edge[0][HALO + j : HALO + j + 1, :]
        for i in range(kx):
            coarse[at + 1 + i : at + 2 + i, :] = c_own[i * ky + j : i * ky + j + 1, :]
        coarse[at + 1 + kx : at + 2 + kx, :] = edge[1][HALO + j : HALO + j + 1, :]
    for j in range(ky + 2):
        at = 8 * j + kx + 2
        coarse[at : 8 * (j + 1), :] = jnp.zeros((6 - kx, coarse.shape[1]), F32)


def next_kernel(
    k, na, nb, n_row, n_col, cells, gathered, before, w_sensors, b_sensors, coarse, w1, b1, w2, b2, mean_line,
    mean_bias, w3, b3, result, payload, sensors, lines,
):
    height = na + 2 * HALO
    predicted = dot(before[...], w_sensors[...]) + b_sensors[0:1, :]
    found = corrections(gathered, coarse, n_row, n_col, cells)
    found = jnp.broadcast_to(found, (found.shape[0], sensors.shape[1]))
    row, col = lax.axis_index("row"), lax.axis_index("col")
    a_at = row * na - HALO + lax.broadcasted_iota(jnp.int32, (height, 1), 0)
    a_ok = (a_at >= 0) & (a_at < n_row * na)
    for j in range(nb // PER_CELL + 2):
        for i in range(height // PER_CELL):
            at = j * height + i * PER_CELL
            lines[at : at + PER_CELL, :] = jnp.broadcast_to(
                found[8 * j + i : 8 * j + i + 1, :], (PER_CELL, found.shape[1])
            )
    zero_ends(sensors)
    first = k - 1
    have = nb + 2 * HALO - 2 * first
    for i in range(have):
        b = first + i
        b_at = col * nb - HALO + b
        inside = jnp.where(a_ok & (b_at >= 0) & (b_at < n_col * nb), 1.0, 0.0)
        cell = b // PER_CELL
        value = predicted[i * height : (i + 1) * height, :] + lines[cell * height : (cell + 1) * height, :]
        sensors[8 + i * height : 8 + (i + 1) * height, :] = jnp.where(inside > 0.5, value, 0.0)
    if k < ITERS:
        vectors = sensor_vectors(sensors, 8 + height, result.shape[0])
    else:
        vectors = own_vectors(na, nb, sensors, 8 + height)
    hidden = hidden_two(vectors, w1, b1, w2, b2)
    if k < ITERS:
        result[...] = hidden
    else:
        result[...] = (dot(hidden, w3[...]) + b3[...]).astype(BF16)
    skip = (k - HALO, height) if k < ITERS else (0, na)
    send_means(hidden, skip[0], na, nb // PER_CELL, skip[1], mean_line, mean_bias, col, cells, payload)


def field_kernel(na, nb, n_row, n_col, cells, gathered, coarse, coeffs, trunk, out, correction, ready, sent):
    steps = ready.shape[0]
    width = trunk.shape[1] // steps
    per = width // TILE
    ky = nb // PER_CELL
    found = corrections(gathered, coarse, n_row, n_col, cells)
    correction[...] = jnp.broadcast_to(found, correction.shape)
    upper = lax.broadcasted_iota(jnp.int32, (8, LANES), 0) < PER_CELL
    adds = {}
    for a in range(0, na, 8):
        for j in range(ky):
            at = a // PER_CELL * ky + j
            adds[a, j] = jnp.where(upper, correction[at : at + 1, :], correction[at + ky : at + ky + 1, :])
    low = low_lanes((8, LANES))
    copies = []
    for step in range(steps):
        values = dot(coeffs[...], trunk[:, step * width : (step + 1) * width])
        for pair in range(nb // 2):
            for a in range(0, na, 8):
                even, odd = (2 * pair * na + a, (2 * pair + 1) * na + a)
                lines = []
                for r in range(0, per, 2):
                    lanes = slice(r * TILE, r * TILE + LANES)
                    x, y = values[even : even + 8, lanes], values[odd : odd + 8, lanes]
                    lines.append(jnp.where(low, x, pltpu.roll(y, TILE, 1)))
                    lines.append(jnp.where(low, pltpu.roll(x, TILE, 1), y))
                block = jnp.stack(lines, axis=0) + adds[a, 2 * pair // PER_CELL][None]
                ready[step, a : a + 8, :, pair * LANES : (pair + 1) * LANES] = jnp.swapaxes(block, 0, 1)
        copies.append(
            pltpu.make_async_copy(ready.at[step], out.at[:, pl.ds(step * per, per), :], sent.at[step])
        )
        copies[-1].start()
    for copy in copies:
        copy.wait()


def body(
    field_start,
    w_sensor,
    bias_sensor,
    w_middle,
    bias_middle,
    w_latent,
    bias_latent,
    trunk_basis,
    coarse_matrix,
):
    rows_here, cols_here = field_start.shape
    n_row, n_col = lax.axis_size("row"), lax.axis_size("col")
    na, nb = rows_here // TILE, cols_here // TILE
    height = na + 2 * HALO
    kx, ky = na // PER_CELL, nb // PER_CELL
    cells = kx * ky
    devices = n_row * n_col
    latent = trunk_basis.shape[0]
    hid = w_sensor.shape[1]
    tile_values, places = 4 * TILE, 8 * TILE
    total = coarse_matrix.shape[1]
    whole = pl.BlockSpec(memory_space=pltpu.VMEM)
    shape = jax.ShapeDtypeStruct
    part = functools.partial

    def shift(x, step):
        return lax.ppermute(x, "row", [(i, (i + step) % n_row) for i in range(n_row)])

    def swap(x, parity):
        pairs = [(i, (i + 1 if i % 2 == parity else i - 1) % n_col) for i in range(n_col)]
        return lax.ppermute(x, "col", pairs)

    def exchange(x):
        return lax.all_to_all(x, ("row", "col"), 0, 0, tiled=True)

    spread_np, order = sensor_layout()
    spread = jnp.asarray(spread_np, BF16)
    half = TILE // 2
    blocks = tuple((int(at), half) for at in order[::half])
    hbm = pl.BlockSpec(memory_space=pltpu.HBM)

    side, inner = shape((nb * HALO, LANES), F32), shape((nb * (na - 2 * HALO), LANES), F32)
    field_rows = field_start.reshape(na, TILE, cols_here)
    up, down, *outer = call(
        part(outer_kernel, nb, ky),
        (shape((8, total), BF16), shape((8, total), BF16), side, side, side, side),
        field_rows[0:HALO],
        field_rows[na - HALO :],
        coarse_matrix,
        scratch=[pltpu.VMEM((8, total), F32)],
    )
    above, below = shift(down, 1), shift(up, -1)
    trunk, mean_trunk, w_first = call(
        part(trunk_kernel, blocks),
        (shape(trunk_basis.shape, BF16), shape((latent, LANES), F32), shape(w_sensor.shape, BF16)),
        trunk_basis,
        w_sensor,
        in_specs=[hbm, whole],
        scratch=[pltpu.SemaphoreType.DMA((4,))],
        flops=1 << 32,
    )
    middle = call(part(extract_tiles, nb), (inner, inner), field_rows[HALO : na - HALO])
    above, below, w_first = lax.optimization_barrier((above, below, w_first))
    mid, first, second = call(
        part(columns_kernel, na, nb, n_row),
        (shape((nb * height, tile_values), BF16), shape((16, total), BF16), shape((16, total), BF16)),
        *outer[:2],
        *middle,
        *outer[2:],
        above,
        below,
        coarse_matrix,
        scratch=[pltpu.VMEM((nb * height, tile_values), F32)] + [pltpu.VMEM((16, total), F32)] * 2,
    )
    second, first = swap(second, 1), swap(first, 0)

    net = (
        w_first,
        bias_sensor.reshape(1, hid),
        w_middle,
        bias_middle.reshape(1, hid),
    )

    b_latent = bias_latent.reshape(1, latent)
    w_sensors, b_sensors, mean_line, mean_bias = call(
        sensor_trunk_kernel,
        (
            shape((hid, places), BF16),
            shape((8, places), F32),
            shape((8, hid), F32),
            shape((8, LANES), F32),
        ),
        trunk,
        spread,
        mean_trunk,
        w_latent,
        b_latent,
        flops=1 << 30,
    )
    mid, w_sensors = lax.optimization_barrier((mid, w_sensors))

    def region(k):
        return (nb + 2 * HALO - 2 * k) * height

    payload_shape = shape((devices, LANES), F32)
    coeffs, payload, coarse = call(
        part(first_kernel, na, nb, n_col, cells),
        (shape((region(1), hid), BF16), payload_shape, shape((8 * (ky + 2), total), F32)),
        mid,
        first,
        second,
        above,
        below,
        coarse_matrix,
        spread,
        *net,
        mean_line,
        mean_bias,
        scratch=[pltpu.VMEM((region(0) + 16, places), F32), pltpu.VMEM((region(0), tile_values), F32)],
    )
    for k in range(2, ITERS + 1):
        gathered = exchange(payload)
        coeffs, payload = call(
            part(next_kernel, k, na, nb, n_row, n_col, cells),
            (shape((region(k) if k < ITERS else nb * na, hid if k < ITERS else latent), BF16), payload_shape),
            gathered,
            coeffs,
            w_sensors,
            b_sensors,
            coarse,
            *net,
            mean_line,
            mean_bias,
            w_latent,
            b_latent,
            scratch=[
                pltpu.VMEM((region(k - 1) + 16, places), F32),
                pltpu.VMEM(((ky + 2) * height, places), F32),
            ],
        )
    gathered = exchange(payload)
    steps = 8
    out = call(
        part(field_kernel, na, nb, n_row, n_col, cells),
        shape((na, TILE, cols_here), F32),
        gathered,
        coarse_matrix,
        coeffs,
        trunk,
        out_specs=hbm,
        scratch=[
            pltpu.VMEM((cells, LANES), F32),
            pltpu.VMEM((steps, na, TILE // steps, cols_here), F32),
            pltpu.SemaphoreType.DMA((steps,)),
        ],
    )
    return out.reshape(rows_here, cols_here)


def solution(mesh):
    placed = (P("row", "col"), P(), P(), P(), P(), P(), P(), P(), P(("row", "col"), None))
    return jax.shard_map(
        body, mesh=mesh, in_specs=placed, out_specs=P("row", "col"), check_vma=False
    )
```

```python
import functools

import jax
import jax.numpy as jnp
import numpy as np
from jax import lax
from jax.experimental import pallas as pl
from jax.experimental.pallas import tpu as pltpu
from jax.sharding import PartitionSpec as P

TILE = 64
ITERS = 4
CELL = 256
PER_CELL = CELL // TILE
HALO = ITERS
LANES = 128
F32 = jnp.float32
BF16 = jnp.bfloat16
VMEM_LIMIT = 48 * 1024 * 1024


def dot(a, b, **kw):
    return jnp.dot(a, b, preferred_element_type=F32, **kw)


def nt_dot(a, b):
    return lax.dot_general(a, b, (((1,), (1,)), ((), ())), preferred_element_type=F32)


def low_lanes(shape):
    return lax.broadcasted_iota(jnp.int32, shape, 1) < TILE


def call(kernel, out_shape, *args, grid=(), in_specs=None, out_specs=None, scratch=(), flops=1 << 31, vmem=VMEM_LIMIT):
    whole = pl.BlockSpec(memory_space=pltpu.VMEM)
    specs = {}
    if grid:
        specs["grid"] = grid
    return pl.pallas_call(
        kernel,
        out_shape=out_shape,
        in_specs=in_specs or [whole] * len(args),
        out_specs=out_specs or jax.tree.map(lambda _: whole, out_shape),
        scratch_shapes=list(scratch),
        compiler_params=pltpu.CompilerParams(vmem_limit_bytes=vmem),
        cost_estimate=pl.CostEstimate(flops=flops, bytes_accessed=1 << 20, transcendentals=0),
        **specs,
    )(*args)


def sensor_layout():
    half = TILE // 2
    row31, row32, col31, col32 = (np.arange(TILE) + TILE * i for i in range(4))
    top, bottom, left, right = (np.arange(2 * TILE) + 2 * TILE * i for i in range(4))
    mid = slice(half, half + TILE)
    groups = [
        (row32, top[mid]),
        (row31, bottom[mid]),
        (np.r_[row32[half:], col32[half:]], np.r_[top[:half], left[:half]]),
        (np.r_[row31[half:], col32[:half]], np.r_[bottom[:half], left[-half:]]),
        (np.r_[row32[:half], col31[half:]], np.r_[top[-half:], right[:half]]),
        (np.r_[row31[:half], col31[:half]], np.r_[bottom[-half:], right[-half:]]),
        (col32, left[mid]),
        (col31, right[mid]),
    ]
    source = np.concatenate([g[0] for g in groups])
    order = np.concatenate([g[1] for g in groups])
    spread = np.zeros((4 * TILE, 8 * TILE), np.float32)
    spread[source, np.arange(8 * TILE)] = 1.0
    return spread, order


def extract_tiles(nb, cells, row_part, col_part):
    here, _, cols = cells.shape
    sel_row = lax.broadcasted_iota(jnp.int32, (2 * 16, cols), 0)
    sel_col = lax.broadcasted_iota(jnp.int32, (2 * 16, cols), 1)
    side, b_of = sel_row >> 4, sel_row & 15
    pick = jnp.where(sel_col == b_of * TILE + (TILE // 2 - 1) + side, 1.0, 0.0).astype(BF16)
    low_row, low_col = low_lanes((here, LANES)), low_lanes((16, LANES))
    picked = nt_dot(pick, cells[...].reshape(here * TILE, cols).astype(BF16))
    r31 = cells[:, TILE // 2 - 1, :]
    r32 = cells[:, TILE // 2, :]
    for pair in range(nb // 2):
        lanes = slice(pair * LANES, (pair + 1) * LANES)
        x, y = r31[:, lanes], r32[:, lanes]
        even, odd = 2 * pair * here, (2 * pair + 1) * here
        row_part[even : even + here, :] = jnp.where(low_row, x, pltpu.roll(y, TILE, 1))
        row_part[odd : odd + here, :] = jnp.where(low_row, pltpu.roll(x, TILE, 1), y)
    for pair in range(here // 2):
        lanes = slice(pair * LANES, (pair + 1) * LANES)
        x, y = picked[0:16, lanes], picked[16:32, lanes]
        even = jnp.where(low_col, x, pltpu.roll(y, TILE, 1))
        odd = jnp.where(low_col, pltpu.roll(x, TILE, 1), y)
        col_part[pl.ds(2 * pair, nb, stride=here), :] = even[0:nb]
        col_part[pl.ds(2 * pair + 1, nb, stride=here), :] = odd[0:nb]


def outer_kernel(nb, ky, top, bottom, coarse, up, down, top_rows, top_cols, bottom_rows, bottom_cols, packed):
    packed[...] = jnp.zeros(packed.shape, F32)
    for target, cells, rows, cols, line in (
        (up, top, top_rows, top_cols, 0),
        (down, bottom, bottom_rows, bottom_cols, coarse.shape[0] - ky),
    ):
        extract_tiles(nb, cells, rows, cols)
        for b in range(nb):
            part = slice(b * HALO, (b + 1) * HALO)
            packed[0:HALO, 2 * b * LANES : (2 * b + 1) * LANES] = rows[part, :]
            packed[0:HALO, (2 * b + 1) * LANES : (2 * b + 2) * LANES] = cols[part, :]
        packed[HALO : HALO + ky, :] = coarse[line : line + ky, :]
        target[...] = packed[...].astype(BF16)


def columns_kernel(
    na, nb, n_row, top_rows, top_cols, mid_rows, mid_cols, bottom_rows, bottom_cols, above, below, coarse,
    both, first, second, tall, left, right,
):
    height, values = na + 2 * HALO, 4 * TILE
    kx, ky = na // PER_CELL, nb // PER_CELL
    row, even = lax.axis_index("row"), lax.axis_index("col") % 2 == 0
    over = jnp.where(row == 0, 0.0, above[...].astype(F32))
    under = jnp.where(row == n_row - 1, 0.0, below[...].astype(F32))
    for b in range(nb):
        at = b * height
        tall[at : at + HALO, :] = over[0:HALO, b * values : (b + 1) * values]
        to = at + HALO
        for rows, cols in ((top_rows, top_cols), (mid_rows, mid_cols), (bottom_rows, bottom_cols)):
            size = rows.shape[0] // nb
            tall[to : to + size, 0:LANES] = rows[b * size : (b + 1) * size, :]
            tall[to : to + size, LANES : 2 * LANES] = cols[b * size : (b + 1) * size, :]
            to += size
        tall[at + HALO + na : at + height, :] = under[0:HALO, b * values : (b + 1) * values]
    both[...] = tall[...].astype(BF16)
    for packed, start, j in ((left, 0, 0), (right, nb - HALO, ky - 1)):
        packed[...] = jnp.zeros(packed.shape, F32)
        for b in range(HALO):
            for g in range(height // 8):
                lanes = slice((b * (height // 8) + g) * values, (b * (height // 8) + g + 1) * values)
                at = (start + b) * height + 8 * g
                packed[0:8, lanes] = tall[at : at + 8, :]
        packed[8:9, :] = over[HALO + j : HALO + j + 1, :]
        for i in range(kx):
            packed[9 + i : 10 + i, :] = coarse[i * ky + j : i * ky + j + 1, :]
        packed[9 + kx : 10 + kx, :] = under[HALO + j : HALO + j + 1, :]
    first[...] = jnp.where(even, right[...], left[...]).astype(BF16)
    second[...] = jnp.where(even, left[...], right[...]).astype(BF16)


def trunk_kernel(blocks, trunk_hbm, w_sensor, trunk, mean_trunk, w_out, arrived):
    steps = arrived.shape[0]
    depth = trunk.shape[0] // steps
    copies = [
        pltpu.make_async_copy(trunk_hbm.at[pl.ds(i * depth, depth)], trunk.at[pl.ds(i * depth, depth)], arrived.at[i])
        for i in range(steps)
    ]
    for copy in copies:
        copy.start()
    at = 0
    for start, size in blocks:
        w_out[at : at + size, :] = w_sensor[start : start + size, :]
        at += size
    share = jnp.full((trunk.shape[1], LANES), 1.0 / (TILE * TILE), BF16)
    for i, copy in enumerate(copies):
        copy.wait()
        rows = slice(i * depth, (i + 1) * depth)
        mean_trunk[rows, :] = dot(trunk[rows, :], share)


def three_parts(line):
    high = line.astype(BF16).astype(F32)
    middle = (line - high).astype(BF16).astype(F32)
    low = line - high - middle
    at = lax.broadcasted_iota(jnp.int32, (16, line.shape[1]), 0)
    parts = jnp.where(at == 0, high, jnp.where(at == 1, middle, jnp.where(at == 2, low, 0.0)))
    return parts.astype(BF16)


def sensor_trunk_kernel(trunk, spread, mean_trunk, w3, b3, w_sensors, b_sensors, mean_line, mean_bias):
    mean = jnp.transpose(mean_trunk[...])[0:8, :]
    line = jnp.sum(nt_dot(three_parts(mean[0:1, :]), w3[...]), axis=0, keepdims=True)
    mean_line[...] = jnp.broadcast_to(line, mean_line.shape)
    mean_bias[...] = jnp.broadcast_to(jnp.sum(mean * b3[...], axis=1, keepdims=True), mean_bias.shape)
    width = 1024
    per = width // TILE
    point = lax.broadcasted_iota(jnp.int32, (width, LANES), 0)
    lane = lax.broadcasted_iota(jnp.int32, (width, LANES), 1)
    column = (point & (TILE - 1)) == TILE // 2 - 1 + (lane >> 6)
    away = jnp.where(column, (lane & (TILE - 1)) - (point >> 6), -1)
    total = None
    for step in range(trunk.shape[1] // width):
        pick = jnp.where(away == step * per, 1.0, 0.0).astype(BF16)
        part = dot(trunk[:, step * width : (step + 1) * width], pick)
        total = part if total is None else total + part
    middle = trunk.shape[1] // 2
    row31 = pltpu.roll(trunk[:, middle - LANES : middle].astype(F32), TILE, 1)
    row32 = pltpu.roll(trunk[:, middle : middle + LANES].astype(F32), TILE, 1)
    rows = jnp.where(low_lanes(row31.shape), row31, row32)
    unique = jnp.concatenate([rows, total], axis=1).astype(BF16)
    columns = dot(unique, spread[...]).astype(BF16)
    both = dot(jnp.concatenate([w3[...], three_parts(b3[...])], axis=0), columns)
    depth = w_sensors.shape[0]
    w_sensors[...] = both[0:depth, :].astype(BF16)
    b_sensors[...] = jnp.broadcast_to(jnp.sum(both[depth:, :], axis=0, keepdims=True), b_sensors.shape)


def sensor_vectors(sensors, base, count):
    height = HALO * 2 + 16
    low = low_lanes((count, LANES))

    def part(shift, group):
        return sensors[base + shift : base + shift + count, group * LANES : (group + 1) * LANES]

    parts = [
        jnp.where(low, part(-1, 0), part(1, 0)),
        jnp.where(low, part(-height - 1, 1), part(-height + 1, 1)),
        jnp.where(low, part(height - 1, 2), part(height + 1, 2)),
        jnp.where(low, part(-height, 3), part(height, 3)),
    ]
    return jnp.concatenate([p.astype(BF16) for p in parts], axis=1)


def hidden_two(vectors, w1, b1, w2, b2):
    hidden = jnp.tanh(dot(vectors, w1[...]) + b1[...]).astype(BF16)
    return jnp.tanh(dot(hidden, w2[...]) + b2[...]).astype(BF16)


def send_means(hidden, columns, na, ky, height, mean_line, mean_bias, col, cells, payload):
    skip = (height - na) // 2
    share = mean_line[0:1, :] * (1.0 / PER_CELL**2)
    lane = lax.broadcasted_iota(jnp.int32, (height, LANES), 1)
    line = lax.broadcasted_iota(jnp.int32, (height, LANES), 0) - skip
    inside = (line >= 0) & (line < na)
    place = jnp.where(inside, (line >> 2) * ky, -LANES)
    total = None
    for j in range(ky):
        tiles = None
        for b in range(PER_CELL * j, PER_CELL * (j + 1)):
            at = (b - columns) * height
            part = hidden[at : at + height, :].astype(F32)
            tiles = part if tiles is None else tiles + part
        sums = jnp.sum(tiles * share, axis=1, keepdims=True) + mean_bias[0:1, 0:1] * (1.0 / PER_CELL)
        mine = ((lane - cells * col) & (LANES - 1)) == place + j
        part = jnp.where(mine, sums, 0.0)
        total = part if total is None else total + part
    payload[...] = jnp.broadcast_to(jnp.sum(total, axis=0, keepdims=True), payload.shape)


def corrections(gathered, coarse, n_row, n_col, cells):
    blocks = n_col * cells // LANES
    lane = lax.broadcasted_iota(jnp.int32, (n_col, LANES), 1)
    source = cells * lax.broadcasted_iota(jnp.int32, (n_col, LANES), 0)
    block = (source + ((lane - source) & (LANES - 1))) // LANES
    total = None
    for r in range(n_row):
        values = gathered[r * n_col : (r + 1) * n_col, :]
        for k in range(blocks):
            line = jnp.sum(jnp.where(block == k, values, 0.0), axis=0, keepdims=True)
            at = (r * blocks + k) * LANES
            term = coarse[:, at : at + LANES] * line
            total = term if total is None else total + term
    return jnp.sum(total, axis=1, keepdims=True)


def own_vectors(na, nb, sensors, base):
    height = na + 2 * HALO
    return jnp.concatenate(
        [sensor_vectors(sensors, base + b * height + HALO, na) for b in range(nb)], axis=0
    )


def zero_ends(sensors):
    rows = sensors.shape[0]
    sensors[0:8, :] = jnp.zeros((8, sensors.shape[1]), F32)
    sensors[rows - 8 : rows, :] = jnp.zeros((8, sensors.shape[1]), F32)


def first_kernel(
    na, nb, n_col, cells, mid, first, second, above, below, c_own, spread, w1, b1, w2, b2, mean_line, mean_bias,
    hidden, payload, coarse, sensors, tiles,
):
    height, values = na + 2 * HALO, 4 * TILE
    side = HALO * height
    wide = nb * height
    tiles[side : side + wide, :] = mid[...].astype(F32)
    col = lax.axis_index("col")
    even = col % 2 == 0
    one, other = first[...].astype(F32), second[...].astype(F32)
    left = jnp.where(col == 0, 0.0, jnp.where(even, other, one))
    right = jnp.where(col == n_col - 1, 0.0, jnp.where(even, one, other))
    edge = [above[...].astype(F32), below[...].astype(F32), left, right]
    for lines, start in ((left, 0), (right, side + wide)):
        for g in range(side // 8):
            tiles[start + 8 * g : start + 8 * (g + 1), :] = lines[0:8, g * values : (g + 1) * values]
    zero_ends(sensors)
    sensors[8 : 8 + 2 * side + wide, :] = dot(tiles[...].astype(BF16), spread[...])
    vectors = sensor_vectors(sensors, 8 + height, hidden.shape[0])
    result = hidden_two(vectors, w1, b1, w2, b2)
    hidden[...] = result
    send_means(result, 1 - HALO, na, nb // PER_CELL, height, mean_line, mean_bias, col, cells, payload)
    kx, ky = na // PER_CELL, nb // PER_CELL
    coarse[0 : kx + 2, :] = edge[2][8 : 10 + kx, :]
    coarse[8 * (ky + 1) : 8 * (ky + 1) + kx + 2, :] = edge[3][8 : 10 + kx, :]
    for j in range(ky):
        at = 8 * (j + 1)
        coarse[at : at + 1, :] = edge[0][HALO + j : HALO + j + 1, :]
        for i in range(kx):
            coarse[at + 1 + i : at + 2 + i, :] = c_own[i * ky + j : i * ky + j + 1, :]
        coarse[at + 1 + kx : at + 2 + kx, :] = edge[1][HALO + j : HALO + j + 1, :]
    for j in range(ky + 2):
        at = 8 * j + kx + 2
        coarse[at : 8 * (j + 1), :] = jnp.zeros((6 - kx, coarse.shape[1]), F32)


def next_kernel(
    k, na, nb, n_row, n_col, cells, gathered, before, w_sensors, b_sensors, coarse, w1, b1, w2, b2, mean_line,
    mean_bias, w3, b3, result, payload, sensors, lines,
):
    height = na + 2 * HALO
    predicted = dot(before[...], w_sensors[...]) + b_sensors[0:1, :]
    found = corrections(gathered, coarse, n_row, n_col, cells)
    found = jnp.broadcast_to(found, (found.shape[0], LANES))
    row, col = lax.axis_index("row"), lax.axis_index("col")
    a_at = row * na - HALO + lax.broadcasted_iota(jnp.int32, (height, 1), 0)
    a_ok = (a_at >= 0) & (a_at < n_row * na)
    for j in range(nb // PER_CELL + 2):
        for i in range(height // PER_CELL):
            at = j * height + i * PER_CELL
            lines[at : at + PER_CELL, :] = jnp.broadcast_to(
                found[8 * j + i : 8 * j + i + 1, :], (PER_CELL, found.shape[1])
            )
    zero_ends(sensors)
    first = k - 1
    have = nb + 2 * HALO - 2 * first
    for i in range(have):
        b = first + i
        b_at = col * nb - HALO + b
        inside = jnp.where(a_ok & (b_at >= 0) & (b_at < n_col * nb), 1.0, 0.0)
        cell = b // PER_CELL
        add = lines[cell * height : (cell + 1) * height, :]
        value = predicted[i * height : (i + 1) * height, :] + jnp.concatenate([add] * (sensors.shape[1] // LANES), axis=1)
        sensors[8 + i * height : 8 + (i + 1) * height, :] = jnp.where(inside > 0.5, value, 0.0)
    if k < ITERS:
        vectors = sensor_vectors(sensors, 8 + height, result.shape[0])
    else:
        vectors = own_vectors(na, nb, sensors, 8 + height)
    hidden = hidden_two(vectors, w1, b1, w2, b2)
    if k < ITERS:
        result[...] = hidden
    else:
        result[...] = (dot(hidden, w3[...]) + b3[...]).astype(BF16)
    skip = (k - HALO, height) if k < ITERS else (0, na)
    send_means(hidden, skip[0], na, nb // PER_CELL, skip[1], mean_line, mean_bias, col, cells, payload)


def field_kernel(na, nb, n_row, n_col, cells, gathered, coarse, coeffs, trunk, out, correction, ready, sent):
    steps = ready.shape[0]
    width = trunk.shape[1] // steps
    per = width // TILE
    ky = nb // PER_CELL
    found = corrections(gathered, coarse, n_row, n_col, cells)
    correction[...] = jnp.broadcast_to(found, correction.shape)
    upper = lax.broadcasted_iota(jnp.int32, (8, LANES), 0) < PER_CELL
    adds = {}
    for a in range(0, na, 8):
        for j in range(ky):
            at = a // PER_CELL * ky + j
            adds[a, j] = jnp.where(upper, correction[at : at + 1, :], correction[at + ky : at + ky + 1, :])
    low = low_lanes((8, LANES))
    copies = []
    for step in range(steps):
        values = dot(coeffs[...], trunk[:, step * width : (step + 1) * width])
        for pair in range(nb // 2):
            for a in range(0, na, 8):
                even, odd = (2 * pair * na + a, (2 * pair + 1) * na + a)
                lines = []
                for r in range(0, per, 2):
                    lanes = slice(r * TILE, r * TILE + LANES)
                    x, y = values[even : even + 8, lanes], values[odd : odd + 8, lanes]
                    lines.append(jnp.where(low, x, pltpu.roll(y, TILE, 1)))
                    lines.append(jnp.where(low, pltpu.roll(x, TILE, 1), y))
                block = jnp.stack(lines, axis=0) + adds[a, 2 * pair // PER_CELL][None]
                ready[step, a : a + 8, :, pair * LANES : (pair + 1) * LANES] = jnp.swapaxes(block, 0, 1)
        copies.append(
            pltpu.make_async_copy(ready.at[step], out.at[:, pl.ds(step * per, per), :], sent.at[step])
        )
        copies[-1].start()
    for copy in copies:
        copy.wait()


def body(
    field_start,
    w_sensor,
    bias_sensor,
    w_middle,
    bias_middle,
    w_latent,
    bias_latent,
    trunk_basis,
    coarse_matrix,
):
    rows_here, cols_here = field_start.shape
    n_row, n_col = lax.axis_size("row"), lax.axis_size("col")
    na, nb = rows_here // TILE, cols_here // TILE
    height = na + 2 * HALO
    kx, ky = na // PER_CELL, nb // PER_CELL
    cells = kx * ky
    devices = n_row * n_col
    latent = trunk_basis.shape[0]
    hid = w_sensor.shape[1]
    tile_values, places = 4 * TILE, 8 * TILE
    total = coarse_matrix.shape[1]
    whole = pl.BlockSpec(memory_space=pltpu.VMEM)
    shape = jax.ShapeDtypeStruct
    part = functools.partial

    def shift(x, step):
        return lax.ppermute(x, "row", [(i, (i + step) % n_row) for i in range(n_row)])

    def swap(x, parity):
        pairs = [(i, (i + 1 if i % 2 == parity else i - 1) % n_col) for i in range(n_col)]
        return lax.ppermute(x, "col", pairs)

    def exchange(x):
        return lax.all_to_all(x, ("row", "col"), 0, 0, tiled=True)

    spread_np, order = sensor_layout()
    spread = jnp.asarray(spread_np, BF16)
    half = TILE // 2
    blocks = tuple((int(at), half) for at in order[::half])
    hbm = pl.BlockSpec(memory_space=pltpu.HBM)

    side, inner = shape((nb * HALO, LANES), F32), shape((nb * (na - 2 * HALO), LANES), F32)
    field_rows = field_start.reshape(na, TILE, cols_here)
    up, down, *outer = call(
        part(outer_kernel, nb, ky),
        (shape((8, total), BF16), shape((8, total), BF16), side, side, side, side),
        field_rows[0:HALO],
        field_rows[na - HALO :],
        coarse_matrix,
        scratch=[pltpu.VMEM((8, total), F32)],
    )
    above, below = shift(down, 1), shift(up, -1)
    trunk, mean_trunk, w_first = call(
        part(trunk_kernel, blocks),
        (shape(trunk_basis.shape, BF16), shape((latent, LANES), F32), shape(w_sensor.shape, BF16)),
        trunk_basis,
        w_sensor,
        in_specs=[hbm, whole],
        scratch=[pltpu.SemaphoreType.DMA((4,))],
        flops=1 << 32,
    )
    middle = call(part(extract_tiles, nb), (inner, inner), field_rows[HALO : na - HALO])
    above, below, w_first = lax.optimization_barrier((above, below, w_first))
    mid, first, second = call(
        part(columns_kernel, na, nb, n_row),
        (shape((nb * height, tile_values), BF16), shape((16, total), BF16), shape((16, total), BF16)),
        *outer[:2],
        *middle,
        *outer[2:],
        above,
        below,
        coarse_matrix,
        scratch=[pltpu.VMEM((nb * height, tile_values), F32)] + [pltpu.VMEM((16, total), F32)] * 2,
    )
    second, first = swap(second, 1), swap(first, 0)

    net = (
        w_first,
        bias_sensor.reshape(1, hid),
        w_middle,
        bias_middle.reshape(1, hid),
    )

    b_latent = bias_latent.reshape(1, latent)
    w_sensors, b_sensors, mean_line, mean_bias = call(
        sensor_trunk_kernel,
        (
            shape((hid, places), BF16),
            shape((8, places), F32),
            shape((8, hid), F32),
            shape((8, LANES), F32),
        ),
        trunk,
        spread,
        mean_trunk,
        w_latent,
        b_latent,
        flops=1 << 30,
    )
    mid, w_sensors = lax.optimization_barrier((mid, w_sensors))

    def region(k):
        return (nb + 2 * HALO - 2 * k) * height

    payload_shape = shape((devices, LANES), F32)
    coeffs, payload, coarse = call(
        part(first_kernel, na, nb, n_col, cells),
        (shape((region(1), hid), BF16), payload_shape, shape((8 * (ky + 2), total), F32)),
        mid,
        first,
        second,
        above,
        below,
        coarse_matrix,
        spread,
        *net,
        mean_line,
        mean_bias,
        scratch=[pltpu.VMEM((region(0) + 16, places), F32), pltpu.VMEM((region(0), tile_values), F32)],
    )
    for k in range(2, ITERS + 1):
        gathered = exchange(payload)
        coeffs, payload = call(
            part(next_kernel, k, na, nb, n_row, n_col, cells),
            (shape((region(k) if k < ITERS else nb * na, hid if k < ITERS else latent), BF16), payload_shape),
            gathered,
            coeffs,
            w_sensors,
            b_sensors,
            coarse,
            *net,
            mean_line,
            mean_bias,
            w_latent,
            b_latent,
            scratch=[
                pltpu.VMEM((region(k - 1) + 16, places), F32),
                pltpu.VMEM(((ky + 2) * height, LANES), F32),
            ],
        )
    gathered = exchange(payload)
    steps = 8
    out = call(
        part(field_kernel, na, nb, n_row, n_col, cells),
        shape((na, TILE, cols_here), F32),
        gathered,
        coarse_matrix,
        coeffs,
        trunk,
        out_specs=hbm,
        scratch=[
            pltpu.VMEM((cells, LANES), F32),
            pltpu.VMEM((steps, na, TILE // steps, cols_here), F32),
            pltpu.SemaphoreType.DMA((steps,)),
        ],
    )
    return out.reshape(rows_here, cols_here)


def solution(mesh):
    placed = (P("row", "col"), P(), P(), P(), P(), P(), P(), P(), P(("row", "col"), None))
    return jax.shard_map(
        body, mesh=mesh, in_specs=placed, out_specs=P("row", "col"), check_vma=False
    )
```
